512 devices in a mesh: clus: 16 (over z_lo, x), dir: 32 (over y, z_hi, core).
Axes of the slice: x: 4, y: 4, z: 16 (z_hi: 4, z_lo: 4; z = z_hi * 4 + z_lo), core: 2. Of those that a mesh axis runs over, the one named last changes fastest.
Arguments:
- child_patterns: float32 [768, 2, 256, 128], P('clus', None, 'dir'), may hold values from -6 to 6
- trans_table: bfloat16 [316, 2, 73728], P(None, None, 'dir'), may hold values from -0.875 to 0.875
- child_parent: int32 [16, 48], P('clus'), may hold values from 0 to 7, never falling along the last dimension, each value on 1 to 8 neighbouring positions
- child_octant: int32 [768], P('clus'), may hold values from 0 to 7
- partner_src: int32 [128, 56], replicated, may hold values from 0 to 127, as said below
- partner_off: int32 [128, 56], replicated, may hold values from 0 to 315
- partner_count: int32 [128], replicated, may hold values from 15 to 56, as said below
Outputs:
- child_incoming: float32 [768, 2, 256, 128], P('clus', None, 'dir')
The draws below stay inside these ranges and needn't reach their ends.
Inputs may be any that keep to these rules, and one draw needn't show every extreme that they name: `partner_src`: each row lists 56 distinct parent clusters, none equal to the row's own index. `partner_count`: the number of live slots at the head of each row of partner_src and partner_off. On one index of clus, all of its 8 parents have 56 live slots. `child_parent`: Non-decreasing along each row; every one of the 8 parents of the row has 1 to 8 children.
All inputs are finite; a program needn't handle non-finite values.
Results may differ from the reference program's by a relative error of at most 0.0003.
Values sent between devices are 32-bit elements; how exact they have to be, the bound alone decides.
A program may use at most 64 MiB of HBM per device.

```python
import math
import jax
import jax.numpy as jnp
import numpy as np
from jax import lax

NTHETA_C = 128
NPHI_C = 256
NTHETA_P = 192
NPHI_P = 384
OFFSETS = 316
PAR_DEV = 8
CHILD_DEV = 48
PARENTS = 128
CHILDREN = 768
PARTNERS = 56
N_CLUS = 16


def draw_partner_src(key, part):
    row_keys = jax.random.split(jax.random.fold_in(key, 11), PARENTS)

    def one_row(row_key, target):
        shuffled = jax.random.permutation(row_key, PARENTS - 1).astype(jnp.int32)
        shuffled = shuffled + (shuffled >= target).astype(jnp.int32)
        return shuffled[:PARTNERS]
    return jax.vmap(one_row)(row_keys, jnp.arange(PARENTS, dtype=jnp.int32)).astype(jnp.int32)


def draw_partner_count(key, part):
    count_key, device_key = jax.random.split(jax.random.fold_in(key, 23))
    counts = jax.random.randint(count_key, (PARENTS,), PARTNERS // 4 + 1, PARTNERS + 1)
    full_device = jax.random.randint(device_key, (), 0, PARENTS // PAR_DEV)
    owner_device = jnp.arange(PARENTS, dtype=jnp.int32) // PAR_DEV
    return jnp.where(owner_device == full_device, PARTNERS, counts).astype(jnp.int32)


def set_ends(values, stream_key, smallest, top_value):
    place = [jax.random.randint(jax.random.fold_in(stream_key, axis), (), 0, length) for axis, length in enumerate(values.shape)]
    main_axis = values.shape.index(max(values.shape))
    next_to = place[:main_axis] + [(place[main_axis] + 1) % values.shape[main_axis]] + place[main_axis + 1:]
    return values.at[tuple(place)].set(smallest).at[tuple(next_to)].set(top_value)


def steps_of(rng, shape, cuts, least, largest):
    level, own = 1.0, jax.random.fold_in(rng, 6)
    for position, shards_of in cuts:
        steps = jnp.exp(jax.random.uniform(jax.random.fold_in(own, position), (shards_of,), jnp.float32, least / len(cuts), largest / len(cuts)))
        level = level * jnp.repeat(steps, shape[position] // shards_of).reshape([-1 if axis == position else 1 for axis in range(len(shape))])
    return level


def split_up(number_of, total, reach, slope):
    weights = [(1 << 20) // math.isqrt(rank ** slope) + 1 for rank in range(2, number_of + 1)]
    rest, holding = total - reach - (number_of - 1), [1] * (number_of - 1)
    while rest > 0:
        free = [i for i in range(number_of - 1) if holding[i] < reach]
        pool, left = sum([weights[i] for i in free]), rest
        for i in free:
            more = min(reach - holding[i], max(1, left * weights[i] // pool), rest)
            holding[i] = holding[i] + more
            rest = rest - more
    return np.array([reach] + holding)


def ragged(rng, count, total, limit, skew):
    if count == 2:
        one = jax.random.randint(rng, (), max(1, total - limit), min(limit, total - 1) + 1)
        return jnp.stack([one, total - one])
    lengths = jnp.asarray(split_up(count, total, limit, skew), jnp.int32)
    pairs = (count - 1) // 2
    donor, taker = lengths[1:1 + 2 * pairs:2], lengths[2:2 + 2 * pairs:2]
    room = jnp.minimum(donor - 1, limit - taker)
    passed = jax.random.randint(jax.random.fold_in(rng, 1), (pairs,), 0, 1 << 20) % (room + 1)
    lengths = lengths.at[1:1 + 2 * pairs:2].set(donor - passed).at[2:2 + 2 * pairs:2].set(taker + passed)
    return lengths[jax.random.permutation(jax.random.fold_in(rng, 2), count)]


def bell_draw(key, extent, width, reach, cuts=(), held_as=jnp.bfloat16):
    level = steps_of(key, extent, cuts, -0.22, 0.18) if cuts else 1.0
    values = jax.random.normal(key, extent, jnp.float32) * width * level
    return jnp.minimum(jnp.maximum(values, -reach), reach).astype(held_as)


def setup_inputs(seed: int = 0) -> dict:
    seeds = jax.random.split(jax.random.key(seed), 8)
    child_patterns = bell_draw(seeds[0], (CHILDREN, 2, NPHI_C, NTHETA_C), 1.0, 6.0, ((0, 16), (2, 32)), jnp.float32)
    trans_table = bell_draw(seeds[1], (OFFSETS, 2, NPHI_P * NTHETA_P), 0.15, 0.875, ((2, 32),))
    child_parent = jax.vmap(lambda own: jnp.searchsorted(jnp.cumsum(ragged(own, PAR_DEV, CHILD_DEV, min(8, CHILD_DEV), 1)), jnp.arange(CHILD_DEV), side="right"))(jax.random.split(seeds[2], N_CLUS)).reshape((N_CLUS, CHILD_DEV)).astype(jnp.int32)
    child_octant = set_ends(jax.random.randint(seeds[3], (CHILDREN,), 0, 8), jax.random.fold_in(seeds[3], 1), 0, 7).astype(jnp.int32)
    partner_src = draw_partner_src(jax.random.fold_in(seeds[7], 71), 0)
    partner_off = set_ends(jax.random.randint(seeds[5], (PARENTS, PARTNERS), 0, OFFSETS), jax.random.fold_in(seeds[5], 1), 0, OFFSETS - 1).astype(jnp.int32)
    partner_count = draw_partner_count(jax.random.fold_in(seeds[7], 71), 0)
    return {"child_patterns": child_patterns, "trans_table": trans_table, "child_parent": child_parent, "child_octant": child_octant, "partner_src": partner_src, "partner_off": partner_off, "partner_count": partner_count}


phase_scale = 8.0 * math.pi
highest = lax.Precision.HIGHEST


def lagrange(offset):
    weights = []
    for anchor in range(5):
        factor = jnp.ones_like(offset)
        for neighbour in range(5):
            if neighbour != anchor:
                factor = factor * (offset - neighbour) / (anchor - neighbour)
        weights.append(factor)
    return weights


def polar_matrix_of(rows_out, rows_in):
    target = (jnp.arange(rows_out, dtype=jnp.float32) + 0.5) * rows_in / rows_out - 0.5
    start_row = jnp.clip(jnp.floor(target + 0.5).astype(jnp.int32) - 2, 0, rows_in - 5)
    weights = lagrange(target - start_row.astype(jnp.float32))
    columns = jnp.arange(rows_in, dtype=jnp.int32)
    matrix = jnp.zeros((rows_out, rows_in), jnp.float32)
    for anchor in range(5):
        matrix = matrix + jnp.where(columns[None, :] == (start_row + anchor)[:, None], weights[anchor][:, None], 0.0)
    return matrix


def azimuth_matrix_of(out_index, in_index, total_out, total_in, period):
    target = (out_index * total_in).astype(jnp.float32) / total_out
    nearest = jnp.floor(target + 0.5).astype(jnp.int32)
    weights = lagrange(target - nearest.astype(jnp.float32) + 2.0)
    matrix = jnp.zeros((out_index.shape[0], in_index.shape[0]), jnp.float32)
    for anchor in range(5):
        columns = nearest + anchor - 2
        if period > 0:
            columns = jnp.mod(columns, period)
        matrix = matrix + jnp.where(in_index[None, :] == columns[:, None], weights[anchor][:, None], 0.0)
    return matrix


def shift_phases(octant, azimuth_index, azimuth_total, polar_total):
    azimuth = 2.0 * math.pi * azimuth_index.astype(jnp.float32) / azimuth_total
    polar = math.pi * (jnp.arange(polar_total, dtype=jnp.float32) + 0.5) / polar_total
    first_axis = jnp.sin(polar)[None, :] * jnp.cos(azimuth)[:, None]
    second_axis = jnp.sin(polar)[None, :] * jnp.sin(azimuth)[:, None]
    third_axis = jnp.cos(polar)[None, :] * jnp.ones_like(azimuth)[:, None]
    first_sign = (1 - 2 * (octant % 2)).astype(jnp.float32)
    second_sign = (1 - 2 * ((octant // 2) % 2)).astype(jnp.float32)
    third_sign = (1 - 2 * (octant // 4)).astype(jnp.float32)
    phase_angle = phase_scale * (first_sign[:, None, None] * first_axis[None] + second_sign[:, None, None] * second_axis[None] + third_sign[:, None, None] * third_axis[None])
    return jnp.cos(phase_angle), jnp.sin(phase_angle)


def reference(child_patterns, trans_table, child_parent, child_octant, partner_src, partner_off, partner_count):
    azimuth_matrix = azimuth_matrix_of(jnp.arange(NPHI_P, dtype=jnp.int32), jnp.arange(NPHI_C, dtype=jnp.int32), NPHI_P, NPHI_C, NPHI_C)
    polar_matrix = polar_matrix_of(NTHETA_P, NTHETA_C)
    azimuth_rows = jnp.arange(NPHI_P, dtype=jnp.int32)
    device_blocks = child_patterns.reshape(N_CLUS, CHILD_DEV, 2, NPHI_C, NTHETA_C)
    octant_blocks = child_octant.reshape(N_CLUS, CHILD_DEV)
    parent_ids = jnp.arange(PAR_DEV, dtype=jnp.int32)

    def aggregate(inputs):
        patterns, parents, octant = inputs
        along_azimuth = jnp.einsum("pc,kacz->kapz", azimuth_matrix, patterns, precision=highest)
        refined = jnp.einsum("kapz,tz->kapt", along_azimuth, polar_matrix, precision=highest)
        cosine, sine_part = shift_phases(octant, azimuth_rows, NPHI_P, NTHETA_P)
        real_part = refined[:, 0] * cosine - refined[:, 1] * sine_part
        imaginary = refined[:, 0] * sine_part + refined[:, 1] * cosine
        shifted = jnp.stack([real_part, imaginary], axis=1)
        onehot = (parents[None, :] == parent_ids[:, None]).astype(jnp.float32)
        return jnp.einsum("gk,kapt->gapt", onehot, shifted, precision=highest)

    radiation = lax.map(aggregate, (device_blocks, child_parent, octant_blocks)).reshape(PARENTS, 2, NPHI_P, NTHETA_P)

    def translate_one(inputs):
        sources, offsets, live_count = inputs
        live_mask = (jnp.arange(PARTNERS, dtype=jnp.int32) < live_count).astype(jnp.float32)
        picked = radiation[sources]
        operator = trans_table[offsets].astype(jnp.float32).reshape(PARTNERS, 2, NPHI_P, NTHETA_P) * live_mask[:, None, None, None]
        real_part = jnp.sum(operator[:, 0] * picked[:, 0] - operator[:, 1] * picked[:, 1], axis=0)
        imaginary = jnp.sum(operator[:, 0] * picked[:, 1] + operator[:, 1] * picked[:, 0], axis=0)
        return jnp.stack([real_part, imaginary], axis=0)

    incoming = lax.map(translate_one, (partner_src, partner_off, partner_count))
    incoming_blocks = incoming.reshape(N_CLUS, PAR_DEV, 2, NPHI_P, NTHETA_P)

    def disaggregate(inputs):
        parent_patterns, parents, octant = inputs
        onehot = (parents[None, :] == parent_ids[:, None]).astype(jnp.float32)
        per_child = jnp.einsum("gk,gapt->kapt", onehot, parent_patterns, precision=highest)
        cosine, sine_part = shift_phases(octant, azimuth_rows, NPHI_P, NTHETA_P)
        real_part = per_child[:, 0] * cosine + per_child[:, 1] * sine_part
        imaginary = per_child[:, 1] * cosine - per_child[:, 0] * sine_part
        returned = jnp.stack([real_part, imaginary], axis=1)
        coarse = jnp.einsum("kapt,tz->kapz", returned, polar_matrix, precision=highest)
        return jnp.einsum("pc,kapz->kacz", azimuth_matrix, coarse, precision=highest)

    result = lax.map(disaggregate, (incoming_blocks, child_parent, octant_blocks))
    return result.reshape(CHILDREN, 2, NPHI_C, NTHETA_C)
```

```python
import functools
import math

import jax
import jax.numpy as jnp
import ml_dtypes
import numpy as np
from jax import lax
from jax.experimental import pallas as pl
from jax.experimental.pallas import tpu as pltpu
from jax.sharding import PartitionSpec as P

NT_C, NP_C, NT_P, NP_P = 128, 256, 192, 384
OFFSETS = 316
N_CLUS, N_DIR = 16, 32
PAR, KIDS = 8, 48
TILES = PAR * 6
ROWS = 6 * TILES
PAD = OFFSETS * 32
MESH = pl.DeviceIdType.MESH
EVEN = np.array([-2, 0, 2, 4, 6, 8, 10, 14])
ODD = np.array([-1, 1, 3, 5, 7, 9, 11, 13])


def lagrange(t):
    out = []
    for m in range(5):
        w = np.ones_like(t)
        for n in range(5):
            if n != m:
                w = w * (t - n) / (m - n)
        out.append(w)
    return out


def polar_matrix():
    x = (np.arange(NT_P) + 0.5) * NT_C / NT_P - 0.5
    s = np.clip(np.floor(x + 0.5).astype(int) - 2, 0, NT_C - 5)
    w = lagrange(x - s)
    m = np.zeros((NT_P, NT_C))
    for k in range(5):
        m[np.arange(NT_P), s + k] = w[k]
    return m


def azimuth_rows(rows):
    x = rows * NP_C / NP_P
    b = np.floor(x + 0.5).astype(int)
    w = lagrange(x - b + 2)
    m = np.zeros((len(rows), 8))
    for k in range(5):
        for j in range(len(rows)):
            i = b[j] + k - 2
            if 0 <= i < 8:
                m[j, i] = w[k][j]
    return m


def halves(a):
    a = a.astype(np.float32)
    hi = a.astype(ml_dtypes.bfloat16)
    lo = (a - hi.astype(np.float32)).astype(ml_dtypes.bfloat16)
    return np.stack([hi, lo])


def in_tiles(even, odd):
    return np.stack([even[:, :128], np.concatenate([even[:, 128:], odd[:, :64]], 1), odd[:, 64:]])


@functools.cache
def constants():
    p = polar_matrix()
    ae, ao = azimuth_rows(EVEN), azimuth_rows(ODD)
    eye = np.eye(16)
    up_left = halves(np.concatenate([np.kron(eye, ae), np.kron(eye, ao)], 0))
    w = np.zeros((256, 384))
    w[:128, :192] = p.T
    w[128:, 192:] = p.T
    up_right = halves(w)
    down_right = halves(np.stack([w[:128, :256].T, w[128:, 128:].T]))
    down_left = halves(np.concatenate([np.kron(eye, ae.T), np.kron(eye, ao.T)], 1))
    theta = math.pi * (np.arange(NT_P) + 0.5) / NT_P
    phases = np.zeros((N_DIR, 3, 2, 3, 8, 128))
    for d in range(N_DIR):
        angle = []
        for rows in (EVEN, ODD):
            phi = 2 * math.pi * ((12 * d + rows) % NP_P) / NP_P
            angle.append(
                8 * math.pi
                * np.stack(
                    [
                        np.sin(theta) * np.cos(phi)[:, None],
                        np.sin(theta) * np.sin(phi)[:, None],
                        np.cos(theta) * np.ones((8, 1)),
                    ]
                )
            )
        for k in range(3):
            t = in_tiles(angle[0][k], angle[1][k])
            phases[d, k] = np.stack([np.cos(t), np.sin(t)])
    return up_left, up_right, down_right, down_left, phases.reshape(N_DIR, 144, 128).astype(np.float32)


def split(x):
    hi = x.astype(jnp.bfloat16)
    return hi, (x - hi.astype(jnp.float32)).astype(jnp.bfloat16)


def dot3(a, b):
    f = functools.partial(jnp.dot, preferred_element_type=jnp.float32)
    return f(a[0], b[0]) + (f(a[1], b[0]) + f(a[0], b[1]))


def position():
    clus, direction = lax.axis_index("clus"), lax.axis_index("dir")
    core = lax.rem(direction, 2)
    x, z = lax.rem(clus, 4), lax.div(clus, 4)
    return clus, direction, core, x, z


def gather_member(core, x, z, k):
    return (1 - core) * (z * 4 + k) + core * (k * 4 + x)


def reduce_member(core, x, z, k):
    return (1 - core) * (k * 4 + x) + core * (z * 4 + k)


def octant_tables(base, table):
    def tile(k, a, c):
        r = (k * 6 + a * 3 + c) * 8
        return base[r : r + 8, :]

    for c in range(3):
        ar, ai, br, bi, cr, ci = (tile(k, a, c) for k in range(3) for a in range(2))
        rr, ii, ri, ir = ar * br, ai * bi, ar * bi, ai * br
        for sx, sy, re, im in ((1, 1, rr - ii, ri + ir), (1, -1, rr + ii, ir - ri)):
            pr, pi, qr, qi = re * cr, im * ci, re * ci, im * cr
            for sz, fr, fi in ((1, pr - pi, qr + qi), (-1, pr + pi, qi - qr)):
                for sign in (1, -1):
                    o = (sx * sign < 0) + 2 * (sy * sign < 0) + 4 * (sz * sign < 0)
                    table[(o * 6 + c) * 8 : (o * 6 + c) * 8 + 8, :] = fr
                    table[(o * 6 + 3 + c) * 8 : (o * 6 + 3 + c) * 8 + 8, :] = fi if sign > 0 else -fi


def build_lists(src_ref, off_ref, count_ref, key_ref, list_ref):
    clus, direction, core, x, z = position()
    lane8 = lax.broadcasted_iota(jnp.int32, (8, 128), 1)
    sub8 = lax.broadcasted_iota(jnp.int32, (8, 128), 0)
    keys, sums = [], []
    key_ref[...] = jnp.full((32, 128), PAD, jnp.int32)
    for k in range(4):
        first = pl.multiple_of(8 * reduce_member(core, x, z, k), 8)
        counts = jnp.sum(
            jnp.where(lane8 == first + sub8, count_ref[...], 0), axis=1, keepdims=True
        )
        src = src_ref[pl.ds(first, 8), :]
        off = off_ref[pl.ds(first, 8), :]
        slot = lax.broadcasted_iota(jnp.int32, src.shape, 1)
        owner = src >> 3
        own_x, own_z = owner & 3, owner >> 2
        here = jnp.where(core == 0, own_z, own_x) == jnp.where(core == 0, z, x)
        where_from = jnp.where(core == 0, own_x, own_z) * 8 + (src & 7)
        live = here & (slot < counts)
        key_ref[8 * k : 8 * k + 8, 0 : src.shape[1]] = jnp.where(live, off * 32 + where_from, PAD)
    key = key_ref[...]
    lane = lax.broadcasted_iota(jnp.int32, (32, 128), 1)
    number = jnp.sum((key < PAD).astype(jnp.int32), axis=1, keepdims=True)
    size = 2
    while size <= 64:
        j = size // 2
        while j >= 1:
            low = (lane & j) == 0
            other = jnp.where(low, pltpu.roll(key, 128 - j, 1), pltpu.roll(key, j, 1))
            take_min = low == ((lane & size) == 0)
            key = jnp.where(take_min, jnp.minimum(key, other), jnp.maximum(key, other))
            j //= 2
        size *= 2
    list_ref[...] = jnp.where(lane < 64, key, number)


def aggregate_kernel(
    parent_ref, octant_ref, child_ref, src_ref, off_ref, count_ref, left_ref, right_ref, phases_ref,
    part_ref, list_ref, z_ref, base_ref, table_ref, acc_ref, key_ref, sem,
):
    copy = pltpu.make_async_copy(phases_ref.at[lax.axis_index("dir")], base_ref, sem)
    copy.start()
    build_lists(src_ref, off_ref, count_ref, key_ref, list_ref)
    for n in range(6):
        x = split(child_ref[8 * n : 8 * n + 8].reshape(128, 128))
        eo = dot3((left_ref[0], left_ref[1]), x)
        y = split(jnp.concatenate([eo[:128], eo[128:]], axis=1))
        z_ref[128 * n : 128 * n + 128, :] = dot3(y, (right_ref[0], right_ref[1]))
    copy.wait()
    octant_tables(base_ref, table_ref)

    def child(k, acc):
        parent = parent_ref[0, k]
        before = parent_ref[0, jnp.maximum(k - 1, 0)]
        keep = jnp.where((parent == before) & (k > 0), 1.0, 0.0)
        o = octant_ref[k]
        new = []
        for c in range(3):
            re = z_ref[pl.ds(pl.multiple_of(k * 16, 8), 8), 128 * c : 128 * c + 128]
            im = z_ref[pl.ds(pl.multiple_of(k * 16 + 8, 8), 8), 128 * c : 128 * c + 128]
            fr = table_ref[pl.ds(pl.multiple_of((o * 6 + c) * 8, 8), 8), :]
            fi = table_ref[pl.ds(pl.multiple_of((o * 6 + 3 + c) * 8, 8), 8), :]
            new.append(acc[c] * keep + (re * fr - im * fi))
            new.append(acc[3 + c] * keep + (re * fi + im * fr))
        new = new[0::2] + new[1::2]
        for t in range(6):
            acc_ref[pl.ds(pl.multiple_of((parent * 6 + t) * 8, 8), 8), :] = new[t]
        return tuple(new)

    lax.fori_loop(0, KIDS, child, tuple(jnp.zeros((8, 128), jnp.float32) for _ in range(6)), unroll=4)
    for s in range(8):
        part_ref[s * TILES : (s + 1) * TILES, :] = acc_ref[pl.ds(s, TILES, stride=8), :]


def enter(peers):
    barrier = pltpu.get_barrier_semaphore()
    for peer in peers:
        pl.semaphore_signal(barrier, inc=1, device_id=peer, device_id_type=MESH)
    pl.semaphore_wait(barrier, len(peers))


def even_lanes():
    column = lax.rem(lax.broadcasted_iota(jnp.int32, (TILES, 128), 0), 3)
    lane = lax.broadcasted_iota(jnp.int32, (TILES, 128), 1)
    return (column == 0) | ((column == 1) & (lane < 64))


def gather_kernel(part_ref, out_ref, halo_ref, send_sem, recv_sem):
    clus, direction, core, x, z = position()
    after = (clus, lax.rem(direction + 1, N_DIR))
    before = (clus, lax.rem(direction + N_DIR - 1, N_DIR))
    me = (1 - core) * x + core * z
    peers = [(gather_member(core, x, z, lax.rem(me + r, 4)), direction) for r in (1, 2, 3)]
    enter([after, before, *peers])
    forward = pltpu.make_async_remote_copy(
        part_ref.at[pl.ds(7 * TILES, TILES)], halo_ref.at[0], send_sem.at[0], recv_sem.at[0],
        device_id=after, device_id_type=MESH,
    )
    backward = pltpu.make_async_remote_copy(
        part_ref.at[pl.ds(0, TILES)], halo_ref.at[1], send_sem.at[1], recv_sem.at[1],
        device_id=before, device_id_type=MESH,
    )
    forward.start()
    backward.start()
    own = pl.multiple_of(me * ROWS, 8)
    out_ref[pl.ds(own, ROWS), :] = part_ref[TILES : TILES + ROWS, :]
    forward.wait_recv()
    even = even_lanes()
    got = halo_ref[0]
    q0 = pl.ds(pl.multiple_of(own, 8), TILES)
    q1 = pl.ds(pl.multiple_of(own + TILES, 8), TILES)
    q5 = pl.ds(pl.multiple_of(own + 5 * TILES, 8), TILES)
    out_ref[q0, :] += jnp.where(even, 0.0, got)
    out_ref[q1, :] += jnp.where(even, got, 0.0)
    backward.wait_recv()
    out_ref[q5, :] += halo_ref[1]
    copies = []
    for r, peer in enumerate(peers):
        block = out_ref.at[pl.ds(own, ROWS)]
        copy = pltpu.make_async_remote_copy(
            block, block, send_sem.at[2 + r], recv_sem.at[2 + r], device_id=peer, device_id_type=MESH
        )
        copy.start()
        copies.append(copy)
    for copy in copies:
        copy.wait()
    forward.wait_send()
    backward.wait_send()


def translate_kernel(list_ref, table_in, s_ref, out_ref, table_ref):
    rows = table_in.shape[0]
    step = 144

    def widen(i, carry):
        at = pl.ds(pl.multiple_of(i * step, 16), step)
        table_ref[at, :] = table_in[at, :].astype(jnp.float32)
        return carry

    lax.fori_loop(0, rows // step, widen, 0)
    table_ref[rows : rows + 40, :] = jnp.zeros((40, 128), jnp.float32)

    def target(t, carry):
        def four(b, acc):
            acc = list(acc)
            for u in range(4):
                code = list_ref[t, b * 4 + u]
                o, s = code >> 5, code & 31
                trow = o * 36
                srow = (s >> 3) * ROWS + (s & 7) * 6
                for c in range(3):
                    tr = table_ref[pl.ds(trow + 2 * c, 6, stride=6), :]
                    ti = table_ref[pl.ds(trow + 2 * c + 1, 6, stride=6), :]
                    sr = s_ref[pl.ds(srow + c, 6, stride=TILES), :]
                    si = s_ref[pl.ds(srow + 3 + c, 6, stride=TILES), :]
                    acc[c] = acc[c] + (tr * sr - ti * si)
                    acc[3 + c] = acc[3 + c] + (tr * si + ti * sr)
            return tuple(acc)

        number = list_ref[t, 64]
        zero = jnp.zeros((6, 128), jnp.float32)
        acc = lax.fori_loop(0, (number + 3) >> 2, four, (zero,) * 6)
        to = (t >> 3) * ROWS + (t & 7) * 6
        for i in range(6):
            out_ref[pl.ds(to + i, 6, stride=TILES), :] = acc[i]
        return carry

    lax.fori_loop(0, 32, target, 0)


def reduce_kernel(in_ref, out_ref, got_ref, pack_ref, halo_ref, send_sem, recv_sem):
    clus, direction, core, x, z = position()
    after = (clus, lax.rem(direction + 1, N_DIR))
    before = (clus, lax.rem(direction + N_DIR - 1, N_DIR))
    me = (1 - core) * z + core * x
    others = [lax.rem(me + r, 4) for r in (1, 2, 3)]
    peers = [(reduce_member(core, x, z, k), direction) for k in others]
    enter([after, before, *peers])
    copies = []
    for r, (k, peer) in enumerate(zip(others, peers)):
        copy = pltpu.make_async_remote_copy(
            in_ref.at[pl.ds(pl.multiple_of(k * ROWS, 8), ROWS)], got_ref.at[r],
            send_sem.at[2 + r], recv_sem.at[2 + r], device_id=peer, device_id_type=MESH,
        )
        copy.start()
        copies.append(copy)
    for copy in copies:
        copy.wait_recv()
    out_ref[TILES : TILES + ROWS, :] = (in_ref[pl.ds(pl.multiple_of(me * ROWS, 8), ROWS), :] + got_ref[0]) + (
        got_ref[1] + got_ref[2]
    )
    pack_ref[0] = jnp.where(even_lanes(), out_ref[2 * TILES : 3 * TILES, :], out_ref[TILES : 2 * TILES, :])
    pack_ref[1] = out_ref[6 * TILES : 7 * TILES, :]
    backward = pltpu.make_async_remote_copy(
        pack_ref.at[0], halo_ref.at[0], send_sem.at[0], recv_sem.at[0], device_id=before, device_id_type=MESH
    )
    forward = pltpu.make_async_remote_copy(
        pack_ref.at[1], halo_ref.at[1], send_sem.at[1], recv_sem.at[1], device_id=after, device_id_type=MESH
    )
    backward.start()
    forward.start()
    backward.wait_recv()
    forward.wait_recv()
    out_ref[7 * TILES : 8 * TILES, :] = halo_ref[0]
    out_ref[0:TILES, :] = halo_ref[1]
    for copy in (backward, forward, *copies):
        copy.wait_send()


def disaggregate_kernel(
    parent_ref, octant_ref, inc_ref, right_ref, left_ref, phases_ref,
    out_ref, r_ref, base_ref, table_ref, tile_ref, sem,
):
    copy = pltpu.make_async_copy(phases_ref.at[lax.axis_index("dir")], base_ref, sem)
    copy.start()
    for t in range(TILES):
        tile_ref[8 * t : 8 * t + 8, :] = inc_ref[pl.ds(t, 8, stride=TILES), :]
    copy.wait()
    octant_tables(base_ref, table_ref)

    def child(k, carry):
        g, o = parent_ref[0, k], octant_ref[k]
        for c in range(3):
            re = tile_ref[pl.ds(pl.multiple_of((g * 6 + c) * 8, 8), 8), :]
            im = tile_ref[pl.ds(pl.multiple_of((g * 6 + 3 + c) * 8, 8), 8), :]
            fr = table_ref[pl.ds(pl.multiple_of((o * 6 + c) * 8, 8), 8), :]
            fi = table_ref[pl.ds(pl.multiple_of((o * 6 + 3 + c) * 8, 8), 8), :]
            r_ref[pl.ds(pl.multiple_of(k * 16, 8), 8), 128 * c : 128 * c + 128] = re * fr + im * fi
            r_ref[pl.ds(pl.multiple_of(k * 16 + 8, 8), 8), 128 * c : 128 * c + 128] = im * fr - re * fi
        return carry

    lax.fori_loop(0, KIDS, child, 0, unroll=4)
    for n in range(6):
        hi, lo = split(r_ref[128 * n : 128 * n + 128, :])
        e = dot3((hi[:, :256], lo[:, :256]), (right_ref[0, 0], right_ref[1, 0]))
        o = dot3((hi[:, 128:], lo[:, 128:]), (right_ref[0, 1], right_ref[1, 1]))
        v = split(jnp.concatenate([e, o], axis=0))
        out_ref[8 * n : 8 * n + 8] = dot3((left_ref[0], left_ref[1]), v).reshape(8, 2, 8, 128)


VMEM_SPEC = pl.BlockSpec(memory_space=pltpu.VMEM)
SMEM_SPEC = pl.BlockSpec(memory_space=pltpu.SMEM)
ANY_SPEC = pl.BlockSpec(memory_space=pl.ANY)
LIMIT = 48 * 2**20


def f32(*shape):
    return jax.ShapeDtypeStruct(shape, jnp.float32)


def on_device(child, table, child_parent, child_octant, partner_src, partner_off, partner_count):
    up_left, up_right, down_right, down_left, phases = (jnp.asarray(a) for a in constants())
    flat_table = table.reshape(OFFSETS, 2, 18, 128).transpose(0, 2, 1, 3).reshape(OFFSETS * 36, 128)
    vm = functools.partial(pltpu.VMEM, dtype=jnp.float32)
    part, lists = pl.pallas_call(
        aggregate_kernel,
        out_shape=(f32(8 * TILES, 128), jax.ShapeDtypeStruct((32, 128), jnp.int32)),
        in_specs=[SMEM_SPEC] * 2 + [VMEM_SPEC] * 6 + [ANY_SPEC],
        out_specs=(VMEM_SPEC, VMEM_SPEC),
        scratch_shapes=[
            vm((768, 384)), vm((144, 128)), vm((384, 128)), vm((384, 128)), pltpu.VMEM((32, 128), jnp.int32),
            pltpu.SemaphoreType.DMA,
        ],
        compiler_params=pltpu.CompilerParams(vmem_limit_bytes=LIMIT),
        name="aggregate",
    )(child_parent, child_octant, child, partner_src, partner_off, partner_count.reshape(1, 128), up_left, up_right, phases)
    sources = pl.pallas_call(
        gather_kernel,
        out_shape=f32(4 * ROWS, 128),
        in_specs=[VMEM_SPEC],
        out_specs=VMEM_SPEC,
        scratch_shapes=[vm((2, TILES, 128)), pltpu.SemaphoreType.DMA((5,)), pltpu.SemaphoreType.DMA((5,))],
        compiler_params=pltpu.CompilerParams(collective_id=0, has_side_effects=True, vmem_limit_bytes=LIMIT),
        name="gather",
    )(part)
    partial = pl.pallas_call(
        translate_kernel,
        out_shape=f32(4 * ROWS, 128),
        in_specs=[SMEM_SPEC, VMEM_SPEC, VMEM_SPEC],
        out_specs=VMEM_SPEC,
        scratch_shapes=[vm((OFFSETS * 36 + 40, 128))],
        compiler_params=pltpu.CompilerParams(vmem_limit_bytes=LIMIT),
        name="translate",
    )(lists, flat_table, sources)
    incoming = pl.pallas_call(
        reduce_kernel,
        out_shape=f32(8 * TILES, 128),
        in_specs=[VMEM_SPEC],
        out_specs=VMEM_SPEC,
        scratch_shapes=[
            vm((3, ROWS, 128)), vm((2, TILES, 128)), vm((2, TILES, 128)),
            pltpu.SemaphoreType.DMA((5,)), pltpu.SemaphoreType.DMA((5,)),
        ],
        compiler_params=pltpu.CompilerParams(collective_id=1, has_side_effects=True, vmem_limit_bytes=LIMIT),
        name="reduce",
    )(partial)
    return pl.pallas_call(
        disaggregate_kernel,
        out_shape=f32(KIDS, 2, 8, 128),
        in_specs=[SMEM_SPEC] * 2 + [VMEM_SPEC] * 3 + [ANY_SPEC],
        out_specs=VMEM_SPEC,
        scratch_shapes=[
            vm((768, 384)), vm((144, 128)), vm((384, 128)), vm((384, 128)), pltpu.SemaphoreType.DMA,
        ],
        compiler_params=pltpu.CompilerParams(vmem_limit_bytes=LIMIT),
        name="disaggregate",
    )(child_parent, child_octant, incoming, down_right, down_left, phases)


def solution(mesh):
    return jax.shard_map(
        on_device,
        mesh=mesh,
        in_specs=(P("clus", None, "dir", None), P(None, None, "dir"), P("clus", None), P("clus"), P(), P(), P()),
        out_specs=P("clus", None, "dir", None),
        check_vma=False,
    )
```

```python
import functools
import math

import jax
import jax.numpy as jnp
import ml_dtypes
import numpy as np
from jax import lax
from jax.experimental import pallas as pl
from jax.experimental.pallas import tpu as pltpu
from jax.sharding import PartitionSpec as P

NT_C, NP_C, NT_P, NP_P = 128, 256, 192, 384
OFFSETS = 316
N_CLUS, N_DIR = 16, 32
PAR, KIDS = 8, 48
TILES = PAR * 6
MESH = pl.DeviceIdType.MESH
EVEN = np.array([-2, 0, 2, 4, 6, 8, 10, 14])
ODD = np.array([-1, 1, 3, 5, 7, 9, 11, 13])


def lagrange(t):
    out = []
    for m in range(5):
        w = np.ones_like(t)
        for n in range(5):
            if n != m:
                w = w * (t - n) / (m - n)
        out.append(w)
    return out


def polar_matrix():
    x = (np.arange(NT_P) + 0.5) * NT_C / NT_P - 0.5
    s = np.clip(np.floor(x + 0.5).astype(int) - 2, 0, NT_C - 5)
    w = lagrange(x - s)
    m = np.zeros((NT_P, NT_C))
    for k in range(5):
        m[np.arange(NT_P), s + k] = w[k]
    return m


def azimuth_rows(rows):
    x = rows * NP_C / NP_P
    b = np.floor(x + 0.5).astype(int)
    w = lagrange(x - b + 2)
    m = np.zeros((len(rows), 8))
    for k in range(5):
        for j in range(len(rows)):
            i = b[j] + k - 2
            if 0 <= i < 8:
                m[j, i] = w[k][j]
    return m


def halves(a):
    a = a.astype(np.float32)
    hi = a.astype(ml_dtypes.bfloat16)
    lo = (a - hi.astype(np.float32)).astype(ml_dtypes.bfloat16)
    return np.stack([hi, lo])


def in_tiles(even, odd):
    return np.stack([even[:, :128], np.concatenate([even[:, 128:], odd[:, :64]], 1), odd[:, 64:]])


@functools.cache
def constants():
    p = polar_matrix()
    ae, ao = azimuth_rows(EVEN), azimuth_rows(ODD)
    eye = np.eye(16)
    up_left = halves(np.concatenate([np.kron(eye, ae), np.kron(eye, ao)], 0))
    w = np.zeros((256, 384))
    w[:128, :192] = p.T
    w[128:, 192:] = p.T
    up_right = halves(w)
    down_right = halves(np.stack([w[:128, :256].T, w[128:, 128:].T]))
    down_left = halves(np.concatenate([np.kron(eye, ae.T), np.kron(eye, ao.T)], 1))
    theta = math.pi * (np.arange(NT_P) + 0.5) / NT_P
    phases = np.zeros((N_DIR, 3, 2, 3, 8, 128))
    for d in range(N_DIR):
        angle = []
        for rows in (EVEN, ODD):
            phi = 2 * math.pi * ((12 * d + rows) % NP_P) / NP_P
            angle.append(
                8 * math.pi
                * np.stack(
                    [
                        np.sin(theta) * np.cos(phi)[:, None],
                        np.sin(theta) * np.sin(phi)[:, None],
                        np.cos(theta) * np.ones((8, 1)),
                    ]
                )
            )
        for k in range(3):
            t = in_tiles(angle[0][k], angle[1][k])
            phases[d, k] = np.stack([np.cos(t), np.sin(t)])
    return up_left, up_right, down_right, down_left, phases.reshape(N_DIR, 144, 128).astype(np.float32)


def split(x):
    hi = x.astype(jnp.bfloat16)
    return hi, (x - hi.astype(jnp.float32)).astype(jnp.bfloat16)


def dot3(a, b):
    f = functools.partial(jnp.dot, preferred_element_type=jnp.float32)
    return f(a[0], b[0]) + (f(a[1], b[0]) + f(a[0], b[1]))


def position():
    clus, direction = lax.axis_index("clus"), lax.axis_index("dir")
    core = lax.rem(direction, 2)
    x, z = lax.rem(clus, 4), lax.div(clus, 4)
    return clus, direction, core, x, z


def gather_member(core, x, z, k):
    return (1 - core) * (z * 4 + k) + core * (k * 4 + x)


def reduce_member(core, x, z, k):
    return (1 - core) * (k * 4 + x) + core * (z * 4 + k)


def octant_tables(base, table):
    def tile(k, a, c):
        r = (k * 6 + a * 3 + c) * 8
        return base[r : r + 8, :]

    for c in range(3):
        ar, ai, br, bi, cr, ci = (tile(k, a, c) for k in range(3) for a in range(2))
        rr, ii, ri, ir = ar * br, ai * bi, ar * bi, ai * br
        for sx, sy, re, im in ((1, 1, rr - ii, ri + ir), (1, -1, rr + ii, ir - ri)):
            pr, pi, qr, qi = re * cr, im * ci, re * ci, im * cr
            for sz, fr, fi in ((1, pr - pi, qr + qi), (-1, pr + pi, qi - qr)):
                for sign in (1, -1):
                    o = (sx * sign < 0) + 2 * (sy * sign < 0) + 4 * (sz * sign < 0)
                    table[o * 6 + c] = fr
                    table[o * 6 + 3 + c] = fi if sign > 0 else -fi


def aligned(i, n=8):
    return pl.multiple_of(i, n)


def build_index(parent_ref, src_ref, off_ref, count_ref, key_ref):
    clus, direction, core, x, z = position()
    src = src_ref[...]
    off = off_ref[...]
    slot = lax.broadcasted_iota(jnp.int32, src.shape, 0)
    own_x, own_z = (src >> 3) & 3, src >> 5
    here = jnp.where(core == 0, own_z, own_x) == jnp.where(core == 0, z, x)
    local = jnp.where(core == 0, own_x, own_z) * 8 + (src & 7)
    local = jnp.where(here & (slot < count_ref[...]), local, -1)
    which = lax.broadcasted_iota(jnp.int32, (32, 128), 0)
    key = jnp.full((32, 128), OFFSETS, jnp.int32)
    for p in range(src.shape[0]):
        key = jnp.where(which == local[p : p + 1], off[p : p + 1], key)
    key_ref[0:32, :] = key
    parent = lax.broadcasted_iota(jnp.int32, (8, KIDS), 0)
    start = jnp.sum((parent_ref[...] < parent).astype(jnp.int32), axis=1, keepdims=True)
    number = jnp.sum((parent_ref[...] == parent).astype(jnp.int32), axis=1, keepdims=True)
    lane = lax.broadcasted_iota(jnp.int32, (8, 128), 1)
    own = jnp.where(lane < number, start + lane, KIDS)
    key_ref[32:40, :] = jnp.where(lane < 8, own, jnp.minimum(start + lane - 8, KIDS - 1))


def even_lanes():
    column = lax.rem(lax.broadcasted_iota(jnp.int32, (TILES, 128), 0), 3)
    lane = lax.broadcasted_iota(jnp.int32, (TILES, 128), 1)
    return (column == 0) | ((column == 1) & (lane < 64))


PAIRS = ((2, 3, 4), (0, 1, 5))
PIECES = (((768, 0, 1152),), ((0, 0, 768), (1920, 768, 384)))
HALF = 1152


def relay(tile_ref, s_ref, part, first):
    def parent(g, carry):
        for n, q in enumerate(PAIRS[part]):
            for c in range(3):
                lanes = slice(128 * (3 * n + c), 128 * (3 * n + c) + 128)
                s_ref[first + g, :, lanes] = tile_ref[pl.ds((g * 6 + c) * 8 + q + 1, 2, stride=24), :]
        return carry

    lax.fori_loop(0, PAR, parent, 0)


def unrelay(sum_ref, tile_ref, part):
    def parent(g, carry):
        for n, q in enumerate(PAIRS[part]):
            for c in range(3):
                lanes = slice(128 * (3 * n + c), 128 * (3 * n + c) + 128)
                tile_ref[pl.ds((g * 6 + c) * 8 + q + 1, 2, stride=24), :] = sum_ref[g, :, lanes]
        return carry

    lax.fori_loop(0, PAR, parent, 0)


def swap(s_ref, x_ref, block):
    def source(i, carry):
        at = block * 8 + i
        x_ref[at, 0:1, :] = s_ref[at, 1:2, :]
        x_ref[at, 1:2, :] = s_ref[at, 0:1, :]
        return carry

    lax.fori_loop(0, PAR, source, 0, unroll=2)


GROUP = 4


def add_pairs(part, key_ref, table_ref, s_ref, x_ref, block, first_target, acc):
    acc = [list(a) for a in acc]
    pieces = PIECES[part]
    for u in range(PAR):
        source = block * 8 + u
        for p, (at, to, n) in enumerate(pieces):
            s = s_ref[source, :, to : to + n]
            x = x_ref[source, :, to : to + n]
            for j in range(GROUP):
                t = table_ref[key_ref[source, first_target + j], :, at : at + n].astype(jnp.float32)
                acc[j][p] = acc[j][p] + t * s
                acc[j][len(pieces) + p] = acc[j][len(pieces) + p] + t * x
    return tuple(tuple(a) for a in acc)


def middle_kernel(
    parent_hbm, octant_hbm, child_hbm, src_hbm, off_hbm, count_hbm, table_hbm, left_hbm, right_hbm, phases_hbm,
    out_ref,
    parent_ref, octant_ref, child_ref, src_ref, off_ref, count_ref, table_ref, left_ref, right_ref, base_ref,
    key_ref, index_ref, z_ref, phase_ref, tile_ref, pack_ref, halo_ref,
    sa_ref, sb_ref, xa_ref, xb_ref, acca_ref, accb_ref, pa_ref, pb_ref, gota_ref, gotb_ref, sum_ref,
    local_sem, send_sem, recv_sem,
):
    clus, direction, core, x, z = position()
    after = (clus, lax.rem(direction + 1, N_DIR))
    before = (clus, lax.rem(direction + N_DIR - 1, N_DIR))
    source_me = (1 - core) * x + core * z
    target_me = (1 - core) * z + core * x
    source_blocks = [lax.rem(source_me + r, 4) for r in range(4)]
    target_blocks = [lax.rem(target_me + r, 4) for r in range(4)]
    source_peers = [(gather_member(core, x, z, k), direction) for k in source_blocks[1:]]
    target_peers = [(reduce_member(core, x, z, k), direction) for k in target_blocks[1:]]
    barrier = pltpu.get_barrier_semaphore()
    peers = [after, before, *source_peers, *target_peers]
    for peer in peers:
        pl.semaphore_signal(barrier, inc=1, device_id=peer, device_id_type=MESH)

    def fetch(n, src, dst):
        copy = pltpu.make_async_copy(src, dst, local_sem.at[n])
        copy.start()
        return copy

    small = [
        fetch(0, parent_hbm, parent_ref),
        fetch(1, src_hbm, src_ref),
        fetch(2, off_hbm, off_ref),
        fetch(3, count_hbm, count_ref),
    ]
    kids = [
        fetch(4 + n, child_hbm.at[pl.ds(16 * n, 16)], child_ref.at[pl.ds(16 * n, 16)]) for n in range(3)
    ]
    weights = [fetch(7, left_hbm, left_ref), fetch(8, right_hbm, right_ref)]
    base = fetch(9, phases_hbm.at[direction], base_ref)
    octants = fetch(10, octant_hbm, octant_ref)
    z_ref[2 * KIDS : 2 * KIDS + 2] = jnp.zeros((2, 8, 384), jnp.float32)
    table = fetch(11, table_hbm, table_ref.at[pl.ds(0, OFFSETS)])
    table_ref[OFFSETS] = jnp.zeros((2, 2304), jnp.bfloat16)

    for copy in small:
        copy.wait()
    build_index(parent_ref, src_ref, off_ref, count_ref, key_ref)
    index = fetch(0, key_ref, index_ref)
    for copy in weights:
        copy.wait()
    for n in range(6):
        if n % 2 == 0:
            kids[n // 2].wait()
        xs = split(child_ref[8 * n : 8 * n + 8].reshape(128, 128))
        eo = dot3((left_ref[0], left_ref[1]), xs)
        y = split(jnp.concatenate([eo[:128], eo[128:]], axis=1))
        z_ref[16 * n : 16 * n + 16] = dot3(y, (right_ref[0], right_ref[1])).reshape(16, 8, 384)
    base.wait()
    octant_tables(base_ref, phase_ref)
    octants.wait()
    index.wait()

    def parent(g, carry):
        acc = [jnp.zeros((8, 128), jnp.float32) for _ in range(6)]
        for m in range(8):
            k = index_ref[32 + g, m]
            o = octant_ref[index_ref[32 + g, 8 + m]]
            for c in range(3):
                re = z_ref[k * 2, :, 128 * c : 128 * c + 128]
                im = z_ref[k * 2 + 1, :, 128 * c : 128 * c + 128]
                fr = phase_ref[o * 6 + c]
                fi = phase_ref[o * 6 + 3 + c]
                acc[c] = acc[c] + (re * fr - im * fi)
                acc[3 + c] = acc[3 + c] + (re * fi + im * fr)
        for t in range(6):
            tile_ref[pl.ds(aligned((g * 6 + t) * 8), 8), :] = acc[t]
        return carry

    lax.fori_loop(0, PAR, parent, 0)

    pl.semaphore_wait(barrier, len(peers))

    def send(n, src, dst, peer):
        copy = pltpu.make_async_remote_copy(
            src, dst, send_sem.at[n], recv_sem.at[n], device_id=peer, device_id_type=MESH
        )
        copy.start()
        return copy

    pack_ref[0] = tile_ref[pl.ds(7, TILES, stride=8), :]
    forward = send(0, pack_ref.at[0], halo_ref.at[0], after)
    pack_ref[1] = tile_ref[pl.ds(0, TILES, stride=8), :]
    backward = send(1, pack_ref.at[1], halo_ref.at[1], before)
    own = source_me * 8
    relay(tile_ref, sa_ref, 0, own)
    block_a = sa_ref.at[pl.ds(own, 8)]
    gather_a = [send(2 + r, block_a, block_a, peer) for r, peer in enumerate(source_peers)]
    swap(sa_ref, xa_ref, source_me)
    table.wait()

    parts = ((sa_ref, xa_ref, acca_ref, pa_ref), (sb_ref, xb_ref, accb_ref, pb_ref))

    def own_pass(part):
        s_ref, x_ref, acc_ref, _ = parts[part]
        k = len(PIECES[part])

        def group(i, carry):
            j, g = lax.div(i, 2), lax.rem(i, 2) * GROUP
            zero = tuple(jnp.zeros((2, n), jnp.float32) for _ in range(2) for _, _, n in PIECES[part])
            acc = add_pairs(
                part, index_ref, table_ref, s_ref, x_ref, source_me, reduce_member(core, x, z, j) * 8 + g, (zero,) * GROUP
            )
            for t in range(GROUP):
                for p, (_, to, n) in enumerate(PIECES[part]):
                    acc_ref[j * 8 + g + t, 0, :, to : to + n] = acc[t][p]
                    acc_ref[j * 8 + g + t, 1, :, to : to + n] = acc[t][k + p]
            return carry

        lax.fori_loop(0, 32 // GROUP, group, 0)

    def rest_pass(part, j):
        s_ref, x_ref, acc_ref, p_ref = parts[part]
        k = len(PIECES[part])

        def group(i, carry):
            g = i * GROUP
            acc = tuple(
                tuple(acc_ref[j * 8 + g + t, h, :, to : to + n] for h in range(2) for _, to, n in PIECES[part])
                for t in range(GROUP)
            )

            def block(r, acc):
                return add_pairs(
                    part, index_ref, table_ref, s_ref, x_ref, lax.rem(source_me + r, 4),
                    reduce_member(core, x, z, j) * 8 + g, acc,
                )

            acc = lax.fori_loop(1, 4, block, acc)
            for t in range(GROUP):
                for p, (_, to, n) in enumerate(PIECES[part]):
                    a, b = acc[t][p], acc[t][k + p]
                    p_ref[j * 8 + g + t, 0:1, to : to + n] = a[0:1] - a[1:2]
                    p_ref[j * 8 + g + t, 1:2, to : to + n] = b[0:1] + b[1:2]
            return carry

        lax.fori_loop(0, PAR // GROUP, group, 0)

    own_pass(0)

    even = even_lanes()
    forward.wait_recv()
    got = halo_ref[0]
    at1, at2, at6 = (pl.ds(s, TILES, stride=8) for s in (1, 2, 6))
    tile_ref[at1, :] = tile_ref[at1, :] + jnp.where(even, 0.0, got)
    tile_ref[at2, :] = tile_ref[at2, :] + jnp.where(even, got, 0.0)
    backward.wait_recv()
    tile_ref[at6, :] = tile_ref[at6, :] + halo_ref[1]
    relay(tile_ref, sb_ref, 1, own)
    block_b = sb_ref.at[pl.ds(own, 8)]
    gather_b = [send(5 + r, block_b, block_b, peer) for r, peer in enumerate(source_peers)]
    swap(sb_ref, xb_ref, source_me)
    own_pass(1)

    reduces = []
    for part, gathers, got_ref in ((0, gather_a, gota_ref), (1, gather_b, gotb_ref)):
        s_ref, x_ref, _, p_ref = parts[part]
        for r, copy in enumerate(gathers):
            copy.wait_recv()
        for r in range(1, 4):
            swap(s_ref, x_ref, source_blocks[r])
        for r in range(1, 4):
            rest_pass(part, target_blocks[r])
            reduces.append(
                send(8 + 3 * part + r - 1, p_ref.at[pl.ds(target_blocks[r] * 8, 8)], got_ref.at[r - 1], target_peers[r - 1])
            )
        rest_pass(part, target_blocks[0])

    def total(part, got_ref):
        p_ref = parts[part][3]
        for copy in reduces[3 * part : 3 * part + 3]:
            copy.wait_recv()

        def parent(g, carry):
            sum_ref[g] = (p_ref[target_me * 8 + g] + got_ref[0, g]) + (got_ref[1, g] + got_ref[2, g])
            return carry

        lax.fori_loop(0, PAR, parent, 0)
        unrelay(sum_ref, out_ref, part)

    total(0, gota_ref)
    total(1, gotb_ref)
    pack_ref[2] = jnp.where(even, out_ref[at2, :], out_ref[at1, :])
    last_back = send(14, pack_ref.at[2], halo_ref.at[2], before)
    pack_ref[3] = out_ref[at6, :]
    last_on = send(15, pack_ref.at[3], halo_ref.at[3], after)
    for copy in (forward, backward, *gather_a, *gather_b, *reduces):
        copy.wait_send()
    last_back.wait()
    last_on.wait()
    out_ref[pl.ds(7, TILES, stride=8), :] = halo_ref[2]
    out_ref[pl.ds(0, TILES, stride=8), :] = halo_ref[3]


def disaggregate_kernel(
    parent_ref, octant_ref, tile_ref, right_ref, left_ref, phases_ref,
    out_ref, r_ref, base_ref, table_ref, sem,
):
    copy = pltpu.make_async_copy(phases_ref.at[lax.axis_index("dir")], base_ref, sem)
    copy.start()
    copy.wait()
    octant_tables(base_ref, table_ref)

    def child(k, carry):
        g, o = parent_ref[0, k], octant_ref[k]
        for c in range(3):
            re = tile_ref[pl.ds(pl.multiple_of((g * 6 + c) * 8, 8), 8), :]
            im = tile_ref[pl.ds(pl.multiple_of((g * 6 + 3 + c) * 8, 8), 8), :]
            fr = table_ref[o * 6 + c]
            fi = table_ref[o * 6 + 3 + c]
            r_ref[pl.ds(pl.multiple_of(k * 16, 8), 8), 128 * c : 128 * c + 128] = re * fr + im * fi
            r_ref[pl.ds(pl.multiple_of(k * 16 + 8, 8), 8), 128 * c : 128 * c + 128] = im * fr - re * fi
        return carry

    lax.fori_loop(0, KIDS, child, 0, unroll=4)
    for n in range(6):
        hi, lo = split(r_ref[128 * n : 128 * n + 128, :])
        e = dot3((hi[:, :256], lo[:, :256]), (right_ref[0, 0], right_ref[1, 0]))
        o = dot3((hi[:, 128:], lo[:, 128:]), (right_ref[0, 1], right_ref[1, 1]))
        v = split(jnp.concatenate([e, o], axis=0))
        out_ref[8 * n : 8 * n + 8] = dot3((left_ref[0], left_ref[1]), v).reshape(8, 2, 8, 128)


VMEM_SPEC = pl.BlockSpec(memory_space=pltpu.VMEM)
SMEM_SPEC = pl.BlockSpec(memory_space=pltpu.SMEM)
ANY_SPEC = pl.BlockSpec(memory_space=pl.ANY)
HBM_SPEC = pl.BlockSpec(memory_space=pltpu.HBM)
LIMIT = 63 * 2**20


def f32(*shape):
    return jax.ShapeDtypeStruct(shape, jnp.float32)


def on_device(child, table, child_parent, child_octant, partner_src, partner_off, partner_count):
    up_left, up_right, down_right, down_left, phases = (jnp.asarray(a) for a in constants())
    vm = functools.partial(pltpu.VMEM, dtype=jnp.float32)
    ints = functools.partial(pltpu.VMEM, dtype=jnp.int32)
    bf16 = functools.partial(pltpu.VMEM, dtype=jnp.bfloat16)
    incoming = pl.pallas_call(
        middle_kernel,
        out_shape=f32(8 * TILES, 128),
        in_specs=[HBM_SPEC] * 10,
        out_specs=VMEM_SPEC,
        scratch_shapes=[
            ints((1, KIDS)), pltpu.SMEM((KIDS,), jnp.int32), vm((KIDS, 2, 8, 128)), ints((56, 128)), ints((56, 128)),
            ints((1, 128)), bf16((OFFSETS + 1, 2, 2304)), bf16((2, 256, 128)), bf16((2, 256, 384)), vm((144, 128)),
            ints((40, 128)), pltpu.SMEM((40, 128), jnp.int32), vm((2 * KIDS + 2, 8, 384)), vm((48, 8, 128)), vm((384, 128)),
            vm((4, TILES, 128)), vm((4, TILES, 128)),
            *[vm((32, 2, HALF))] * 4, *[vm((32, 2, 2, HALF))] * 2, *[vm((32, 2, HALF))] * 2,
            *[vm((3, 8, 2, HALF))] * 2, vm((8, 2, HALF)),
            pltpu.SemaphoreType.DMA((12,)), pltpu.SemaphoreType.DMA((16,)), pltpu.SemaphoreType.DMA((16,)),
        ],
        compiler_params=pltpu.CompilerParams(collective_id=0, has_side_effects=True, vmem_limit_bytes=LIMIT),
        name="middle",
    )(
        child_parent, child_octant, child, partner_src.T, partner_off.T, partner_count.reshape(1, 128), table,
        up_left, up_right, phases,
    )
    return pl.pallas_call(
        disaggregate_kernel,
        out_shape=f32(KIDS, 2, 8, 128),
        in_specs=[SMEM_SPEC] * 2 + [VMEM_SPEC] * 3 + [ANY_SPEC],
        out_specs=VMEM_SPEC,
        scratch_shapes=[vm((768, 384)), vm((144, 128)), vm((48, 8, 128)), pltpu.SemaphoreType.DMA],
        compiler_params=pltpu.CompilerParams(vmem_limit_bytes=LIMIT),
        name="disaggregate",
    )(child_parent, child_octant, incoming, down_right, down_left, phases)


def solution(mesh):
    return jax.shard_map(
        on_device,
        mesh=mesh,
        in_specs=(P("clus", None, "dir", None), P(None, None, "dir"), P("clus", None), P("clus"), P(), P(), P()),
        out_specs=P("clus", None, "dir", None),
        check_vma=False,
    )
```

```python
import functools
import math

import jax
import jax.numpy as jnp
import ml_dtypes
import numpy as np
from jax import lax
from jax.experimental import pallas as pl
from jax.experimental.pallas import tpu as pltpu
from jax.sharding import PartitionSpec as P

NT_C, NP_C, NT_P, NP_P = 128, 256, 192, 384
OFFSETS = 316
N_CLUS, N_DIR = 16, 32
PAR, KIDS = 8, 48
TILES = PAR * 6
MESH = pl.DeviceIdType.MESH
EVEN = np.array([-2, 0, 2, 4, 6, 8, 10, 14])
ODD = np.array([-1, 1, 3, 5, 7, 9, 11, 13])


def lagrange(t):
    out = []
    for m in range(5):
        w = np.ones_like(t)
        for n in range(5):
            if n != m:
                w = w * (t - n) / (m - n)
        out.append(w)
    return out


def polar_matrix():
    x = (np.arange(NT_P) + 0.5) * NT_C / NT_P - 0.5
    s = np.clip(np.floor(x + 0.5).astype(int) - 2, 0, NT_C - 5)
    w = lagrange(x - s)
    m = np.zeros((NT_P, NT_C))
    for k in range(5):
        m[np.arange(NT_P), s + k] = w[k]
    return m


def azimuth_rows(rows):
    x = rows * NP_C / NP_P
    b = np.floor(x + 0.5).astype(int)
    w = lagrange(x - b + 2)
    m = np.zeros((len(rows), 8))
    for k in range(5):
        for j in range(len(rows)):
            i = b[j] + k - 2
            if 0 <= i < 8:
                m[j, i] = w[k][j]
    return m


def halves(a):
    a = a.astype(np.float32)
    hi = a.astype(ml_dtypes.bfloat16)
    lo = (a - hi.astype(np.float32)).astype(ml_dtypes.bfloat16)
    return np.stack([hi, lo])


def in_tiles(even, odd):
    return np.stack([even[:, :128], np.concatenate([even[:, 128:], odd[:, :64]], 1), odd[:, 64:]])


@functools.cache
def constants():
    p = polar_matrix()
    ae, ao = azimuth_rows(EVEN), azimuth_rows(ODD)
    eye = np.eye(16)
    up_left = halves(np.concatenate([np.kron(eye, ae), np.kron(eye, ao)], 0))
    w = np.zeros((256, 384))
    w[:128, :192] = p.T
    w[128:, 192:] = p.T
    up_right = halves(w)
    down_right = halves(np.stack([w[:128, :256].T, w[128:, 128:].T]))
    down_left = halves(np.concatenate([np.kron(eye, ae.T), np.kron(eye, ao.T)], 1))
    theta = math.pi * (np.arange(NT_P) + 0.5) / NT_P
    phases = np.zeros((N_DIR, 3, 2, 3, 8, 128))
    for d in range(N_DIR):
        angle = []
        for rows in (EVEN, ODD):
            phi = 2 * math.pi * ((12 * d + rows) % NP_P) / NP_P
            angle.append(
                8 * math.pi
                * np.stack(
                    [
                        np.sin(theta) * np.cos(phi)[:, None],
                        np.sin(theta) * np.sin(phi)[:, None],
                        np.cos(theta) * np.ones((8, 1)),
                    ]
                )
            )
        for k in range(3):
            t = in_tiles(angle[0][k], angle[1][k])
            phases[d, k] = np.stack([np.cos(t), np.sin(t)])
    return up_left, up_right, down_right, down_left, phases.reshape(N_DIR, 144, 128).astype(np.float32)


def split(x):
    hi = x.astype(jnp.bfloat16)
    return hi, (x - hi.astype(jnp.float32)).astype(jnp.bfloat16)


def dot3(a, b):
    f = functools.partial(jnp.dot, preferred_element_type=jnp.float32)
    return f(a[0], b[0]) + (f(a[1], b[0]) + f(a[0], b[1]))


def position():
    clus, direction = lax.axis_index("clus"), lax.axis_index("dir")
    core = lax.rem(direction, 2)
    x, z = lax.rem(clus, 4), lax.div(clus, 4)
    return clus, direction, core, x, z


def gather_member(core, x, z, k):
    return (1 - core) * (z * 4 + k) + core * (k * 4 + x)


def reduce_member(core, x, z, k):
    return (1 - core) * (k * 4 + x) + core * (z * 4 + k)


def octant_tables(base, table, edge):
    def tile(k, a, c):
        r = (k * 6 + a * 3 + c) * 8
        return base[r : r + 8, :]

    for c in range(3):
        ar, ai, br, bi, cr, ci = (tile(k, a, c) for k in range(3) for a in range(2))
        rr, ii, ri, ir = ar * br, ai * bi, ar * bi, ai * br
        for sx, sy, re, im in ((1, 1, rr - ii, ri + ir), (1, -1, rr + ii, ir - ri)):
            pr, pi, qr, qi = re * cr, im * ci, re * ci, im * cr
            for sz, fr, fi in ((1, pr - pi, qr + qi), (-1, pr + pi, qi - qr)):
                for sign in (1, -1):
                    o = (sx * sign < 0) + 2 * (sy * sign < 0) + 4 * (sz * sign < 0)
                    for t, f in ((c, fr), (3 + c, fi if sign > 0 else -fi)):
                        table[o * 6 + t] = f
                        edge[0, t, o : o + 1, :] = f[0:1]
                        edge[1, t, o : o + 1, :] = f[7:8]


def aligned(i, n=8):
    return pl.multiple_of(i, n)


def build_kids(parent_ref, kids_ref):
    parent = lax.broadcasted_iota(jnp.int32, (8, KIDS), 0)
    start = jnp.sum((parent_ref[...] < parent).astype(jnp.int32), axis=1, keepdims=True)
    number = jnp.sum((parent_ref[...] == parent).astype(jnp.int32), axis=1, keepdims=True)
    lane = lax.broadcasted_iota(jnp.int32, (8, 128), 1)
    own = jnp.where(lane < number, start + lane, KIDS)
    kids_ref[...] = jnp.where(lane < 8, own, jnp.minimum(start + lane - 8, KIDS - 1))


def build_index(src_ref, off_ref, count_ref, key_ref):
    clus, direction, core, x, z = position()
    src = src_ref[...]
    off = off_ref[...]
    slot = lax.broadcasted_iota(jnp.int32, src.shape, 0)
    own_x, own_z = (src >> 3) & 3, src >> 5
    here = jnp.where(core == 0, own_z, own_x) == jnp.where(core == 0, z, x)
    local = jnp.where(core == 0, own_x, own_z) * 8 + (src & 7)
    local = jnp.where(here & (slot < count_ref[...]), local, -1)
    which = lax.broadcasted_iota(jnp.int32, (32, 128), 0)
    key = jnp.full((32, 128), OFFSETS, jnp.int32)
    for p in range(src.shape[0]):
        key = jnp.where(which == local[p : p + 1], off[p : p + 1], key)
    key_ref[...] = key


def one_hot(row, n):
    square = (KIDS, KIDS)
    diagonal = lax.broadcasted_iota(jnp.int32, square, 0) == lax.broadcasted_iota(jnp.int32, square, 1)
    column = jnp.sum(jnp.where(diagonal, row, 0), axis=1, keepdims=True)
    hot = column == lax.broadcasted_iota(jnp.int32, (KIDS, n), 1)
    return jnp.where(hot, 1.0, 0.0).astype(jnp.bfloat16)


def pick(hot, tiles):
    hi, lo = split(jnp.concatenate(tiles, axis=1))
    f = functools.partial(jnp.dot, preferred_element_type=jnp.float32)
    return f(hot, hi) + f(hot, lo)


def even_lanes():
    column = lax.rem(lax.broadcasted_iota(jnp.int32, (TILES, 128), 0), 3)
    lane = lax.broadcasted_iota(jnp.int32, (TILES, 128), 1)
    return (column == 0) | ((column == 1) & (lane < 64))


PAIRS = ((2, 3, 4), (0, 1, 5))
PIECES = (((768, 0, 1152),), ((0, 0, 768), (1920, 768, 384)))
HALF = 1152


def relay(tile_ref, s_ref, part, first):
    def parent(g, carry):
        for n, q in enumerate(PAIRS[part]):
            for c in range(3):
                lanes = slice(128 * (3 * n + c), 128 * (3 * n + c) + 128)
                s_ref[first + g, :, lanes] = tile_ref[pl.ds((g * 6 + c) * 8 + q + 1, 2, stride=24), :]
        return carry

    lax.fori_loop(0, PAR, parent, 0)


def unrelay(sum_ref, tile_ref, part):
    def parent(g, carry):
        for n, q in enumerate(PAIRS[part]):
            for c in range(3):
                lanes = slice(128 * (3 * n + c), 128 * (3 * n + c) + 128)
                tile_ref[pl.ds((g * 6 + c) * 8 + q + 1, 2, stride=24), :] = sum_ref[g, :, lanes]
        return carry

    lax.fori_loop(0, PAR, parent, 0)


def swap(s_ref, x_ref, block):
    def source(i, carry):
        at = block * 8 + i
        x_ref[at, 0:1, :] = s_ref[at, 1:2, :]
        x_ref[at, 1:2, :] = s_ref[at, 0:1, :]
        return carry

    lax.fori_loop(0, PAR, source, 0, unroll=2)


GROUP = 4


def add_pairs(part, key_ref, table_ref, s_ref, x_ref, block, first_target, acc):
    acc = [list(a) for a in acc]
    pieces = PIECES[part]
    for u in range(PAR):
        source = block * 8 + u
        for p, (at, to, n) in enumerate(pieces):
            s = s_ref[source, :, to : to + n]
            x = x_ref[source, :, to : to + n]
            for j in range(GROUP):
                t = table_ref[key_ref[source, first_target + j], :, at : at + n].astype(jnp.float32)
                acc[j][p] = acc[j][p] + t * s
                acc[j][len(pieces) + p] = acc[j][len(pieces) + p] + t * x
    return tuple(tuple(a) for a in acc)


def middle_kernel(
    parent_hbm, octant_hbm, child_hbm, src_hbm, off_hbm, count_hbm, table_hbm, left_hbm, right_hbm, phases_hbm,
    right2_hbm, left2_hbm,
    out_ref,
    parent_ref, octants_ref, parents_ref, octant_ref, child_ref, src_ref, off_ref, count_ref, table_ref, left_ref,
    right_ref, base_ref, right2_ref, left2_ref, edge_ref,
    key_ref, index_ref, kids_ref, kid_ref, z_ref, phase_ref, tile_ref, inc_ref, r_ref, pack_ref, halo_ref,
    sa_ref, sb_ref, xa_ref, xb_ref, acca_ref, accb_ref, pa_ref, pb_ref, gota_ref, gotb_ref, sum_ref,
    local_sem, send_sem, recv_sem,
):
    clus, direction, core, x, z = position()
    after = (clus, lax.rem(direction + 1, N_DIR))
    before = (clus, lax.rem(direction + N_DIR - 1, N_DIR))
    source_me = (1 - core) * x + core * z
    target_me = (1 - core) * z + core * x
    source_blocks, target_blocks = (
        [me, 3 - me, lax.rem(me + 2, 4), me + 1 - 2 * lax.rem(me, 2)] for me in (source_me, target_me)
    )
    source_peers = [(gather_member(core, x, z, k), direction) for k in source_blocks[1:]]
    target_peers = [(reduce_member(core, x, z, k), direction) for k in target_blocks[1:]]
    barrier = pltpu.get_barrier_semaphore()
    peers = [after, before, *source_peers, *target_peers]
    for peer in peers:
        pl.semaphore_signal(barrier, inc=1, device_id=peer, device_id_type=MESH)

    def fetch(n, src, dst):
        copy = pltpu.make_async_copy(src, dst, local_sem.at[n])
        copy.start()
        return copy

    parents = fetch(0, parent_hbm, parent_ref)
    first = [
        fetch(1, left_hbm, left_ref),
        fetch(2, child_hbm, child_ref),
        fetch(3, right_hbm, right_ref),
        fetch(4, phases_hbm.at[direction], base_ref),
        fetch(5, src_hbm, src_ref),
        fetch(6, off_hbm, off_ref),
        fetch(7, count_hbm, count_ref),
    ]
    second = [
        fetch(8, octant_hbm, octant_ref),
        fetch(9, parent_hbm, parents_ref),
        fetch(10, octant_hbm, octants_ref),
    ]
    z_ref[2 * KIDS : 2 * KIDS + 2] = jnp.zeros((2, 8, 384), jnp.float32)
    table_ref[OFFSETS] = jnp.zeros((2, 2304), jnp.bfloat16)
    parents.wait()
    build_kids(parent_ref, kids_ref)
    kids = fetch(0, kids_ref, kid_ref)
    for copy in first:
        copy.wait()
    third = [
        fetch(11, table_hbm, table_ref.at[pl.ds(0, OFFSETS)]),
        fetch(12, right2_hbm, right2_ref),
        fetch(13, left2_hbm, left2_ref),
    ]
    build_index(src_ref, off_ref, count_ref, key_ref)
    for n in range(6):
        xs = split(child_ref[8 * n : 8 * n + 8].reshape(128, 128))
        eo = dot3((left_ref[0], left_ref[1]), xs)
        y = split(jnp.concatenate([eo[:128], eo[128:]], axis=1))
        z_ref[16 * n : 16 * n + 16] = dot3(y, (right_ref[0], right_ref[1])).reshape(16, 8, 384)
    octant_tables(base_ref, phase_ref, edge_ref)
    index = fetch(1, key_ref, index_ref)
    kids.wait()
    for copy in second:
        copy.wait()

    def parent(g, carry):
        acc = [jnp.zeros((8, 128), jnp.float32) for _ in range(6)]
        for m in range(8):
            k = kid_ref[g, m]
            o = octant_ref[0, kid_ref[g, 8 + m]]
            for c in range(3):
                re = z_ref[k * 2, :, 128 * c : 128 * c + 128]
                im = z_ref[k * 2 + 1, :, 128 * c : 128 * c + 128]
                fr = phase_ref[o * 6 + c]
                fi = phase_ref[o * 6 + 3 + c]
                acc[c] = acc[c] + (re * fr - im * fi)
                acc[3 + c] = acc[3 + c] + (re * fi + im * fr)
        for t in range(6):
            tile_ref[pl.ds(aligned((g * 6 + t) * 8), 8), :] = acc[t]
        return carry

    lax.fori_loop(0, PAR, parent, 0)

    pl.semaphore_wait(barrier, len(peers))

    def send(n, src, dst, peer):
        copy = pltpu.make_async_remote_copy(
            src, dst, send_sem.at[n], recv_sem.at[n], device_id=peer, device_id_type=MESH
        )
        copy.start()
        return copy

    pack_ref[0] = tile_ref[pl.ds(7, TILES, stride=8), :]
    forward = send(0, pack_ref.at[0], halo_ref.at[0], after)
    pack_ref[1] = tile_ref[pl.ds(0, TILES, stride=8), :]
    backward = send(1, pack_ref.at[1], halo_ref.at[1], before)
    own = source_me * 8
    relay(tile_ref, sa_ref, 0, own)
    block_a = sa_ref.at[pl.ds(own, 8)]
    gather_a = [send(2 + r, block_a, block_a, peer) for r, peer in enumerate(source_peers)]
    swap(sa_ref, xa_ref, source_me)
    for copy in (index, *third):
        copy.wait()

    parts = ((sa_ref, xa_ref, acca_ref, pa_ref), (sb_ref, xb_ref, accb_ref, pb_ref))

    def own_pass(part):
        s_ref, x_ref, acc_ref, _ = parts[part]
        k = len(PIECES[part])

        def group(i, carry):
            j, g = lax.div(i, 2), lax.rem(i, 2) * GROUP
            zero = tuple(jnp.zeros((2, n), jnp.float32) for _ in range(2) for _, _, n in PIECES[part])
            acc = add_pairs(
                part, index_ref, table_ref, s_ref, x_ref, source_me, reduce_member(core, x, z, j) * 8 + g, (zero,) * GROUP
            )
            for t in range(GROUP):
                for p, (_, to, n) in enumerate(PIECES[part]):
                    acc_ref[j * 8 + g + t, 0, :, to : to + n] = acc[t][p]
                    acc_ref[j * 8 + g + t, 1, :, to : to + n] = acc[t][k + p]
            return carry

        lax.fori_loop(0, 32 // GROUP, group, 0)

    def rest_pass(part, j):
        s_ref, x_ref, acc_ref, p_ref = parts[part]
        k = len(PIECES[part])

        def group(i, carry):
            g = i * GROUP
            acc = tuple(
                tuple(acc_ref[j * 8 + g + t, h, :, to : to + n] for h in range(2) for _, to, n in PIECES[part])
                for t in range(GROUP)
            )

            def block(r, acc):
                return add_pairs(
                    part, index_ref, table_ref, s_ref, x_ref, lax.rem(source_me + r, 4),
                    reduce_member(core, x, z, j) * 8 + g, acc,
                )

            acc = lax.fori_loop(1, 4, block, acc)
            for t in range(GROUP):
                for p, (_, to, n) in enumerate(PIECES[part]):
                    a, b = acc[t][p], acc[t][k + p]
                    p_ref[j * 8 + g + t, 0:1, to : to + n] = a[0:1] - a[1:2]
                    p_ref[j * 8 + g + t, 1:2, to : to + n] = b[0:1] + b[1:2]
            return carry

        lax.fori_loop(0, PAR // GROUP, group, 0)

    own_pass(0)

    even = even_lanes()
    forward.wait_recv()
    got = halo_ref[0]
    at1, at2, at6 = (pl.ds(s, TILES, stride=8) for s in (1, 2, 6))
    tile_ref[at1, :] = tile_ref[at1, :] + jnp.where(even, 0.0, got)
    tile_ref[at2, :] = tile_ref[at2, :] + jnp.where(even, got, 0.0)
    backward.wait_recv()
    tile_ref[at6, :] = tile_ref[at6, :] + halo_ref[1]
    relay(tile_ref, sb_ref, 1, own)
    block_b = sb_ref.at[pl.ds(own, 8)]
    gather_b = [send(5 + r, block_b, block_b, peer) for r, peer in enumerate(source_peers)]
    swap(sb_ref, xb_ref, source_me)
    own_pass(1)

    reduces = []
    for part, gathers, got_ref in ((0, gather_a, gota_ref), (1, gather_b, gotb_ref)):
        s_ref, x_ref, _, p_ref = parts[part]
        for r, copy in enumerate(gathers):
            copy.wait_recv()
        for r in range(1, 4):
            swap(s_ref, x_ref, source_blocks[r])
        for r in range(1, 4):
            rest_pass(part, target_blocks[r])
            reduces.append(
                send(8 + 3 * part + r - 1, p_ref.at[pl.ds(target_blocks[r] * 8, 8)], got_ref.at[r - 1], target_peers[r - 1])
            )
        rest_pass(part, target_blocks[0])

    def total(part, got_ref):
        p_ref = parts[part][3]
        for copy in reduces[3 * part : 3 * part + 3]:
            copy.wait_recv()

        def parent(g, carry):
            sum_ref[g] = (p_ref[target_me * 8 + g] + got_ref[0, g]) + (got_ref[1, g] + got_ref[2, g])
            return carry

        lax.fori_loop(0, PAR, parent, 0)
        unrelay(sum_ref, tile_ref, part)

    total(1, gotb_ref)
    pack_ref[2] = jnp.where(even, tile_ref[at2, :], tile_ref[at1, :])
    last_back = send(14, pack_ref.at[2], halo_ref.at[2], before)
    pack_ref[3] = tile_ref[at6, :]
    last_on = send(15, pack_ref.at[3], halo_ref.at[3], after)
    total(0, gota_ref)
    pair = lax.broadcasted_iota(jnp.int32, (8, 128), 0)
    inside = (pair > 0) & (pair < 7)
    for t in range(TILES):
        inc_ref[t] = jnp.where(inside, tile_ref[8 * t : 8 * t + 8, :], 0.0)

    def child(k, carry):
        g, o = parents_ref[0, k], octant_ref[0, k]
        for c in range(3):
            re, im = inc_ref[g * 6 + c], inc_ref[g * 6 + 3 + c]
            fr, fi = phase_ref[o * 6 + c], phase_ref[o * 6 + 3 + c]
            r_ref[k * 2, :, 128 * c : 128 * c + 128] = re * fr + im * fi
            r_ref[k * 2 + 1, :, 128 * c : 128 * c + 128] = im * fr - re * fi
        return carry

    lax.fori_loop(0, KIDS, child, 0, unroll=4)

    def to_child(r):
        hi, lo = split(r)
        return (
            dot3((hi[:, :256], lo[:, :256]), (right2_ref[0, 0], right2_ref[1, 0])),
            dot3((hi[:, 128:], lo[:, 128:]), (right2_ref[0, 1], right2_ref[1, 1])),
        )

    for n in range(6):
        v = split(jnp.concatenate(to_child(r_ref[16 * n : 16 * n + 16].reshape(128, 384)), axis=0))
        out_ref[128 * n : 128 * n + 128, :] = dot3((left2_ref[0], left2_ref[1]), v)
    hot_parent, hot_octant = one_hot(parent_ref[...], 8), one_hot(octants_ref[...], 8)
    shifts = [pick(hot_octant, [edge_ref[e, t] for t in range(6)]) for e in range(2)]
    for copy in (forward, backward, *gather_a, *gather_b, *reduces):
        copy.wait_send()
    last_back.wait()
    last_on.wait()
    rows = []
    for e in range(2):
        values = pick(hot_parent, [halo_ref[3 - e, pl.ds(t, 8, stride=6), :] for t in range(6)])
        re, im, fr, fi = values[:, :384], values[:, 384:], shifts[e][:, :384], shifts[e][:, 384:]
        rows += [re * fr + im * fi, im * fr - re * fi]
    even_part, odd_part = to_child(jnp.concatenate(rows, axis=0))
    weight_even, weight_odd = azimuth_rows(EVEN), azimuth_rows(ODD)
    for e, s in enumerate((0, 7)):
        for a in range(2):
            at = (2 * e + a) * KIDS
            for i in range(8):
                we, wo = float(weight_even[s, i]), float(weight_odd[s, i])
                if we or wo:
                    place = pl.ds(a * 8 + i, KIDS, stride=16)
                    out_ref[place, :] = out_ref[place, :] + (
                        we * even_part[at : at + KIDS] + wo * odd_part[at : at + KIDS]
                    )


VMEM_SPEC = pl.BlockSpec(memory_space=pltpu.VMEM)
HBM_SPEC = pl.BlockSpec(memory_space=pltpu.HBM)
LIMIT = 63 * 2**20


def f32(*shape):
    return jax.ShapeDtypeStruct(shape, jnp.float32)


def on_device(child, table, child_parent, child_octant, partner_src, partner_off, partner_count):
    up_left, up_right, down_right, down_left, phases = (jnp.asarray(a) for a in constants())
    vm = functools.partial(pltpu.VMEM, dtype=jnp.float32)
    ints = functools.partial(pltpu.VMEM, dtype=jnp.int32)
    bf16 = functools.partial(pltpu.VMEM, dtype=jnp.bfloat16)
    scalars = functools.partial(pltpu.SMEM, dtype=jnp.int32)
    out = pl.pallas_call(
        middle_kernel,
        out_shape=f32(KIDS * 16, 128),
        in_specs=[HBM_SPEC] * 12,
        out_specs=VMEM_SPEC,
        scratch_shapes=[
            ints((1, KIDS)), ints((1, KIDS)), scalars((1, KIDS)), scalars((1, KIDS)), vm((KIDS, 2, 8, 128)),
            ints((56, 128)), ints((56, 128)), ints((1, 128)), bf16((OFFSETS + 1, 2, 2304)), bf16((2, 256, 128)),
            bf16((2, 256, 384)), vm((144, 128)), bf16((2, 2, 256, 128)), bf16((2, 128, 256)), vm((2, 6, 8, 128)),
            ints((32, 128)), scalars((32, 128)), ints((8, 128)), scalars((8, 128)),
            vm((2 * KIDS + 2, 8, 384)), vm((48, 8, 128)), vm((8 * TILES, 128)), vm((TILES, 8, 128)),
            vm((2 * KIDS, 8, 384)), vm((4, TILES, 128)), vm((4, TILES, 128)),
            *[vm((32, 2, HALF))] * 4, *[vm((32, 2, 2, HALF))] * 2, *[vm((32, 2, HALF))] * 2,
            *[vm((3, 8, 2, HALF))] * 2, vm((8, 2, HALF)),
            pltpu.SemaphoreType.DMA((14,)), pltpu.SemaphoreType.DMA((16,)), pltpu.SemaphoreType.DMA((16,)),
        ],
        compiler_params=pltpu.CompilerParams(collective_id=0, has_side_effects=True, vmem_limit_bytes=LIMIT),
        name="middle",
    )(
        child_parent, child_octant.reshape(1, KIDS), child, partner_src.T, partner_off.T, partner_count.reshape(1, 128),
        table, up_left, up_right, phases, down_right, down_left,
    )
    return out.reshape(KIDS, 2, 8, 128)


def solution(mesh):
    return jax.shard_map(
        on_device,
        mesh=mesh,
        in_specs=(P("clus", None, "dir", None), P(None, None, "dir"), P("clus", None), P("clus"), P(), P(), P()),
        out_specs=P("clus", None, "dir", None),
        check_vma=False,
    )
```

```python
import functools
import math

import jax
import jax.numpy as jnp
import ml_dtypes
import numpy as np
from jax import lax
from jax.experimental import pallas as pl
from jax.experimental.pallas import tpu as pltpu
from jax.sharding import PartitionSpec as P

NT_C, NP_C, NT_P, NP_P = 128, 256, 192, 384
OFFSETS = 316
N_CLUS, N_DIR = 16, 32
PAR, KIDS = 8, 48
TILES = PAR * 6
MESH = pl.DeviceIdType.MESH
EVEN = np.array([-2, 0, 2, 4, 6, 8, 10, 14])
ODD = np.array([-1, 1, 3, 5, 7, 9, 11, 13])


def lagrange(t):
    out = []
    for m in range(5):
        w = np.ones_like(t)
        for n in range(5):
            if n != m:
                w = w * (t - n) / (m - n)
        out.append(w)
    return out


def polar_matrix():
    x = (np.arange(NT_P) + 0.5) * NT_C / NT_P - 0.5
    s = np.clip(np.floor(x + 0.5).astype(int) - 2, 0, NT_C - 5)
    w = lagrange(x - s)
    m = np.zeros((NT_P, NT_C))
    for k in range(5):
        m[np.arange(NT_P), s + k] = w[k]
    return m


def azimuth_rows(rows):
    x = rows * NP_C / NP_P
    b = np.floor(x + 0.5).astype(int)
    w = lagrange(x - b + 2)
    m = np.zeros((len(rows), 8))
    for k in range(5):
        for j in range(len(rows)):
            i = b[j] + k - 2
            if 0 <= i < 8:
                m[j, i] = w[k][j]
    return m


def halves(a):
    a = a.astype(np.float32)
    hi = a.astype(ml_dtypes.bfloat16)
    lo = (a - hi.astype(np.float32)).astype(ml_dtypes.bfloat16)
    return np.stack([hi, lo])


def in_tiles(even, odd):
    return np.stack([even[:, :128], np.concatenate([even[:, 128:], odd[:, :64]], 1), odd[:, 64:]])


@functools.cache
def constants():
    p = polar_matrix()
    ae, ao = azimuth_rows(EVEN), azimuth_rows(ODD)
    eye = np.eye(16)
    up_left = halves(np.concatenate([np.kron(eye, ae), np.kron(eye, ao)], 0))
    w = np.zeros((256, 384))
    w[:128, :192] = p.T
    w[128:, 192:] = p.T
    up_right = halves(w)
    down_right = halves(np.stack([w[:128, :256].T, w[128:, 128:].T]))
    down_left = halves(np.concatenate([np.kron(eye, ae.T), np.kron(eye, ao.T)], 1))
    theta = math.pi * (np.arange(NT_P) + 0.5) / NT_P
    phases = np.zeros((N_DIR, 3, 2, 3, 8, 128))
    for d in range(N_DIR):
        angle = []
        for rows in (EVEN, ODD):
            phi = 2 * math.pi * ((12 * d + rows) % NP_P) / NP_P
            angle.append(
                8 * math.pi
                * np.stack(
                    [
                        np.sin(theta) * np.cos(phi)[:, None],
                        np.sin(theta) * np.sin(phi)[:, None],
                        np.cos(theta) * np.ones((8, 1)),
                    ]
                )
            )
        for k in range(3):
            t = in_tiles(angle[0][k], angle[1][k])
            phases[d, k] = np.stack([np.cos(t), np.sin(t)])
    return up_left, up_right, down_right, down_left, phases.reshape(N_DIR, 144, 128).astype(np.float32)


def split(x):
    hi = x.astype(jnp.bfloat16)
    return hi, (x - hi.astype(jnp.float32)).astype(jnp.bfloat16)


def dot3(a, b):
    f = functools.partial(jnp.dot, preferred_element_type=jnp.float32)
    return f(a[0], b[0]) + (f(a[1], b[0]) + f(a[0], b[1]))


def position():
    clus, direction = lax.axis_index("clus"), lax.axis_index("dir")
    core = lax.rem(direction, 2)
    x, z = lax.rem(clus, 4), lax.div(clus, 4)
    return clus, direction, core, x, z


def gather_member(core, x, z, k):
    return (1 - core) * (z * 4 + k) + core * (k * 4 + x)


def reduce_member(core, x, z, k):
    return (1 - core) * (k * 4 + x) + core * (z * 4 + k)


def octant_tables(base, table, edge):
    def tile(k, a, c):
        r = (k * 6 + a * 3 + c) * 8
        return base[r : r + 8, :]

    for c in range(3):
        ar, ai, br, bi, cr, ci = (tile(k, a, c) for k in range(3) for a in range(2))
        rr, ii, ri, ir = ar * br, ai * bi, ar * bi, ai * br
        for sx, sy, re, im in ((1, 1, rr - ii, ri + ir), (1, -1, rr + ii, ir - ri)):
            pr, pi, qr, qi = re * cr, im * ci, re * ci, im * cr
            for sz, fr, fi in ((1, pr - pi, qr + qi), (-1, pr + pi, qi - qr)):
                for sign in (1, -1):
                    o = (sx * sign < 0) + 2 * (sy * sign < 0) + 4 * (sz * sign < 0)
                    for t, f in ((c, fr), (3 + c, fi if sign > 0 else -fi)):
                        table[o * 6 + t] = f
                        edge[0, t, o : o + 1, :] = f[0:1]
                        edge[1, t, o : o + 1, :] = f[7:8]


def aligned(i, n=8):
    return pl.multiple_of(i, n)


def build_kids(parent_ref, kids_ref):
    parent = lax.broadcasted_iota(jnp.int32, (8, KIDS), 0)
    start = jnp.sum((parent_ref[...] < parent).astype(jnp.int32), axis=1, keepdims=True)
    number = jnp.sum((parent_ref[...] == parent).astype(jnp.int32), axis=1, keepdims=True)
    lane = lax.broadcasted_iota(jnp.int32, (8, 128), 1)
    own = jnp.where(lane < number, start + lane, KIDS)
    kids_ref[...] = jnp.where(lane < 8, own, jnp.minimum(start + lane - 8, KIDS - 1))


def build_index(src_ref, off_ref, count_ref, key_ref):
    clus, direction, core, x, z = position()
    src = src_ref[...]
    off = off_ref[...]
    slot = lax.broadcasted_iota(jnp.int32, src.shape, 0)
    own_x, own_z = (src >> 3) & 3, src >> 5
    here = jnp.where(core == 0, own_z, own_x) == jnp.where(core == 0, z, x)
    local = jnp.where(core == 0, own_x, own_z) * 8 + (src & 7)
    local = jnp.where(here & (slot < count_ref[...]), local, -1)
    which = lax.broadcasted_iota(jnp.int32, (32, 128), 0)
    key = jnp.full((32, 128), OFFSETS, jnp.int32)
    for p in range(src.shape[0]):
        key = jnp.where(which == local[p : p + 1], off[p : p + 1], key)
    key_ref[...] = key


def one_hot(row, n):
    square = (KIDS, KIDS)
    diagonal = lax.broadcasted_iota(jnp.int32, square, 0) == lax.broadcasted_iota(jnp.int32, square, 1)
    column = jnp.sum(jnp.where(diagonal, row, 0), axis=1, keepdims=True)
    hot = column == lax.broadcasted_iota(jnp.int32, (KIDS, n), 1)
    return jnp.where(hot, 1.0, 0.0).astype(jnp.bfloat16)


def pick(hot, tiles):
    hi, lo = split(jnp.concatenate(tiles, axis=1))
    f = functools.partial(jnp.dot, preferred_element_type=jnp.float32)
    return f(hot, hi) + f(hot, lo)


def even_lanes():
    column = lax.rem(lax.broadcasted_iota(jnp.int32, (TILES, 128), 0), 3)
    lane = lax.broadcasted_iota(jnp.int32, (TILES, 128), 1)
    return (column == 0) | ((column == 1) & (lane < 64))


PAIRS = ((2, 3, 4), (0, 1, 5))
PIECES = (((768, 0, 1152),), ((0, 0, 768), (1920, 768, 384)))
HALF = 1152


def relay(tile_ref, s_ref, part, first):
    def parent(g, carry):
        for n, q in enumerate(PAIRS[part]):
            for c in range(3):
                lanes = slice(128 * (3 * n + c), 128 * (3 * n + c) + 128)
                s_ref[first + g, :, lanes] = tile_ref[pl.ds((g * 6 + c) * 8 + q + 1, 2, stride=24), :]
        return carry

    lax.fori_loop(0, PAR, parent, 0)


def unrelay(sum_ref, tile_ref, part):
    def parent(g, carry):
        for n, q in enumerate(PAIRS[part]):
            for c in range(3):
                lanes = slice(128 * (3 * n + c), 128 * (3 * n + c) + 128)
                tile_ref[pl.ds((g * 6 + c) * 8 + q + 1, 2, stride=24), :] = sum_ref[g, :, lanes]
        return carry

    lax.fori_loop(0, PAR, parent, 0)


def swap(s_ref, x_ref, block):
    def source(i, carry):
        at = block * 8 + i
        x_ref[at, 0:1, :] = s_ref[at, 1:2, :]
        x_ref[at, 1:2, :] = s_ref[at, 0:1, :]
        return carry

    lax.fori_loop(0, PAR, source, 0, unroll=2)


GROUP = 4


def add_pairs(part, key_ref, table_ref, s_ref, x_ref, block, first_target, acc):
    acc = [list(a) for a in acc]
    pieces = PIECES[part]
    for u in range(PAR):
        source = block * 8 + u
        for p, (at, to, n) in enumerate(pieces):
            s = s_ref[source, :, to : to + n]
            x = x_ref[source, :, to : to + n]
            for j in range(GROUP):
                t = table_ref[key_ref[source, first_target + j], :, at : at + n].astype(jnp.float32)
                acc[j][p] = acc[j][p] + t * s
                acc[j][len(pieces) + p] = acc[j][len(pieces) + p] + t * x
    return tuple(tuple(a) for a in acc)


def middle_kernel(
    parent_hbm, octant_hbm, child_hbm, src_hbm, off_hbm, count_hbm, table_hbm, left_hbm, right_hbm, phases_hbm,
    right2_hbm, left2_hbm,
    out_ref,
    parent_ref, octants_ref, parents_ref, octant_ref, child_ref, src_ref, off_ref, count_ref, table_ref, left_ref,
    right_ref, base_ref, right2_ref, left2_ref, edge_ref,
    key_ref, index_ref, kids_ref, kid_ref, y_ref, z_ref, phase_ref, tile_ref, inc_ref, r_ref, pack_ref, halo_ref,
    sa_ref, sb_ref, xa_ref, xb_ref, acca_ref, accb_ref, pa_ref, pb_ref, gota_ref, gotb_ref, sum_ref,
    local_sem, send_sem, recv_sem,
):
    clus, direction, core, x, z = position()
    after = (clus, lax.rem(direction + 1, N_DIR))
    before = (clus, lax.rem(direction + N_DIR - 1, N_DIR))
    source_me = (1 - core) * x + core * z
    target_me = (1 - core) * z + core * x
    source_blocks, target_blocks = (
        [me, 3 - me, lax.rem(me + 2, 4), me + 1 - 2 * lax.rem(me, 2)] for me in (source_me, target_me)
    )
    source_peers = [(gather_member(core, x, z, k), direction) for k in source_blocks[1:]]
    target_peers = [(reduce_member(core, x, z, k), direction) for k in target_blocks[1:]]
    barrier = pltpu.get_barrier_semaphore()
    peers = [after, before, *source_peers, *target_peers]
    for peer in peers:
        pl.semaphore_signal(barrier, inc=1, device_id=peer, device_id_type=MESH)

    def fetch(n, src, dst):
        copy = pltpu.make_async_copy(src, dst, local_sem.at[n])
        copy.start()
        return copy

    parents = fetch(0, parent_hbm, parent_ref)
    first = [
        fetch(1, left_hbm, left_ref),
        fetch(2, child_hbm, child_ref),
        fetch(3, right_hbm, right_ref),
        fetch(4, phases_hbm.at[direction], base_ref),
        fetch(5, src_hbm, src_ref),
        fetch(6, off_hbm, off_ref),
        fetch(7, count_hbm, count_ref),
    ]
    second = [
        fetch(8, octant_hbm, octant_ref),
        fetch(9, parent_hbm, parents_ref),
        fetch(10, octant_hbm, octants_ref),
    ]
    z_ref[2 * KIDS : 2 * KIDS + 2] = jnp.zeros((2, 8, 384), jnp.float32)
    table_ref[OFFSETS] = jnp.zeros((2, 2304), jnp.bfloat16)
    parents.wait()
    build_kids(parent_ref, kids_ref)
    kids = fetch(0, kids_ref, kid_ref)
    for copy in first:
        copy.wait()
    third = [
        fetch(11, table_hbm, table_ref.at[pl.ds(0, OFFSETS)]),
        fetch(12, right2_hbm, right2_ref),
        fetch(13, left2_hbm, left2_ref),
    ]
    build_index(src_ref, off_ref, count_ref, key_ref)
    for n in range(6):
        xs = split(child_ref[8 * n : 8 * n + 8].reshape(128, 128))
        eo = dot3((left_ref[0], left_ref[1]), xs)
        y = split(jnp.concatenate([eo[:128], eo[128:]], axis=1))
        for h in range(2):
            y_ref[h, 128 * n : 128 * n + 128, :] = y[h]
    z_ref[0 : 2 * KIDS] = dot3((y_ref[0], y_ref[1]), (right_ref[0], right_ref[1])).reshape(2 * KIDS, 8, 384)
    octant_tables(base_ref, phase_ref, edge_ref)
    index = fetch(1, key_ref, index_ref)
    kids.wait()
    for copy in second:
        copy.wait()

    def parent(g, carry):
        acc = [jnp.zeros((8, 128), jnp.float32) for _ in range(6)]
        for m in range(8):
            k = kid_ref[g, m]
            o = octant_ref[0, kid_ref[g, 8 + m]]
            for c in range(3):
                re = z_ref[k * 2, :, 128 * c : 128 * c + 128]
                im = z_ref[k * 2 + 1, :, 128 * c : 128 * c + 128]
                fr = phase_ref[o * 6 + c]
                fi = phase_ref[o * 6 + 3 + c]
                acc[c] = acc[c] + (re * fr - im * fi)
                acc[3 + c] = acc[3 + c] + (re * fi + im * fr)
        for t in range(6):
            tile_ref[pl.ds(aligned((g * 6 + t) * 8), 8), :] = acc[t]
        return carry

    lax.fori_loop(0, PAR, parent, 0)

    pl.semaphore_wait(barrier, len(peers))

    def send(n, src, dst, peer):
        copy = pltpu.make_async_remote_copy(
            src, dst, send_sem.at[n], recv_sem.at[n], device_id=peer, device_id_type=MESH
        )
        copy.start()
        return copy

    pack_ref[0] = tile_ref[pl.ds(7, TILES, stride=8), :]
    forward = send(0, pack_ref.at[0], halo_ref.at[0], after)
    pack_ref[1] = tile_ref[pl.ds(0, TILES, stride=8), :]
    backward = send(1, pack_ref.at[1], halo_ref.at[1], before)
    own = source_me * 8
    relay(tile_ref, sa_ref, 0, own)
    block_a = sa_ref.at[pl.ds(own, 8)]
    gather_a = [send(2 + r, block_a, block_a, peer) for r, peer in enumerate(source_peers)]
    swap(sa_ref, xa_ref, source_me)
    for copy in (index, *third):
        copy.wait()

    parts = ((sa_ref, xa_ref, acca_ref, pa_ref), (sb_ref, xb_ref, accb_ref, pb_ref))

    def own_pass(part):
        s_ref, x_ref, acc_ref, _ = parts[part]
        k = len(PIECES[part])

        def group(i, carry):
            j, g = lax.div(i, 2), lax.rem(i, 2) * GROUP
            zero = tuple(jnp.zeros((2, n), jnp.float32) for _ in range(2) for _, _, n in PIECES[part])
            acc = add_pairs(
                part, index_ref, table_ref, s_ref, x_ref, source_me, reduce_member(core, x, z, j) * 8 + g, (zero,) * GROUP
            )
            for t in range(GROUP):
                for p, (_, to, n) in enumerate(PIECES[part]):
                    acc_ref[j * 8 + g + t, 0, :, to : to + n] = acc[t][p]
                    acc_ref[j * 8 + g + t, 1, :, to : to + n] = acc[t][k + p]
            return carry

        lax.fori_loop(0, 32 // GROUP, group, 0)

    def rest_pass(part, j):
        s_ref, x_ref, acc_ref, p_ref = parts[part]
        k = len(PIECES[part])

        def group(i, carry):
            g = i * GROUP
            acc = tuple(
                tuple(acc_ref[j * 8 + g + t, h, :, to : to + n] for h in range(2) for _, to, n in PIECES[part])
                for t in range(GROUP)
            )

            def block(r, acc):
                return add_pairs(
                    part, index_ref, table_ref, s_ref, x_ref, lax.rem(source_me + r, 4),
                    reduce_member(core, x, z, j) * 8 + g, acc,
                )

            acc = lax.fori_loop(1, 4, block, acc)
            for t in range(GROUP):
                for p, (_, to, n) in enumerate(PIECES[part]):
                    a, b = acc[t][p], acc[t][k + p]
                    p_ref[j * 8 + g + t, 0:1, to : to + n] = a[0:1] - a[1:2]
                    p_ref[j * 8 + g + t, 1:2, to : to + n] = b[0:1] + b[1:2]
            return carry

        lax.fori_loop(0, PAR // GROUP, group, 0)

    own_pass(0)

    even = even_lanes()
    forward.wait_recv()
    got = halo_ref[0]
    at1, at2, at6 = (pl.ds(s, TILES, stride=8) for s in (1, 2, 6))
    tile_ref[at1, :] = tile_ref[at1, :] + jnp.where(even, 0.0, got)
    tile_ref[at2, :] = tile_ref[at2, :] + jnp.where(even, got, 0.0)
    backward.wait_recv()
    tile_ref[at6, :] = tile_ref[at6, :] + halo_ref[1]
    relay(tile_ref, sb_ref, 1, own)
    block_b = sb_ref.at[pl.ds(own, 8)]
    gather_b = [send(5 + r, block_b, block_b, peer) for r, peer in enumerate(source_peers)]
    swap(sb_ref, xb_ref, source_me)
    own_pass(1)

    def gathered(part, gathers):
        for copy in gathers:
            copy.wait_recv()
        for r in range(1, 4):
            swap(parts[part][0], parts[part][1], source_blocks[r])

    def reduce_to(part, r, got_ref):
        block = parts[part][3].at[pl.ds(target_blocks[r] * 8, 8)]
        return send(8 + 3 * part + r - 1, block, got_ref.at[r - 1], target_peers[r - 1])

    gathered(0, gather_a)
    for r in range(4):
        rest_pass(0, target_blocks[r])
    gathered(1, gather_b)
    reduces_b = []
    for r in range(1, 4):
        rest_pass(1, target_blocks[r])
        reduces_b.append(reduce_to(1, r, gotb_ref))
    reduces = [reduce_to(0, r, gota_ref) for r in range(1, 4)] + reduces_b
    rest_pass(1, target_blocks[0])

    def total(part, got_ref):
        p_ref = parts[part][3]
        for copy in reduces[3 * part : 3 * part + 3]:
            copy.wait_recv()

        def parent(g, carry):
            sum_ref[g] = (p_ref[target_me * 8 + g] + got_ref[0, g]) + (got_ref[1, g] + got_ref[2, g])
            return carry

        lax.fori_loop(0, PAR, parent, 0)
        unrelay(sum_ref, tile_ref, part)

    total(1, gotb_ref)
    pack_ref[2] = jnp.where(even, tile_ref[at2, :], tile_ref[at1, :])
    last_back = send(14, pack_ref.at[2], halo_ref.at[2], before)
    pack_ref[3] = tile_ref[at6, :]
    last_on = send(15, pack_ref.at[3], halo_ref.at[3], after)
    total(0, gota_ref)
    pair = lax.broadcasted_iota(jnp.int32, (8, 128), 0)
    inside = (pair > 0) & (pair < 7)
    for t in range(TILES):
        inc_ref[t] = jnp.where(inside, tile_ref[8 * t : 8 * t + 8, :], 0.0)

    def child(k, carry):
        g, o = parents_ref[0, k], octant_ref[0, k]
        for c in range(3):
            re, im = inc_ref[g * 6 + c], inc_ref[g * 6 + 3 + c]
            fr, fi = phase_ref[o * 6 + c], phase_ref[o * 6 + 3 + c]
            r_ref[k * 2, :, 128 * c : 128 * c + 128] = re * fr + im * fi
            r_ref[k * 2 + 1, :, 128 * c : 128 * c + 128] = im * fr - re * fi
        return carry

    lax.fori_loop(0, KIDS, child, 0, unroll=4)

    def to_child(r):
        hi, lo = split(r)
        return (
            dot3((hi[:, :256], lo[:, :256]), (right2_ref[0, 0], right2_ref[1, 0])),
            dot3((hi[:, 128:], lo[:, 128:]), (right2_ref[0, 1], right2_ref[1, 1])),
        )

    for n in range(6):
        v = split(jnp.concatenate(to_child(r_ref[16 * n : 16 * n + 16].reshape(128, 384)), axis=0))
        out_ref[128 * n : 128 * n + 128, :] = dot3((left2_ref[0], left2_ref[1]), v)
    hot_parent, hot_octant = one_hot(parent_ref[...], 8), one_hot(octants_ref[...], 8)
    shifts = [pick(hot_octant, [edge_ref[e, t] for t in range(6)]) for e in range(2)]
    for copy in (forward, backward, *gather_a, *gather_b, *reduces):
        copy.wait_send()
    last_back.wait()
    last_on.wait()
    rows = []
    for e in range(2):
        values = pick(hot_parent, [halo_ref[3 - e, pl.ds(t, 8, stride=6), :] for t in range(6)])
        re, im, fr, fi = values[:, :384], values[:, 384:], shifts[e][:, :384], shifts[e][:, 384:]
        rows += [re * fr + im * fi, im * fr - re * fi]
    even_part, odd_part = to_child(jnp.concatenate(rows, axis=0))
    weight_even, weight_odd = azimuth_rows(EVEN), azimuth_rows(ODD)
    for e, s in enumerate((0, 7)):
        for a in range(2):
            at = (2 * e + a) * KIDS
            for i in range(8):
                we, wo = float(weight_even[s, i]), float(weight_odd[s, i])
                if we or wo:
                    place = pl.ds(a * 8 + i, KIDS, stride=16)
                    out_ref[place, :] = out_ref[place, :] + (
                        we * even_part[at : at + KIDS] + wo * odd_part[at : at + KIDS]
                    )


VMEM_SPEC = pl.BlockSpec(memory_space=pltpu.VMEM)
HBM_SPEC = pl.BlockSpec(memory_space=pltpu.HBM)
LIMIT = 63 * 2**20


def f32(*shape):
    return jax.ShapeDtypeStruct(shape, jnp.float32)


def on_device(child, table, child_parent, child_octant, partner_src, partner_off, partner_count):
    up_left, up_right, down_right, down_left, phases = (jnp.asarray(a) for a in constants())
    vm = functools.partial(pltpu.VMEM, dtype=jnp.float32)
    ints = functools.partial(pltpu.VMEM, dtype=jnp.int32)
    bf16 = functools.partial(pltpu.VMEM, dtype=jnp.bfloat16)
    scalars = functools.partial(pltpu.SMEM, dtype=jnp.int32)
    out = pl.pallas_call(
        middle_kernel,
        out_shape=f32(KIDS * 16, 128),
        in_specs=[HBM_SPEC] * 12,
        out_specs=VMEM_SPEC,
        scratch_shapes=[
            ints((1, KIDS)), ints((1, KIDS)), scalars((1, KIDS)), scalars((1, KIDS)), vm((KIDS, 2, 8, 128)),
            ints((56, 128)), ints((56, 128)), ints((1, 128)), bf16((OFFSETS + 1, 2, 2304)), bf16((2, 256, 128)),
            bf16((2, 256, 384)), vm((144, 128)), bf16((2, 2, 256, 128)), bf16((2, 128, 256)), vm((2, 6, 8, 128)),
            ints((32, 128)), scalars((32, 128)), ints((8, 128)), scalars((8, 128)),
            bf16((2, 768, 256)), vm((2 * KIDS + 2, 8, 384)), vm((48, 8, 128)), vm((8 * TILES, 128)), vm((TILES, 8, 128)),
            vm((2 * KIDS, 8, 384)), vm((4, TILES, 128)), vm((4, TILES, 128)),
            *[vm((32, 2, HALF))] * 4, *[vm((32, 2, 2, HALF))] * 2, *[vm((32, 2, HALF))] * 2,
            *[vm((3, 8, 2, HALF))] * 2, vm((8, 2, HALF)),
            pltpu.SemaphoreType.DMA((14,)), pltpu.SemaphoreType.DMA((16,)), pltpu.SemaphoreType.DMA((16,)),
        ],
        compiler_params=pltpu.CompilerParams(collective_id=0, has_side_effects=True, vmem_limit_bytes=LIMIT),
        name="middle",
    )(
        child_parent, child_octant.reshape(1, KIDS), child, partner_src.T, partner_off.T, partner_count.reshape(1, 128),
        table, up_left, up_right, phases, down_right, down_left,
    )
    return out.reshape(KIDS, 2, 8, 128)


def solution(mesh):
    return jax.shard_map(
        on_device,
        mesh=mesh,
        in_specs=(P("clus", None, "dir", None), P(None, None, "dir"), P("clus", None), P("clus"), P(), P(), P()),
        out_specs=P("clus", None, "dir", None),
        check_vma=False,
    )
```

```python
import functools
import math

import jax
import jax.numpy as jnp
import ml_dtypes
import numpy as np
from jax import lax
from jax.experimental import pallas as pl
from jax.experimental.pallas import tpu as pltpu
from jax.sharding import PartitionSpec as P

NT_C, NP_C, NT_P, NP_P = 128, 256, 192, 384
OFFSETS = 316
N_CLUS, N_DIR = 16, 32
PAR, KIDS = 8, 48
TILES = PAR * 6
MESH = pl.DeviceIdType.MESH
EVEN = np.array([-2, 0, 2, 4, 6, 8, 10, 14])
ODD = np.array([-1, 1, 3, 5, 7, 9, 11, 13])


def lagrange(t):
    out = []
    for m in range(5):
        w = np.ones_like(t)
        for n in range(5):
            if n != m:
                w = w * (t - n) / (m - n)
        out.append(w)
    return out


def polar_matrix():
    x = (np.arange(NT_P) + 0.5) * NT_C / NT_P - 0.5
    s = np.clip(np.floor(x + 0.5).astype(int) - 2, 0, NT_C - 5)
    w = lagrange(x - s)
    m = np.zeros((NT_P, NT_C))
    for k in range(5):
        m[np.arange(NT_P), s + k] = w[k]
    return m


SCALE = 243


def azimuth_rows(rows):
    x = rows * NP_C / NP_P
    b = np.floor(x + 0.5).astype(int)
    w = lagrange(x - b + 2)
    m = np.zeros((len(rows), 8))
    for k in range(5):
        for j in range(len(rows)):
            i = b[j] + k - 2
            if 0 <= i < 8:
                m[j, i] = w[k][j] * SCALE
    return np.round(m)


def halves(a):
    a = a.astype(np.float32)
    hi = a.astype(ml_dtypes.bfloat16)
    lo = (a - hi.astype(np.float32)).astype(ml_dtypes.bfloat16)
    return np.stack([hi, lo])


def in_tiles(even, odd):
    return np.stack([even[:, :128], np.concatenate([even[:, 128:], odd[:, :64]], 1), odd[:, 64:]])


@functools.cache
def constants():
    p = polar_matrix()
    ae, ao = azimuth_rows(EVEN), azimuth_rows(ODD)
    eye = np.eye(16)
    up_left = np.concatenate([np.kron(eye, ae), np.kron(eye, ao)], 0).astype(ml_dtypes.bfloat16)
    w = np.zeros((256, 384))
    w[:128, :192] = p.T
    w[128:, 192:] = p.T
    w = w / SCALE
    up_right = halves(w)
    down_right = halves(np.stack([w[:128, :256].T, w[128:, 128:].T]))
    down_left = np.concatenate([np.kron(eye, ae.T), np.kron(eye, ao.T)], 1).astype(ml_dtypes.bfloat16)
    theta = math.pi * (np.arange(NT_P) + 0.5) / NT_P
    phases = np.zeros((N_DIR, 3, 2, 3, 8, 128))
    for d in range(N_DIR):
        angle = []
        for rows in (EVEN, ODD):
            phi = 2 * math.pi * ((12 * d + rows) % NP_P) / NP_P
            angle.append(
                8 * math.pi
                * np.stack(
                    [
                        np.sin(theta) * np.cos(phi)[:, None],
                        np.sin(theta) * np.sin(phi)[:, None],
                        np.cos(theta) * np.ones((8, 1)),
                    ]
                )
            )
        for k in range(3):
            t = in_tiles(angle[0][k], angle[1][k])
            phases[d, k] = np.stack([np.cos(t), np.sin(t)])
    return up_left, up_right, down_right, down_left, phases.reshape(N_DIR, 144, 128).astype(np.float32)


def split(x):
    hi = x.astype(jnp.bfloat16)
    return hi, (x - hi.astype(jnp.float32)).astype(jnp.bfloat16)


def dot3(a, b):
    f = functools.partial(jnp.dot, preferred_element_type=jnp.float32)
    return f(a[0], b[0]) + (f(a[1], b[0]) + f(a[0], b[1]))


def dot2(a, b):
    f = functools.partial(jnp.dot, preferred_element_type=jnp.float32)
    return f(a, b[0]) + f(a, b[1])


def position():
    clus, direction = lax.axis_index("clus"), lax.axis_index("dir")
    core = lax.rem(direction, 2)
    x, z = lax.rem(clus, 4), lax.div(clus, 4)
    return clus, direction, core, x, z


def gather_member(core, x, z, k):
    return (1 - core) * (z * 4 + k) + core * (k * 4 + x)


def reduce_member(core, x, z, k):
    return (1 - core) * (k * 4 + x) + core * (z * 4 + k)


def octant_tables(base, table, edge):
    def tile(k, a, c):
        r = (k * 6 + a * 3 + c) * 8
        return base[r : r + 8, :]

    for c in range(3):
        ar, ai, br, bi, cr, ci = (tile(k, a, c) for k in range(3) for a in range(2))
        rr, ii, ri, ir = ar * br, ai * bi, ar * bi, ai * br
        for sx, sy, re, im in ((1, 1, rr - ii, ri + ir), (1, -1, rr + ii, ir - ri)):
            pr, pi, qr, qi = re * cr, im * ci, re * ci, im * cr
            for sz, fr, fi in ((1, pr - pi, qr + qi), (-1, pr + pi, qi - qr)):
                for sign in (1, -1):
                    o = (sx * sign < 0) + 2 * (sy * sign < 0) + 4 * (sz * sign < 0)
                    for t, f in ((c, fr), (3 + c, fi if sign > 0 else -fi)):
                        table[o * 6 + t] = f
                        edge[0, t, o : o + 1, :] = f[0:1]
                        edge[1, t, o : o + 1, :] = f[7:8]


def aligned(i, n=8):
    return pl.multiple_of(i, n)


def build_kids(parent_ref, kids_ref):
    parent = lax.broadcasted_iota(jnp.int32, (8, KIDS), 0)
    start = jnp.sum((parent_ref[...] < parent).astype(jnp.int32), axis=1, keepdims=True)
    number = jnp.sum((parent_ref[...] == parent).astype(jnp.int32), axis=1, keepdims=True)
    lane = lax.broadcasted_iota(jnp.int32, (8, 128), 1)
    own = jnp.where(lane < number, start + lane, KIDS)
    kids_ref[...] = jnp.where(lane < 8, own, jnp.minimum(start + lane - 8, KIDS - 1))


def build_index(src_ref, off_ref, count_ref, key_ref):
    clus, direction, core, x, z = position()
    src = src_ref[...]
    off = off_ref[...]
    slot = lax.broadcasted_iota(jnp.int32, src.shape, 0)
    own_x, own_z = (src >> 3) & 3, src >> 5
    here = jnp.where(core == 0, own_z, own_x) == jnp.where(core == 0, z, x)
    local = jnp.where(core == 0, own_x, own_z) * 8 + (src & 7)
    local = jnp.where(here & (slot < count_ref[...]), local, -1)
    which = lax.broadcasted_iota(jnp.int32, (32, 128), 0)
    key = jnp.full((32, 128), OFFSETS, jnp.int32)
    for p in range(src.shape[0]):
        key = jnp.where(which == local[p : p + 1], off[p : p + 1], key)
    key_ref[...] = key


def one_hot(row, n):
    square = (KIDS, KIDS)
    diagonal = lax.broadcasted_iota(jnp.int32, square, 0) == lax.broadcasted_iota(jnp.int32, square, 1)
    column = jnp.sum(jnp.where(diagonal, row, 0), axis=1, keepdims=True)
    hot = column == lax.broadcasted_iota(jnp.int32, (KIDS, n), 1)
    return jnp.where(hot, 1.0, 0.0).astype(jnp.bfloat16)


def pick(hot, tiles):
    return dot2(hot, split(jnp.concatenate(tiles, axis=1)))


def even_lanes():
    column = lax.rem(lax.broadcasted_iota(jnp.int32, (TILES, 128), 0), 3)
    lane = lax.broadcasted_iota(jnp.int32, (TILES, 128), 1)
    return (column == 0) | ((column == 1) & (lane < 64))


PAIRS = ((2, 3, 4), (0, 1, 5))
PIECES = (((768, 0, 1152),), ((0, 0, 768), (1920, 768, 384)))
HALF = 1152


def relay(tile_ref, s_ref, part, first):
    def parent(g, carry):
        for n, q in enumerate(PAIRS[part]):
            for c in range(3):
                lanes = slice(128 * (3 * n + c), 128 * (3 * n + c) + 128)
                s_ref[first + g, :, lanes] = tile_ref[pl.ds((g * 6 + c) * 8 + q + 1, 2, stride=24), :]
        return carry

    lax.fori_loop(0, PAR, parent, 0)


def unrelay(sum_ref, tile_ref, part):
    def parent(g, carry):
        for n, q in enumerate(PAIRS[part]):
            for c in range(3):
                lanes = slice(128 * (3 * n + c), 128 * (3 * n + c) + 128)
                tile_ref[pl.ds((g * 6 + c) * 8 + q + 1, 2, stride=24), :] = sum_ref[g, :, lanes]
        return carry

    lax.fori_loop(0, PAR, parent, 0)


def swap(s_ref, x_ref, block):
    def source(i, carry):
        at = block * 8 + i
        x_ref[at, 0:1, :] = s_ref[at, 1:2, :]
        x_ref[at, 1:2, :] = s_ref[at, 0:1, :]
        return carry

    lax.fori_loop(0, PAR, source, 0, unroll=2)


GROUP = 4


def add_pairs(part, key_ref, table_ref, s_ref, x_ref, block, first_target, acc):
    acc = [list(a) for a in acc]
    pieces = PIECES[part]
    for u in range(PAR):
        source = block * 8 + u
        for p, (at, to, n) in enumerate(pieces):
            s = s_ref[source, :, to : to + n]
            x = x_ref[source, :, to : to + n]
            for j in range(GROUP):
                t = table_ref[key_ref[source, first_target + j], :, at : at + n].astype(jnp.float32)
                acc[j][p] = acc[j][p] + t * s
                acc[j][len(pieces) + p] = acc[j][len(pieces) + p] + t * x
    return tuple(tuple(a) for a in acc)


def middle_kernel(
    parent_hbm, octant_hbm, child_hbm, src_hbm, off_hbm, count_hbm, table_hbm, left_hbm, right_hbm, phases_hbm,
    right2_hbm, left2_hbm,
    out_ref,
    parent_ref, octants_ref, parents_ref, octant_ref, child_ref, src_ref, off_ref, count_ref, table_ref, left_ref,
    right_ref, base_ref, right2_ref, left2_ref, edge_ref,
    key_ref, index_ref, kids_ref, kid_ref, y_ref, z_ref, phase_ref, tile_ref, inc_ref, r_ref, pack_ref, halo_ref,
    sa_ref, sb_ref, xa_ref, xb_ref, acca_ref, accb_ref, pa_ref, pb_ref, gota_ref, gotb_ref, sum_ref,
    local_sem, send_sem, recv_sem,
):
    clus, direction, core, x, z = position()
    after = (clus, lax.rem(direction + 1, N_DIR))
    before = (clus, lax.rem(direction + N_DIR - 1, N_DIR))
    source_me = (1 - core) * x + core * z
    target_me = (1 - core) * z + core * x
    source_blocks, target_blocks = (
        [me, 3 - me, lax.rem(me + 2, 4), me + 1 - 2 * lax.rem(me, 2)] for me in (source_me, target_me)
    )
    source_peers = [(gather_member(core, x, z, k), direction) for k in source_blocks[1:]]
    target_peers = [(reduce_member(core, x, z, k), direction) for k in target_blocks[1:]]
    barrier = pltpu.get_barrier_semaphore()
    peers = [after, before, *source_peers, *target_peers]
    for peer in peers:
        pl.semaphore_signal(barrier, inc=1, device_id=peer, device_id_type=MESH)

    def fetch(n, src, dst):
        copy = pltpu.make_async_copy(src, dst, local_sem.at[n])
        copy.start()
        return copy

    parents = fetch(0, parent_hbm, parent_ref)
    first = [
        fetch(1, left_hbm, left_ref),
        fetch(2, child_hbm, child_ref),
        fetch(3, right_hbm, right_ref),
        fetch(4, phases_hbm.at[direction], base_ref),
        fetch(5, src_hbm, src_ref),
        fetch(6, off_hbm, off_ref),
        fetch(7, count_hbm, count_ref),
    ]
    second = [
        fetch(8, octant_hbm, octant_ref),
        fetch(9, parent_hbm, parents_ref),
        fetch(10, octant_hbm, octants_ref),
    ]
    z_ref[2 * KIDS : 2 * KIDS + 2] = jnp.zeros((2, 8, 384), jnp.float32)
    table_ref[OFFSETS] = jnp.zeros((2, 2304), jnp.bfloat16)
    parents.wait()
    build_kids(parent_ref, kids_ref)
    kids = fetch(0, kids_ref, kid_ref)
    for copy in first:
        copy.wait()
    third = [
        fetch(11, table_hbm, table_ref.at[pl.ds(0, OFFSETS)]),
        fetch(12, right2_hbm, right2_ref),
        fetch(13, left2_hbm, left2_ref),
    ]
    build_index(src_ref, off_ref, count_ref, key_ref)
    for n in range(6):
        xs = split(child_ref[8 * n : 8 * n + 8].reshape(128, 128))
        eo = dot2(left_ref[...], xs)
        y = split(jnp.concatenate([eo[:128], eo[128:]], axis=1))
        for h in range(2):
            y_ref[h, 128 * n : 128 * n + 128, :] = y[h]
    z_ref[0 : 2 * KIDS] = dot3((y_ref[0], y_ref[1]), (right_ref[0], right_ref[1])).reshape(2 * KIDS, 8, 384)
    octant_tables(base_ref, phase_ref, edge_ref)
    index = fetch(1, key_ref, index_ref)
    kids.wait()
    for copy in second:
        copy.wait()

    def parent(g, carry):
        acc = [jnp.zeros((8, 128), jnp.float32) for _ in range(6)]
        for m in range(8):
            k = kid_ref[g, m]
            o = octant_ref[0, kid_ref[g, 8 + m]]
            for c in range(3):
                re = z_ref[k * 2, :, 128 * c : 128 * c + 128]
                im = z_ref[k * 2 + 1, :, 128 * c : 128 * c + 128]
                fr = phase_ref[o * 6 + c]
                fi = phase_ref[o * 6 + 3 + c]
                acc[c] = acc[c] + (re * fr - im * fi)
                acc[3 + c] = acc[3 + c] + (re * fi + im * fr)
        for t in range(6):
            tile_ref[pl.ds(aligned((g * 6 + t) * 8), 8), :] = acc[t]
        return carry

    lax.fori_loop(0, PAR, parent, 0)

    pl.semaphore_wait(barrier, len(peers))

    def send(n, src, dst, peer):
        copy = pltpu.make_async_remote_copy(
            src, dst, send_sem.at[n], recv_sem.at[n], device_id=peer, device_id_type=MESH
        )
        copy.start()
        return copy

    pack_ref[0] = tile_ref[pl.ds(7, TILES, stride=8), :]
    forward = send(0, pack_ref.at[0], halo_ref.at[0], after)
    pack_ref[1] = tile_ref[pl.ds(0, TILES, stride=8), :]
    backward = send(1, pack_ref.at[1], halo_ref.at[1], before)
    own = source_me * 8
    relay(tile_ref, sa_ref, 0, own)
    block_a = sa_ref.at[pl.ds(own, 8)]
    gather_a = [send(2 + r, block_a, block_a, peer) for r, peer in enumerate(source_peers)]
    swap(sa_ref, xa_ref, source_me)
    for copy in (index, *third):
        copy.wait()

    parts = ((sa_ref, xa_ref, acca_ref, pa_ref), (sb_ref, xb_ref, accb_ref, pb_ref))

    def own_pass(part):
        s_ref, x_ref, acc_ref, _ = parts[part]
        k = len(PIECES[part])

        def group(i, carry):
            j, g = lax.div(i, 2), lax.rem(i, 2) * GROUP
            zero = tuple(jnp.zeros((2, n), jnp.float32) for _ in range(2) for _, _, n in PIECES[part])
            acc = add_pairs(
                part, index_ref, table_ref, s_ref, x_ref, source_me, reduce_member(core, x, z, j) * 8 + g, (zero,) * GROUP
            )
            for t in range(GROUP):
                for p, (_, to, n) in enumerate(PIECES[part]):
                    acc_ref[j * 8 + g + t, 0, :, to : to + n] = acc[t][p]
                    acc_ref[j * 8 + g + t, 1, :, to : to + n] = acc[t][k + p]
            return carry

        lax.fori_loop(0, 32 // GROUP, group, 0)

    def load(part, target):
        acc_ref = parts[part][2]
        return tuple(
            tuple(acc_ref[target + t, h, :, to : to + n] for h in range(2) for _, to, n in PIECES[part])
            for t in range(GROUP)
        )

    def block_pass(part, block):
        s_ref, x_ref, acc_ref, _ = parts[part]
        k = len(PIECES[part])

        def group(i, carry):
            j, g = lax.div(i, 2), lax.rem(i, 2) * GROUP
            acc = add_pairs(
                part, index_ref, table_ref, s_ref, x_ref, block, reduce_member(core, x, z, j) * 8 + g, load(part, j * 8 + g)
            )
            for t in range(GROUP):
                for p, (_, to, n) in enumerate(PIECES[part]):
                    acc_ref[j * 8 + g + t, 0, :, to : to + n] = acc[t][p]
                    acc_ref[j * 8 + g + t, 1, :, to : to + n] = acc[t][k + p]
            return carry

        lax.fori_loop(0, 32 // GROUP, group, 0)

    def last_pass(part, j, blocks):
        s_ref, x_ref, _, p_ref = parts[part]
        k = len(PIECES[part])

        def group(i, carry):
            g = i * GROUP
            acc = load(part, j * 8 + g)
            for block in blocks:
                acc = add_pairs(
                    part, index_ref, table_ref, s_ref, x_ref, block, reduce_member(core, x, z, j) * 8 + g, acc
                )
            for t in range(GROUP):
                for p, (_, to, n) in enumerate(PIECES[part]):
                    a, b = acc[t][p], acc[t][k + p]
                    p_ref[j * 8 + g + t, 0:1, to : to + n] = a[0:1] - a[1:2]
                    p_ref[j * 8 + g + t, 1:2, to : to + n] = b[0:1] + b[1:2]
            return carry

        lax.fori_loop(0, PAR // GROUP, group, 0)

    own_pass(0)

    even = even_lanes()
    forward.wait_recv()
    got = halo_ref[0]
    at1, at2, at6 = (pl.ds(s, TILES, stride=8) for s in (1, 2, 6))
    tile_ref[at1, :] = tile_ref[at1, :] + jnp.where(even, 0.0, got)
    tile_ref[at2, :] = tile_ref[at2, :] + jnp.where(even, got, 0.0)
    backward.wait_recv()
    tile_ref[at6, :] = tile_ref[at6, :] + halo_ref[1]
    relay(tile_ref, sb_ref, 1, own)
    block_b = sb_ref.at[pl.ds(own, 8)]
    gather_b = [send(5 + r, block_b, block_b, peer) for r, peer in enumerate(source_peers)]
    swap(sb_ref, xb_ref, source_me)
    own_pass(1)

    def gathered(part, copy, r):
        copy.wait_recv()
        swap(parts[part][0], parts[part][1], source_blocks[r])

    def reduce_to(part, r, got_ref):
        block = parts[part][3].at[pl.ds(target_blocks[r] * 8, 8)]
        return send(8 + 3 * part + r - 1, block, got_ref.at[r - 1], target_peers[r - 1])

    for r in (3, 2, 1):
        gathered(0, gather_a[r - 1], r)
    for r in (1, 2):
        last_pass(0, target_blocks[r], source_blocks[1:])
    for r in (3, 2):
        gathered(1, gather_b[r - 1], r)
        block_pass(1, source_blocks[r])
    gathered(1, gather_b[0], 1)
    reduces_b = []
    for r in (1, 2, 3):
        last_pass(1, target_blocks[r], source_blocks[1:2])
        reduces_b.append(reduce_to(1, r, gotb_ref))
    reduces = [reduce_to(0, r, gota_ref) for r in (1, 2)]
    last_pass(0, target_blocks[3], source_blocks[1:])
    reduces += [reduce_to(0, 3, gota_ref), *reduces_b]
    last_pass(1, target_blocks[0], source_blocks[1:2])
    last_pass(0, target_blocks[0], source_blocks[1:])

    def total(part, got_ref):
        p_ref = parts[part][3]
        for copy in reduces[3 * part : 3 * part + 3]:
            copy.wait_recv()

        def parent(g, carry):
            sum_ref[g] = (p_ref[target_me * 8 + g] + got_ref[0, g]) + (got_ref[1, g] + got_ref[2, g])
            return carry

        lax.fori_loop(0, PAR, parent, 0)
        unrelay(sum_ref, tile_ref, part)

    total(1, gotb_ref)
    pack_ref[2] = jnp.where(even, tile_ref[at2, :], tile_ref[at1, :])
    last_back = send(14, pack_ref.at[2], halo_ref.at[2], before)
    pack_ref[3] = tile_ref[at6, :]
    last_on = send(15, pack_ref.at[3], halo_ref.at[3], after)
    total(0, gota_ref)
    pair = lax.broadcasted_iota(jnp.int32, (8, 128), 0)
    inside = (pair > 0) & (pair < 7)
    for t in range(TILES):
        inc_ref[t] = jnp.where(inside, tile_ref[8 * t : 8 * t + 8, :], 0.0)

    def child(k, carry):
        g, o = parents_ref[0, k], octant_ref[0, k]
        for c in range(3):
            re, im = inc_ref[g * 6 + c], inc_ref[g * 6 + 3 + c]
            fr, fi = phase_ref[o * 6 + c], phase_ref[o * 6 + 3 + c]
            r_ref[k * 2, :, 128 * c : 128 * c + 128] = re * fr + im * fi
            r_ref[k * 2 + 1, :, 128 * c : 128 * c + 128] = im * fr - re * fi
        return carry

    lax.fori_loop(0, KIDS, child, 0, unroll=4)

    def to_child(r):
        hi, lo = split(r)
        return (
            dot3((hi[:, :256], lo[:, :256]), (right2_ref[0, 0], right2_ref[1, 0])),
            dot3((hi[:, 128:], lo[:, 128:]), (right2_ref[0, 1], right2_ref[1, 1])),
        )

    for n in range(6):
        v = split(jnp.concatenate(to_child(r_ref[16 * n : 16 * n + 16].reshape(128, 384)), axis=0))
        out_ref[128 * n : 128 * n + 128, :] = dot2(left2_ref[...], v)
    hot_parent, hot_octant = one_hot(parent_ref[...], 8), one_hot(octants_ref[...], 8)
    shifts = [pick(hot_octant, [edge_ref[e, t] for t in range(6)]) for e in range(2)]
    for copy in (forward, backward, *gather_a, *gather_b, *reduces):
        copy.wait_send()
    last_back.wait()
    last_on.wait()
    rows = []
    for e in range(2):
        values = pick(hot_parent, [halo_ref[3 - e, pl.ds(t, 8, stride=6), :] for t in range(6)])
        re, im, fr, fi = values[:, :384], values[:, 384:], shifts[e][:, :384], shifts[e][:, 384:]
        rows += [re * fr + im * fi, im * fr - re * fi]
    even_part, odd_part = to_child(jnp.concatenate(rows, axis=0))
    weight_even, weight_odd = azimuth_rows(EVEN), azimuth_rows(ODD)
    for e, s in enumerate((0, 7)):
        for a in range(2):
            at = (2 * e + a) * KIDS
            for i in range(8):
                we, wo = float(weight_even[s, i]), float(weight_odd[s, i])
                if we or wo:
                    place = pl.ds(a * 8 + i, KIDS, stride=16)
                    out_ref[place, :] = out_ref[place, :] + (
                        we * even_part[at : at + KIDS] + wo * odd_part[at : at + KIDS]
                    )


def finish_kernel(in_ref, out_ref, sem):
    copies = [
        pltpu.make_async_copy(in_ref.at[pl.ds(96 * n, 96)], out_ref.at[pl.ds(96 * n, 96)], sem.at[n]) for n in range(8)
    ]
    for copy in copies:
        copy.start()
    for copy in copies:
        copy.wait()


VMEM_SPEC = pl.BlockSpec(memory_space=pltpu.VMEM)
HBM_SPEC = pl.BlockSpec(memory_space=pltpu.HBM)
LIMIT = 63 * 2**20


def f32(*shape):
    return jax.ShapeDtypeStruct(shape, jnp.float32)


def on_device(child, table, child_parent, child_octant, partner_src, partner_off, partner_count):
    up_left, up_right, down_right, down_left, phases = (jnp.asarray(a) for a in constants())
    vm = functools.partial(pltpu.VMEM, dtype=jnp.float32)
    ints = functools.partial(pltpu.VMEM, dtype=jnp.int32)
    bf16 = functools.partial(pltpu.VMEM, dtype=jnp.bfloat16)
    scalars = functools.partial(pltpu.SMEM, dtype=jnp.int32)
    out = pl.pallas_call(
        middle_kernel,
        out_shape=f32(KIDS * 16, 128),
        in_specs=[HBM_SPEC] * 12,
        out_specs=VMEM_SPEC,
        scratch_shapes=[
            ints((1, KIDS)), ints((1, KIDS)), scalars((1, KIDS)), scalars((1, KIDS)), vm((KIDS, 2, 8, 128)),
            ints((56, 128)), ints((56, 128)), ints((1, 128)), bf16((OFFSETS + 1, 2, 2304)), bf16((256, 128)),
            bf16((2, 256, 384)), vm((144, 128)), bf16((2, 2, 256, 128)), bf16((128, 256)), vm((2, 6, 8, 128)),
            ints((32, 128)), scalars((32, 128)), ints((8, 128)), scalars((8, 128)),
            bf16((2, 768, 256)), vm((2 * KIDS + 2, 8, 384)), vm((48, 8, 128)), vm((8 * TILES, 128)), vm((TILES, 8, 128)),
            vm((2 * KIDS, 8, 384)), vm((4, TILES, 128)), vm((4, TILES, 128)),
            *[vm((32, 2, HALF))] * 4, *[vm((32, 2, 2, HALF))] * 2, *[vm((32, 2, HALF))] * 2,
            *[vm((3, 8, 2, HALF))] * 2, vm((8, 2, HALF)),
            pltpu.SemaphoreType.DMA((14,)), pltpu.SemaphoreType.DMA((16,)), pltpu.SemaphoreType.DMA((16,)),
        ],
        compiler_params=pltpu.CompilerParams(collective_id=0, has_side_effects=True, vmem_limit_bytes=LIMIT),
        name="middle",
    )(
        child_parent, child_octant.reshape(1, KIDS), child, partner_src.T, partner_off.T, partner_count.reshape(1, 128),
        table, up_left, up_right, phases, down_right, down_left,
    )
    out = pl.pallas_call(
        finish_kernel,
        out_shape=f32(KIDS * 16, 128),
        in_specs=[HBM_SPEC],
        out_specs=HBM_SPEC,
        scratch_shapes=[pltpu.SemaphoreType.DMA((8,))],
        compiler_params=pltpu.CompilerParams(vmem_limit_bytes=LIMIT),
        name="finish",
    )(out)
    return out.reshape(KIDS, 2, 8, 128)


def solution(mesh):
    return jax.shard_map(
        on_device,
        mesh=mesh,
        in_specs=(P("clus", None, "dir", None), P(None, None, "dir"), P("clus", None), P("clus"), P(), P(), P()),
        out_specs=P("clus", None, "dir", None),
        check_vma=False,
    )
```

```python
import functools
import math

import jax
import jax.numpy as jnp
import ml_dtypes
import numpy as np
from jax import lax
from jax.experimental import pallas as pl
from jax.experimental.pallas import tpu as pltpu
from jax.sharding import PartitionSpec as P

NT_C, NP_C, NT_P, NP_P = 128, 256, 192, 384
OFFSETS = 316
N_CLUS, N_DIR = 16, 32
PAR, KIDS = 8, 48
TILES = PAR * 6
MESH = pl.DeviceIdType.MESH
EVEN = np.array([-2, 0, 2, 4, 6, 8, 10, 14])
ODD = np.array([-1, 1, 3, 5, 7, 9, 11, 13])


def lagrange(t):
    out = []
    for m in range(5):
        w = np.ones_like(t)
        for n in range(5):
            if n != m:
                w = w * (t - n) / (m - n)
        out.append(w)
    return out


def polar_matrix():
    x = (np.arange(NT_P) + 0.5) * NT_C / NT_P - 0.5
    s = np.clip(np.floor(x + 0.5).astype(int) - 2, 0, NT_C - 5)
    w = lagrange(x - s)
    m = np.zeros((NT_P, NT_C))
    for k in range(5):
        m[np.arange(NT_P), s + k] = w[k]
    return m


SCALE = 243


def azimuth_rows(rows):
    x = rows * NP_C / NP_P
    b = np.floor(x + 0.5).astype(int)
    w = lagrange(x - b + 2)
    m = np.zeros((len(rows), 8))
    for k in range(5):
        for j in range(len(rows)):
            i = b[j] + k - 2
            if 0 <= i < 8:
                m[j, i] = w[k][j] * SCALE
    return np.round(m)


def halves(a):
    a = a.astype(np.float32)
    hi = a.astype(ml_dtypes.bfloat16)
    lo = (a - hi.astype(np.float32)).astype(ml_dtypes.bfloat16)
    return np.stack([hi, lo])


def in_tiles(even, odd):
    return np.stack([even[:, :128], np.concatenate([even[:, 128:], odd[:, :64]], 1), odd[:, 64:]])


@functools.cache
def constants():
    p = polar_matrix()
    ae, ao = azimuth_rows(EVEN), azimuth_rows(ODD)
    eye = np.eye(16)
    up_left = np.concatenate([np.kron(eye, ae), np.kron(eye, ao)], 0).astype(ml_dtypes.bfloat16)
    w = np.zeros((256, 384))
    w[:128, :192] = p.T
    w[128:, 192:] = p.T
    w = w / SCALE
    up_right = halves(w)
    down_right = halves(np.stack([w[:128, :256].T, w[128:, 128:].T]))
    down_left = np.concatenate([np.kron(eye, ae.T), np.kron(eye, ao.T)], 1).astype(ml_dtypes.bfloat16)
    theta = math.pi * (np.arange(NT_P) + 0.5) / NT_P
    phases = np.zeros((N_DIR, 3, 2, 3, 8, 128))
    for d in range(N_DIR):
        angle = []
        for rows in (EVEN, ODD):
            phi = 2 * math.pi * ((12 * d + rows) % NP_P) / NP_P
            angle.append(
                8 * math.pi
                * np.stack(
                    [
                        np.sin(theta) * np.cos(phi)[:, None],
                        np.sin(theta) * np.sin(phi)[:, None],
                        np.cos(theta) * np.ones((8, 1)),
                    ]
                )
            )
        for k in range(3):
            t = in_tiles(angle[0][k], angle[1][k])
            phases[d, k] = np.stack([np.cos(t), np.sin(t)])
    return up_left, up_right, down_right, down_left, phases.reshape(N_DIR, 144, 128).astype(np.float32)


def split(x):
    hi = x.astype(jnp.bfloat16)
    return hi, (x - hi.astype(jnp.float32)).astype(jnp.bfloat16)


def dot3(a, b):
    f = functools.partial(jnp.dot, preferred_element_type=jnp.float32)
    return f(a[0], b[0]) + (f(a[1], b[0]) + f(a[0], b[1]))


def dot2(a, b):
    f = functools.partial(jnp.dot, preferred_element_type=jnp.float32)
    return f(a, b[0]) + f(a, b[1])


def position():
    clus, direction = lax.axis_index("clus"), lax.axis_index("dir")
    core = lax.rem(direction, 2)
    x, z = lax.rem(clus, 4), lax.div(clus, 4)
    return clus, direction, core, x, z


def gather_member(core, x, z, k):
    return (1 - core) * (z * 4 + k) + core * (k * 4 + x)


def reduce_member(core, x, z, k):
    return (1 - core) * (k * 4 + x) + core * (z * 4 + k)


def octant_tables(base, table, edge):
    def tile(k, a, c):
        r = (k * 6 + a * 3 + c) * 8
        return base[r : r + 8, :]

    for c in range(3):
        ar, ai, br, bi, cr, ci = (tile(k, a, c) for k in range(3) for a in range(2))
        rr, ii, ri, ir = ar * br, ai * bi, ar * bi, ai * br
        for sx, sy, re, im in ((1, 1, rr - ii, ri + ir), (1, -1, rr + ii, ir - ri)):
            pr, pi, qr, qi = re * cr, im * ci, re * ci, im * cr
            for sz, fr, fi in ((1, pr - pi, qr + qi), (-1, pr + pi, qi - qr)):
                for sign in (1, -1):
                    o = (sx * sign < 0) + 2 * (sy * sign < 0) + 4 * (sz * sign < 0)
                    for t, f in ((c, fr), (3 + c, fi if sign > 0 else -fi)):
                        table[o * 6 + t] = f
                        edge[0, t, o : o + 1, :] = f[0:1]
                        edge[1, t, o : o + 1, :] = f[7:8]


def aligned(i, n=8):
    return pl.multiple_of(i, n)


def build_kids(parent_ref, kids_ref):
    parent = lax.broadcasted_iota(jnp.int32, (8, KIDS), 0)
    start = jnp.sum((parent_ref[...] < parent).astype(jnp.int32), axis=1, keepdims=True)
    number = jnp.sum((parent_ref[...] == parent).astype(jnp.int32), axis=1, keepdims=True)
    lane = lax.broadcasted_iota(jnp.int32, (8, 128), 1)
    own = jnp.where(lane < number, start + lane, KIDS)
    kids_ref[...] = jnp.where(lane < 8, own, jnp.minimum(start + lane - 8, KIDS - 1))


def build_index(src_ref, off_ref, count_ref, key_ref):
    clus, direction, core, x, z = position()
    src = src_ref[...]
    off = off_ref[...]
    slot = lax.broadcasted_iota(jnp.int32, src.shape, 0)
    own_x, own_z = (src >> 3) & 3, src >> 5
    here = jnp.where(core == 0, own_z, own_x) == jnp.where(core == 0, z, x)
    local = jnp.where(core == 0, own_x, own_z) * 8 + (src & 7)
    local = jnp.where(here & (slot < count_ref[...]), local, -1)
    which = lax.broadcasted_iota(jnp.int32, (32, 128), 0)
    key = jnp.full((32, 128), OFFSETS, jnp.int32)
    for p in range(src.shape[0]):
        key = jnp.where(which == local[p : p + 1], off[p : p + 1], key)
    key_ref[...] = key


def one_hot(row, n):
    square = (KIDS, KIDS)
    diagonal = lax.broadcasted_iota(jnp.int32, square, 0) == lax.broadcasted_iota(jnp.int32, square, 1)
    column = jnp.sum(jnp.where(diagonal, row, 0), axis=1, keepdims=True)
    hot = column == lax.broadcasted_iota(jnp.int32, (KIDS, n), 1)
    return jnp.where(hot, 1.0, 0.0).astype(jnp.bfloat16)


def pick(hot, tiles):
    return dot2(hot, split(jnp.concatenate(tiles, axis=1)))


def even_lanes():
    column = lax.rem(lax.broadcasted_iota(jnp.int32, (TILES, 128), 0), 3)
    lane = lax.broadcasted_iota(jnp.int32, (TILES, 128), 1)
    return (column == 0) | ((column == 1) & (lane < 64))


PAIRS = ((2, 3, 4), (0, 1, 5))
PIECES = (((768, 0, 1152),), ((0, 0, 768), (1920, 768, 384)))
HALF = 1152


def relay(tile_ref, s_ref, part, first):
    def parent(g, carry):
        for n, q in enumerate(PAIRS[part]):
            for c in range(3):
                lanes = slice(128 * (3 * n + c), 128 * (3 * n + c) + 128)
                s_ref[first + g, :, lanes] = tile_ref[pl.ds((g * 6 + c) * 8 + q + 1, 2, stride=24), :]
        return carry

    lax.fori_loop(0, PAR, parent, 0)


def unrelay(sum_ref, tile_ref, part):
    def parent(g, carry):
        for n, q in enumerate(PAIRS[part]):
            for c in range(3):
                lanes = slice(128 * (3 * n + c), 128 * (3 * n + c) + 128)
                tile_ref[pl.ds((g * 6 + c) * 8 + q + 1, 2, stride=24), :] = sum_ref[g, :, lanes]
        return carry

    lax.fori_loop(0, PAR, parent, 0)


def swap(s_ref, x_ref, block):
    def source(i, carry):
        at = block * 8 + i
        x_ref[at, 0:1, :] = s_ref[at, 1:2, :]
        x_ref[at, 1:2, :] = s_ref[at, 0:1, :]
        return carry

    lax.fori_loop(0, PAR, source, 0, unroll=2)


GROUP = 4


def add_pairs(part, key_ref, table_ref, s_ref, x_ref, block, first_target, acc):
    acc = [list(a) for a in acc]
    pieces = PIECES[part]
    for u in range(PAR):
        source = block * 8 + u
        for p, (at, to, n) in enumerate(pieces):
            s = s_ref[source, :, to : to + n]
            x = x_ref[source, :, to : to + n]
            for j in range(GROUP):
                t = table_ref[key_ref[source, first_target + j], :, at : at + n].astype(jnp.float32)
                acc[j][p] = acc[j][p] + t * s
                acc[j][len(pieces) + p] = acc[j][len(pieces) + p] + t * x
    return tuple(tuple(a) for a in acc)


def middle_kernel(
    parent_hbm, octant_hbm, child_hbm, src_hbm, off_hbm, count_hbm, table_hbm, left_hbm, right_hbm, phases_hbm,
    right2_hbm, left2_hbm,
    out_ref,
    parent_ref, octants_ref, parents_ref, octant_ref, child_ref, src_ref, off_ref, count_ref, table_ref, left_ref,
    right_ref, base_ref, right2_ref, left2_ref, edge_ref,
    key_ref, index_ref, kids_ref, kid_ref, y_ref, z_ref, phase_ref, tile_ref, inc_ref, r_ref, v_ref, pack_ref, halo_ref,
    sa_ref, sb_ref, xa_ref, xb_ref, acca_ref, accb_ref, pa_ref, pb_ref, gota_ref, pu_ref, gotu_ref, goto_ref, su_ref, sum_ref,
    local_sem, send_sem, recv_sem,
):
    clus, direction, core, x, z = position()
    after = (clus, lax.rem(direction + 1, N_DIR))
    before = (clus, lax.rem(direction + N_DIR - 1, N_DIR))
    source_me = (1 - core) * x + core * z
    target_me = (1 - core) * z + core * x
    source_blocks, target_blocks = (
        [me, 3 - me, lax.rem(me + 2, 4), me + 1 - 2 * lax.rem(me, 2)] for me in (source_me, target_me)
    )
    source_peers = [(gather_member(core, x, z, k), direction) for k in source_blocks[1:]]
    target_peers = [(reduce_member(core, x, z, k), direction) for k in target_blocks[1:]]
    barrier = pltpu.get_barrier_semaphore()
    peers = [after, before, *source_peers, *target_peers]
    for peer in peers:
        pl.semaphore_signal(barrier, inc=1, device_id=peer, device_id_type=MESH)

    def fetch(n, src, dst):
        copy = pltpu.make_async_copy(src, dst, local_sem.at[n])
        copy.start()
        return copy

    parents = fetch(0, parent_hbm, parent_ref)
    first = [
        fetch(1, left_hbm, left_ref),
        fetch(2, child_hbm, child_ref),
        fetch(3, right_hbm, right_ref),
        fetch(4, phases_hbm.at[direction], base_ref),
        fetch(5, src_hbm, src_ref),
        fetch(6, off_hbm, off_ref),
        fetch(7, count_hbm, count_ref),
    ]
    second = [
        fetch(8, octant_hbm, octant_ref),
        fetch(9, parent_hbm, parents_ref),
        fetch(10, octant_hbm, octants_ref),
    ]
    z_ref[2 * KIDS : 2 * KIDS + 2] = jnp.zeros((2, 8, 384), jnp.float32)
    table_ref[OFFSETS] = jnp.zeros((2, 2304), jnp.bfloat16)
    parents.wait()
    build_kids(parent_ref, kids_ref)
    kids = fetch(0, kids_ref, kid_ref)
    for copy in first:
        copy.wait()
    third = [
        fetch(11, table_hbm, table_ref.at[pl.ds(0, OFFSETS)]),
        fetch(12, right2_hbm, right2_ref),
        fetch(13, left2_hbm, left2_ref),
    ]
    build_index(src_ref, off_ref, count_ref, key_ref)
    for n in range(6):
        xs = split(child_ref[8 * n : 8 * n + 8].reshape(128, 128))
        eo = dot2(left_ref[...], xs)
        y = split(jnp.concatenate([eo[:128], eo[128:]], axis=1))
        for h in range(2):
            y_ref[h, 128 * n : 128 * n + 128, :] = y[h]
    z_ref[0 : 2 * KIDS] = dot3((y_ref[0], y_ref[1]), (right_ref[0], right_ref[1])).reshape(2 * KIDS, 8, 384)
    octant_tables(base_ref, phase_ref, edge_ref)
    index = fetch(1, key_ref, index_ref)
    kids.wait()
    for copy in second:
        copy.wait()

    def parent(g, carry):
        acc = [jnp.zeros((8, 128), jnp.float32) for _ in range(6)]
        for m in range(8):
            k = kid_ref[g, m]
            o = octant_ref[0, kid_ref[g, 8 + m]]
            for c in range(3):
                re = z_ref[k * 2, :, 128 * c : 128 * c + 128]
                im = z_ref[k * 2 + 1, :, 128 * c : 128 * c + 128]
                fr = phase_ref[o * 6 + c]
                fi = phase_ref[o * 6 + 3 + c]
                acc[c] = acc[c] + (re * fr - im * fi)
                acc[3 + c] = acc[3 + c] + (re * fi + im * fr)
        for t in range(6):
            tile_ref[pl.ds(aligned((g * 6 + t) * 8), 8), :] = acc[t]
        return carry

    lax.fori_loop(0, PAR, parent, 0)

    pl.semaphore_wait(barrier, len(peers))

    def send(n, src, dst, peer):
        copy = pltpu.make_async_remote_copy(
            src, dst, send_sem.at[n], recv_sem.at[n], device_id=peer, device_id_type=MESH
        )
        copy.start()
        return copy

    pack_ref[0] = tile_ref[pl.ds(7, TILES, stride=8), :]
    forward = send(0, pack_ref.at[0], halo_ref.at[0], after)
    pack_ref[1] = tile_ref[pl.ds(0, TILES, stride=8), :]
    backward = send(1, pack_ref.at[1], halo_ref.at[1], before)
    own = source_me * 8
    relay(tile_ref, sa_ref, 0, own)
    block_a = sa_ref.at[pl.ds(own, 8)]
    gather_a = [send(2 + r, block_a, block_a, peer) for r, peer in enumerate(source_peers)]
    swap(sa_ref, xa_ref, source_me)
    for copy in (index, *third):
        copy.wait()

    parts = ((sa_ref, xa_ref, acca_ref, pa_ref), (sb_ref, xb_ref, accb_ref, pb_ref))

    def own_pass(part):
        s_ref, x_ref, acc_ref, _ = parts[part]
        k = len(PIECES[part])

        def group(i, carry):
            j, g = lax.div(i, 2), lax.rem(i, 2) * GROUP
            zero = tuple(jnp.zeros((2, n), jnp.float32) for _ in range(2) for _, _, n in PIECES[part])
            acc = add_pairs(
                part, index_ref, table_ref, s_ref, x_ref, source_me, reduce_member(core, x, z, j) * 8 + g, (zero,) * GROUP
            )
            for t in range(GROUP):
                for p, (_, to, n) in enumerate(PIECES[part]):
                    acc_ref[j * 8 + g + t, 0, :, to : to + n] = acc[t][p]
                    acc_ref[j * 8 + g + t, 1, :, to : to + n] = acc[t][k + p]
            return carry

        lax.fori_loop(0, 32 // GROUP, group, 0)

    def load(part, target):
        acc_ref = parts[part][2]
        return tuple(
            tuple(acc_ref[target + t, h, :, to : to + n] for h in range(2) for _, to, n in PIECES[part])
            for t in range(GROUP)
        )

    def block_pass(part, block):
        s_ref, x_ref, acc_ref, _ = parts[part]
        k = len(PIECES[part])

        def group(i, carry):
            j, g = lax.div(i, 2), lax.rem(i, 2) * GROUP
            acc = add_pairs(
                part, index_ref, table_ref, s_ref, x_ref, block, reduce_member(core, x, z, j) * 8 + g, load(part, j * 8 + g)
            )
            for t in range(GROUP):
                for p, (_, to, n) in enumerate(PIECES[part]):
                    acc_ref[j * 8 + g + t, 0, :, to : to + n] = acc[t][p]
                    acc_ref[j * 8 + g + t, 1, :, to : to + n] = acc[t][k + p]
            return carry

        lax.fori_loop(0, 32 // GROUP, group, 0)

    def last_pass(part, j, blocks):
        s_ref, x_ref, _, p_ref = parts[part]
        k = len(PIECES[part])

        def group(i, carry):
            g = i * GROUP
            acc = load(part, j * 8 + g)
            for block in blocks:
                acc = add_pairs(
                    part, index_ref, table_ref, s_ref, x_ref, block, reduce_member(core, x, z, j) * 8 + g, acc
                )
            for t in range(GROUP):
                for p, (_, to, n) in enumerate(PIECES[part]):
                    a, b = acc[t][p], acc[t][k + p]
                    p_ref[j * 8 + g + t, 0:1, to : to + n] = a[0:1] - a[1:2]
                    p_ref[j * 8 + g + t, 1:2, to : to + n] = b[0:1] + b[1:2]
            return carry

        lax.fori_loop(0, PAR // GROUP, group, 0)

    own_pass(0)

    even = even_lanes()
    forward.wait_recv()
    got = halo_ref[0]
    at1, at2, at6 = (pl.ds(s, TILES, stride=8) for s in (1, 2, 6))
    tile_ref[at1, :] = tile_ref[at1, :] + jnp.where(even, 0.0, got)
    tile_ref[at2, :] = tile_ref[at2, :] + jnp.where(even, got, 0.0)
    backward.wait_recv()
    tile_ref[at6, :] = tile_ref[at6, :] + halo_ref[1]
    relay(tile_ref, sb_ref, 1, own)
    block_b = sb_ref.at[pl.ds(own, 8)]
    gather_b = [send(5 + r, block_b, block_b, peer) for r, peer in enumerate(source_peers)]
    swap(sb_ref, xb_ref, source_me)
    own_pass(1)

    def gathered(part, copy, r):
        copy.wait_recv()
        swap(parts[part][0], parts[part][1], source_blocks[r])

    def reduce_to(part, r, got_ref):
        block = parts[part][3].at[pl.ds(target_blocks[r] * 8, 8)]
        return send(8 + 3 * part + r - 1, block, got_ref.at[r - 1], target_peers[r - 1])

    for r in (3, 2, 1):
        gathered(0, gather_a[r - 1], r)
    for r in (1, 2):
        last_pass(0, target_blocks[r], source_blocks[1:])
    for r in (3, 2):
        gathered(1, gather_b[r - 1], r)
        block_pass(1, source_blocks[r])
    gathered(1, gather_b[0], 1)
    low = lax.broadcasted_iota(jnp.int32, (2, 128), 1) < 64
    for_before, for_after = 2 * core, 2 - 2 * core

    def pack(j):
        def parent(g, carry):
            t = j * 8 + g
            p = [pb_ref[t, :, 128 * n : 128 * n + 128] for n in range(9)]
            chunks = (
                (for_before, (p[3], jnp.where(low, p[4], p[1]), p[2])),
                (1, (p[0], jnp.where(low, p[1], p[4]), p[5])),
                (for_after, p[6:9]),
            )
            for chunk, tiles in chunks:
                for c in range(3):
                    pu_ref[chunk, t, :, 128 * c : 128 * c + 128] = tiles[c]
            return carry

        lax.fori_loop(0, PAR, parent, 0, unroll=2)

    urgent = []
    for r in (1, 2, 3):
        last_pass(1, target_blocks[r], source_blocks[1:2])
        pack(target_blocks[r])
        chunk = pu_ref.at[0, pl.ds(target_blocks[r] * 8, 8)]
        urgent.append(send(10 + r, chunk, gotu_ref.at[r - 1], target_peers[r - 1]))
    others = []
    for r in (1, 2, 3):
        chunks = pu_ref.at[pl.ds(1, 2), pl.ds(target_blocks[r] * 8, 8)]
        others.append(send(15 + r, chunks, goto_ref.at[r - 1], target_peers[r - 1]))
    reduces = [reduce_to(0, r, gota_ref) for r in (1, 2)]
    last_pass(0, target_blocks[3], source_blocks[1:])
    reduces.append(reduce_to(0, 3, gota_ref))
    last_pass(1, target_blocks[0], source_blocks[1:2])
    pack(target_blocks[0])
    last_pass(0, target_blocks[0], source_blocks[1:])

    def to_rows(chunk, slot):
        def parent(g, carry):
            for c in range(3):
                pack_ref[slot, pl.ds(g * 6 + c, 2, stride=3), :] = su_ref[chunk, g, :, 128 * c : 128 * c + 128]
            return carry

        lax.fori_loop(0, PAR, parent, 0, unroll=2)

    for copy in urgent:
        copy.wait_recv()

    def first_total(g, carry):
        su_ref[0, g] = (pu_ref[0, target_me * 8 + g] + gotu_ref[0, g]) + (gotu_ref[1, g] + gotu_ref[2, g])
        return carry

    lax.fori_loop(0, PAR, first_total, 0, unroll=2)
    to_rows(0, 2)
    far = (clus, lax.rem(direction + N_DIR - 1 + 2 * core, N_DIR))
    near = (clus, direction + 1 - 2 * core)
    last_far = send(14, pack_ref.at[2], halo_ref.at[2 + core], far)
    for copy in others:
        copy.wait_recv()

    def other_totals(g, carry):
        for n in range(2):
            own_sum = pu_ref[1 + n, target_me * 8 + g]
            su_ref[1 + n, g] = (own_sum + goto_ref[0, n, g]) + (goto_ref[1, n, g] + goto_ref[2, n, g])
        return carry

    lax.fori_loop(0, PAR, other_totals, 0, unroll=2)
    to_rows(2, 3)
    last_near = send(15, pack_ref.at[3], halo_ref.at[3 - core], near)

    def unpack(g, carry):
        f, rest, last = (
            [su_ref[chunk, g, :, 128 * c : 128 * c + 128] for c in range(3)] for chunk in (for_before, 1, for_after)
        )
        pairs = (
            (0, (rest[0], jnp.where(low, rest[1], f[1]), f[2])),
            (1, (f[0], jnp.where(low, f[1], rest[1]), rest[2])),
            (5, last),
        )
        for q, tiles in pairs:
            for c in range(3):
                tile_ref[pl.ds((g * 6 + c) * 8 + q + 1, 2, stride=24), :] = tiles[c]
        return carry

    lax.fori_loop(0, PAR, unpack, 0)
    for copy in reduces:
        copy.wait_recv()

    def last_total(g, carry):
        sum_ref[g] = (pa_ref[target_me * 8 + g] + gota_ref[0, g]) + (gota_ref[1, g] + gota_ref[2, g])
        return carry

    lax.fori_loop(0, PAR, last_total, 0, unroll=2)
    unrelay(sum_ref, tile_ref, 0)
    pair = lax.broadcasted_iota(jnp.int32, (8, 128), 0)
    inside = (pair > 0) & (pair < 7)
    for t in range(TILES):
        inc_ref[t] = jnp.where(inside, tile_ref[8 * t : 8 * t + 8, :], 0.0)

    def child(k, carry):
        g, o = parents_ref[0, k], octant_ref[0, k]
        for c in range(3):
            re, im = inc_ref[g * 6 + c], inc_ref[g * 6 + 3 + c]
            fr, fi = phase_ref[o * 6 + c], phase_ref[o * 6 + 3 + c]
            r_ref[k * 2, :, 128 * c : 128 * c + 128] = re * fr + im * fi
            r_ref[k * 2 + 1, :, 128 * c : 128 * c + 128] = im * fr - re * fi
        return carry

    lax.fori_loop(0, KIDS, child, 0, unroll=4)

    def to_child(r):
        hi, lo = split(r)
        return (
            dot3((hi[:, :256], lo[:, :256]), (right2_ref[0, 0], right2_ref[1, 0])),
            dot3((hi[:, 128:], lo[:, 128:]), (right2_ref[0, 1], right2_ref[1, 1])),
        )

    v_ref[0], v_ref[1] = to_child(r_ref[...].reshape(768, 384))
    for n in range(6):
        at = slice(128 * n, 128 * n + 128)
        out_ref[at, :] = dot2(left2_ref[...], split(jnp.concatenate([v_ref[0, at, :], v_ref[1, at, :]], axis=0)))
    hot_parent, hot_octant = one_hot(parent_ref[...], 8), one_hot(octants_ref[...], 8)
    shifts = [pick(hot_octant, [edge_ref[e, t] for t in range(6)]) for e in range(2)]
    for copy in (forward, backward, *gather_a, *gather_b, *reduces, *urgent, *others):
        copy.wait_send()
    last_near.wait()
    last_far.wait()
    rows = []
    for e in range(2):
        values = pick(hot_parent, [halo_ref[3 - e, pl.ds(t, 8, stride=6), :] for t in range(6)])
        re, im, fr, fi = values[:, :384], values[:, 384:], shifts[e][:, :384], shifts[e][:, 384:]
        rows += [re * fr + im * fi, im * fr - re * fi]
    even_part, odd_part = to_child(jnp.concatenate(rows, axis=0))
    weight_even, weight_odd = azimuth_rows(EVEN), azimuth_rows(ODD)
    for e, s in enumerate((0, 7)):
        for a in range(2):
            at = (2 * e + a) * KIDS
            for i in range(8):
                we, wo = float(weight_even[s, i]), float(weight_odd[s, i])
                if we or wo:
                    place = pl.ds(a * 8 + i, KIDS, stride=16)
                    out_ref[place, :] = out_ref[place, :] + (
                        we * even_part[at : at + KIDS] + wo * odd_part[at : at + KIDS]
                    )


VMEM_SPEC = pl.BlockSpec(memory_space=pltpu.VMEM)
HBM_SPEC = pl.BlockSpec(memory_space=pltpu.HBM)
LIMIT = 63 * 2**20


def f32(*shape):
    return jax.ShapeDtypeStruct(shape, jnp.float32)


def on_device(child, table, child_parent, child_octant, partner_src, partner_off, partner_count):
    up_left, up_right, down_right, down_left, phases = (jnp.asarray(a) for a in constants())
    vm = functools.partial(pltpu.VMEM, dtype=jnp.float32)
    ints = functools.partial(pltpu.VMEM, dtype=jnp.int32)
    bf16 = functools.partial(pltpu.VMEM, dtype=jnp.bfloat16)
    scalars = functools.partial(pltpu.SMEM, dtype=jnp.int32)
    out = pl.pallas_call(
        middle_kernel,
        out_shape=f32(KIDS * 16, 128),
        in_specs=[HBM_SPEC] * 12,
        out_specs=VMEM_SPEC,
        scratch_shapes=[
            ints((1, KIDS)), ints((1, KIDS)), scalars((1, KIDS)), scalars((1, KIDS)), vm((KIDS, 2, 8, 128)),
            ints((56, 128)), ints((56, 128)), ints((1, 128)), bf16((OFFSETS + 1, 2, 2304)), bf16((256, 128)),
            bf16((2, 256, 384)), vm((144, 128)), bf16((2, 2, 256, 128)), bf16((128, 256)), vm((2, 6, 8, 128)),
            ints((32, 128)), scalars((32, 128)), ints((8, 128)), scalars((8, 128)),
            bf16((2, 768, 256)), vm((2 * KIDS + 2, 8, 384)), vm((48, 8, 128)), vm((8 * TILES, 128)), vm((TILES, 8, 128)),
            vm((2 * KIDS, 8, 384)), vm((2, 768, 128)), vm((4, TILES, 128)), vm((4, TILES, 128)),
            *[vm((32, 2, HALF))] * 4, *[vm((32, 2, 2, HALF))] * 2, *[vm((32, 2, HALF))] * 2,
            vm((3, 8, 2, HALF)), vm((3, 32, 2, 384)), vm((3, 8, 2, 384)), vm((3, 2, 8, 2, 384)), vm((3, 8, 2, 384)),
            vm((8, 2, HALF)),
            pltpu.SemaphoreType.DMA((14,)), pltpu.SemaphoreType.DMA((19,)), pltpu.SemaphoreType.DMA((19,)),
        ],
        compiler_params=pltpu.CompilerParams(collective_id=0, has_side_effects=True, vmem_limit_bytes=LIMIT),
        name="middle",
    )(
        child_parent, child_octant.reshape(1, KIDS), child, partner_src.T, partner_off.T, partner_count.reshape(1, 128),
        table, up_left, up_right, phases, down_right, down_left,
    )
    return out.reshape(KIDS, 2, 8, 128)


def solution(mesh):
    return jax.shard_map(
        on_device,
        mesh=mesh,
        in_specs=(P("clus", None, "dir", None), P(None, None, "dir"), P("clus", None), P("clus"), P(), P(), P()),
        out_specs=P("clus", None, "dir", None),
        check_vma=False,
    )
```

```python
import functools
import math

import jax
import jax.numpy as jnp
import ml_dtypes
import numpy as np
from jax import lax
from jax.experimental import pallas as pl
from jax.experimental.pallas import tpu as pltpu
from jax.sharding import PartitionSpec as P

NT_C, NP_C, NT_P, NP_P = 128, 256, 192, 384
OFFSETS = 316
N_CLUS, N_DIR = 16, 32
PAR, KIDS = 8, 48
TILES = PAR * 6
MESH = pl.DeviceIdType.MESH
EVEN = np.array([-2, 0, 2, 4, 6, 8, 10, 14])
ODD = np.array([-1, 1, 3, 5, 7, 9, 11, 13])


def lagrange(t):
    out = []
    for m in range(5):
        w = np.ones_like(t)
        for n in range(5):
            if n != m:
                w = w * (t - n) / (m - n)
        out.append(w)
    return out


def polar_matrix():
    x = (np.arange(NT_P) + 0.5) * NT_C / NT_P - 0.5
    s = np.clip(np.floor(x + 0.5).astype(int) - 2, 0, NT_C - 5)
    w = lagrange(x - s)
    m = np.zeros((NT_P, NT_C))
    for k in range(5):
        m[np.arange(NT_P), s + k] = w[k]
    return m


SCALE = 243


def azimuth_rows(rows):
    x = rows * NP_C / NP_P
    b = np.floor(x + 0.5).astype(int)
    w = lagrange(x - b + 2)
    m = np.zeros((len(rows), 8))
    for k in range(5):
        for j in range(len(rows)):
            i = b[j] + k - 2
            if 0 <= i < 8:
                m[j, i] = w[k][j] * SCALE
    return np.round(m)


def halves(a):
    a = a.astype(np.float32)
    hi = a.astype(ml_dtypes.bfloat16)
    lo = (a - hi.astype(np.float32)).astype(ml_dtypes.bfloat16)
    return np.stack([hi, lo])


def in_tiles(even, odd):
    return np.stack([even[:, :128], np.concatenate([even[:, 128:], odd[:, :64]], 1), odd[:, 64:]])


@functools.cache
def constants():
    p = polar_matrix()
    ae, ao = azimuth_rows(EVEN), azimuth_rows(ODD)
    eye = np.eye(16)
    up_left = np.concatenate([np.kron(eye, ae), np.kron(eye, ao)], 0).astype(ml_dtypes.bfloat16)
    w = np.zeros((256, 384))
    w[:128, :192] = p.T
    w[128:, 192:] = p.T
    w = w / SCALE
    up_right = halves(w)
    down_right = halves(np.stack([w[:128, :256].T, w[128:, 128:].T]))
    down_left = np.concatenate([np.kron(eye, ae.T), np.kron(eye, ao.T)], 1).astype(ml_dtypes.bfloat16)
    theta = math.pi * (np.arange(NT_P) + 0.5) / NT_P
    phases = np.zeros((N_DIR, 3, 2, 3, 8, 128))
    for d in range(N_DIR):
        angle = []
        for rows in (EVEN, ODD):
            phi = 2 * math.pi * ((12 * d + rows) % NP_P) / NP_P
            angle.append(
                8 * math.pi
                * np.stack(
                    [
                        np.sin(theta) * np.cos(phi)[:, None],
                        np.sin(theta) * np.sin(phi)[:, None],
                        np.cos(theta) * np.ones((8, 1)),
                    ]
                )
            )
        for k in range(3):
            t = in_tiles(angle[0][k], angle[1][k])
            phases[d, k] = np.stack([np.cos(t), np.sin(t)])
    return up_left, up_right, down_right, down_left, phases.reshape(N_DIR, 144, 128).astype(np.float32)


def split(x):
    hi = x.astype(jnp.bfloat16)
    return hi, (x - hi.astype(jnp.float32)).astype(jnp.bfloat16)


def dot3(a, b):
    f = functools.partial(jnp.dot, preferred_element_type=jnp.float32)
    return f(a[0], b[0]) + (f(a[1], b[0]) + f(a[0], b[1]))


def dot2(a, b):
    f = functools.partial(jnp.dot, preferred_element_type=jnp.float32)
    return f(a, b[0]) + f(a, b[1])


def position():
    clus, direction = lax.axis_index("clus"), lax.axis_index("dir")
    core = lax.rem(direction, 2)
    x, z = lax.rem(clus, 4), lax.div(clus, 4)
    return clus, direction, core, x, z


def gather_member(core, x, z, k):
    return (1 - core) * (z * 4 + k) + core * (k * 4 + x)


def reduce_member(core, x, z, k):
    return (1 - core) * (k * 4 + x) + core * (z * 4 + k)


def octant_tables(base, table, edge):
    def tile(k, a, c):
        r = (k * 6 + a * 3 + c) * 8
        return base[r : r + 8, :]

    for c in range(3):
        ar, ai, br, bi, cr, ci = (tile(k, a, c) for k in range(3) for a in range(2))
        rr, ii, ri, ir = ar * br, ai * bi, ar * bi, ai * br
        for sx, sy, re, im in ((1, 1, rr - ii, ri + ir), (1, -1, rr + ii, ir - ri)):
            pr, pi, qr, qi = re * cr, im * ci, re * ci, im * cr
            for sz, fr, fi in ((1, pr - pi, qr + qi), (-1, pr + pi, qi - qr)):
                for sign in (1, -1):
                    o = (sx * sign < 0) + 2 * (sy * sign < 0) + 4 * (sz * sign < 0)
                    for t, f in ((c, fr), (3 + c, fi if sign > 0 else -fi)):
                        table[o * 6 + t] = f
                        edge[0, t, o : o + 1, :] = f[0:1]
                        edge[1, t, o : o + 1, :] = f[7:8]


def aligned(i, n=8):
    return pl.multiple_of(i, n)


def build_kids(parent_ref, kids_ref):
    parent = lax.broadcasted_iota(jnp.int32, (8, KIDS), 0)
    start = jnp.sum((parent_ref[...] < parent).astype(jnp.int32), axis=1, keepdims=True)
    number = jnp.sum((parent_ref[...] == parent).astype(jnp.int32), axis=1, keepdims=True)
    lane = lax.broadcasted_iota(jnp.int32, (8, 128), 1)
    own = jnp.where(lane < number, start + lane, KIDS)
    kids_ref[...] = jnp.where(lane < 8, own, jnp.minimum(start + lane - 8, KIDS - 1))


def build_index(src_ref, off_ref, count_ref, key_ref):
    clus, direction, core, x, z = position()
    src = src_ref[...]
    off = off_ref[...]
    slot = lax.broadcasted_iota(jnp.int32, src.shape, 0)
    own_x, own_z = (src >> 3) & 3, src >> 5
    here = jnp.where(core == 0, own_z, own_x) == jnp.where(core == 0, z, x)
    local = jnp.where(core == 0, own_x, own_z) * 8 + (src & 7)
    local = jnp.where(here & (slot < count_ref[...]), local, -1)
    which = lax.broadcasted_iota(jnp.int32, (32, 128), 0)
    key = jnp.full((32, 128), OFFSETS, jnp.int32)
    for p in range(src.shape[0]):
        key = jnp.where(which == local[p : p + 1], off[p : p + 1], key)
    key_ref[...] = key


def one_hot(row, n):
    square = (KIDS, KIDS)
    diagonal = lax.broadcasted_iota(jnp.int32, square, 0) == lax.broadcasted_iota(jnp.int32, square, 1)
    column = jnp.sum(jnp.where(diagonal, row, 0), axis=1, keepdims=True)
    hot = column == lax.broadcasted_iota(jnp.int32, (KIDS, n), 1)
    return jnp.where(hot, 1.0, 0.0).astype(jnp.bfloat16)


def pick(hot, tiles):
    return dot2(hot, split(jnp.concatenate(tiles, axis=1)))


def even_lanes():
    column = lax.rem(lax.broadcasted_iota(jnp.int32, (TILES, 128), 0), 3)
    lane = lax.broadcasted_iota(jnp.int32, (TILES, 128), 1)
    return (column == 0) | ((column == 1) & (lane < 64))


PAIRS = ((2, 3, 4), (0, 1, 5))
PIECES = (((768, 0, 1152),), ((0, 0, 768), (1920, 768, 384)))
HALF = 1152


def relay(tile_ref, s_ref, part, first, places=(0, 1, 2)):
    def parent(g, carry):
        for n, q in ((n, PAIRS[part][n]) for n in places):
            for c in range(3):
                lanes = slice(128 * (3 * n + c), 128 * (3 * n + c) + 128)
                s_ref[first + g, :, lanes] = tile_ref[pl.ds((g * 6 + c) * 8 + q + 1, 2, stride=24), :]
        return carry

    lax.fori_loop(0, PAR, parent, 0)


def unrelay(sum_ref, tile_ref, part):
    def parent(g, carry):
        for n, q in enumerate(PAIRS[part]):
            for c in range(3):
                lanes = slice(128 * (3 * n + c), 128 * (3 * n + c) + 128)
                tile_ref[pl.ds((g * 6 + c) * 8 + q + 1, 2, stride=24), :] = sum_ref[g, :, lanes]
        return carry

    lax.fori_loop(0, PAR, parent, 0)


def swap(s_ref, x_ref, block):
    def source(i, carry):
        at = block * 8 + i
        x_ref[at, 0:1, :] = s_ref[at, 1:2, :]
        x_ref[at, 1:2, :] = s_ref[at, 0:1, :]
        return carry

    lax.fori_loop(0, PAR, source, 0, unroll=2)


GROUP = 4


def add_pairs(part, key_ref, table_ref, s_ref, x_ref, block, first_target, acc):
    acc = [list(a) for a in acc]
    pieces = PIECES[part]
    for u in range(PAR):
        source = block * 8 + u
        for p, (at, to, n) in enumerate(pieces):
            s = s_ref[source, :, to : to + n]
            x = x_ref[source, :, to : to + n]
            for j in range(GROUP):
                t = table_ref[key_ref[source, first_target + j], :, at : at + n].astype(jnp.float32)
                acc[j][p] = acc[j][p] + t * s
                acc[j][len(pieces) + p] = acc[j][len(pieces) + p] + t * x
    return tuple(tuple(a) for a in acc)


def middle_kernel(
    parent_hbm, octant_hbm, child_hbm, src_hbm, off_hbm, count_hbm, table_hbm, left_hbm, right_hbm, phases_hbm,
    right2_hbm, left2_hbm,
    out_ref,
    parent_ref, octants_ref, parents_ref, octant_ref, child_ref, src_ref, off_ref, count_ref, table_ref, left_ref,
    right_ref, base_ref, right2_ref, left2_ref, edge_ref,
    key_ref, index_ref, kids_ref, kid_ref, y_ref, z_ref, phase_ref, tile_ref, inc_ref, r_ref, v_ref, pack_ref, halo_ref,
    sa_ref, sb_ref, xa_ref, xb_ref, acca_ref, accb_ref, pa_ref, pb_ref, gota_ref, pu_ref, gotu_ref, goto_ref, su_ref, sum_ref,
    local_sem, send_sem, recv_sem,
):
    clus, direction, core, x, z = position()
    after = (clus, lax.rem(direction + 1, N_DIR))
    before = (clus, lax.rem(direction + N_DIR - 1, N_DIR))
    source_me = (1 - core) * x + core * z
    target_me = (1 - core) * z + core * x
    source_blocks, target_blocks = (
        [me, 3 - me, lax.rem(me + 2, 4), me + 1 - 2 * lax.rem(me, 2)] for me in (source_me, target_me)
    )
    source_peers = [(gather_member(core, x, z, k), direction) for k in source_blocks[1:]]
    target_peers = [(reduce_member(core, x, z, k), direction) for k in target_blocks[1:]]
    barrier = pltpu.get_barrier_semaphore()
    peers = [after, before, *source_peers, *target_peers]
    for peer in peers:
        pl.semaphore_signal(barrier, inc=1, device_id=peer, device_id_type=MESH)

    def fetch(n, src, dst):
        copy = pltpu.make_async_copy(src, dst, local_sem.at[n])
        copy.start()
        return copy

    parents = fetch(0, parent_hbm, parent_ref)
    first = [
        fetch(1, left_hbm, left_ref),
        fetch(2, child_hbm, child_ref),
        fetch(3, right_hbm, right_ref),
        fetch(4, phases_hbm.at[direction], base_ref),
        fetch(5, src_hbm, src_ref),
        fetch(6, off_hbm, off_ref),
        fetch(7, count_hbm, count_ref),
    ]
    second = [
        fetch(8, octant_hbm, octant_ref),
        fetch(9, parent_hbm, parents_ref),
        fetch(10, octant_hbm, octants_ref),
    ]
    z_ref[2 * KIDS : 2 * KIDS + 2] = jnp.zeros((2, 8, 384), jnp.float32)
    table_ref[OFFSETS] = jnp.zeros((2, 2304), jnp.bfloat16)
    parents.wait()
    build_kids(parent_ref, kids_ref)
    kids = fetch(0, kids_ref, kid_ref)
    for copy in first:
        copy.wait()
    third = [
        fetch(11, table_hbm, table_ref.at[pl.ds(0, OFFSETS)]),
        fetch(12, right2_hbm, right2_ref),
        fetch(13, left2_hbm, left2_ref),
    ]
    build_index(src_ref, off_ref, count_ref, key_ref)
    for n in range(6):
        xs = split(child_ref[8 * n : 8 * n + 8].reshape(128, 128))
        eo = dot2(left_ref[...], xs)
        y = split(jnp.concatenate([eo[:128], eo[128:]], axis=1))
        for h in range(2):
            y_ref[h, 128 * n : 128 * n + 128, :] = y[h]
    z_ref[0 : 2 * KIDS] = dot3((y_ref[0], y_ref[1]), (right_ref[0], right_ref[1])).reshape(2 * KIDS, 8, 384)
    octant_tables(base_ref, phase_ref, edge_ref)
    index = fetch(1, key_ref, index_ref)
    kids.wait()
    for copy in second:
        copy.wait()

    def parent(g, carry):
        acc = [jnp.zeros((8, 128), jnp.float32) for _ in range(6)]
        for m in range(8):
            k = kid_ref[g, m]
            o = octant_ref[0, kid_ref[g, 8 + m]]
            for c in range(3):
                re = z_ref[k * 2, :, 128 * c : 128 * c + 128]
                im = z_ref[k * 2 + 1, :, 128 * c : 128 * c + 128]
                fr = phase_ref[o * 6 + c]
                fi = phase_ref[o * 6 + 3 + c]
                acc[c] = acc[c] + (re * fr - im * fi)
                acc[3 + c] = acc[3 + c] + (re * fi + im * fr)
        for t in range(6):
            tile_ref[pl.ds(aligned((g * 6 + t) * 8), 8), :] = acc[t]
        return carry

    lax.fori_loop(0, PAR, parent, 0)

    pl.semaphore_wait(barrier, len(peers))

    def send(n, src, dst, peer):
        copy = pltpu.make_async_remote_copy(
            src, dst, send_sem.at[n], recv_sem.at[n], device_id=peer, device_id_type=MESH
        )
        copy.start()
        return copy

    pack_ref[0] = tile_ref[pl.ds(7, TILES, stride=8), :]
    forward = send(0, pack_ref.at[0], halo_ref.at[0], after)
    pack_ref[1] = tile_ref[pl.ds(0, TILES, stride=8), :]
    backward = send(1, pack_ref.at[1], halo_ref.at[1], before)
    own = source_me * 8
    relay(tile_ref, sa_ref, 0, own)
    block_a = sa_ref.at[pl.ds(own, 8)]
    gather_a = [send(2 + r, block_a, block_a, peer) for r, peer in enumerate(source_peers)]
    swap(sa_ref, xa_ref, source_me)
    for copy in (index, *third):
        copy.wait()

    parts = ((sa_ref, xa_ref, acca_ref, pa_ref), (sb_ref, xb_ref, accb_ref, pb_ref))

    def own_pass(part):
        s_ref, x_ref, acc_ref, _ = parts[part]
        k = len(PIECES[part])

        def group(i, carry):
            j, g = lax.div(i, 2), lax.rem(i, 2) * GROUP
            zero = tuple(jnp.zeros((2, n), jnp.float32) for _ in range(2) for _, _, n in PIECES[part])
            acc = add_pairs(
                part, index_ref, table_ref, s_ref, x_ref, source_me, reduce_member(core, x, z, j) * 8 + g, (zero,) * GROUP
            )
            for t in range(GROUP):
                for p, (_, to, n) in enumerate(PIECES[part]):
                    acc_ref[j * 8 + g + t, 0, :, to : to + n] = acc[t][p]
                    acc_ref[j * 8 + g + t, 1, :, to : to + n] = acc[t][k + p]
            return carry

        lax.fori_loop(0, 32 // GROUP, group, 0)

    def load(part, target):
        acc_ref = parts[part][2]
        return tuple(
            tuple(acc_ref[target + t, h, :, to : to + n] for h in range(2) for _, to, n in PIECES[part])
            for t in range(GROUP)
        )

    def block_pass(part, block):
        s_ref, x_ref, acc_ref, _ = parts[part]
        k = len(PIECES[part])

        def group(i, carry):
            j, g = lax.div(i, 2), lax.rem(i, 2) * GROUP
            acc = add_pairs(
                part, index_ref, table_ref, s_ref, x_ref, block, reduce_member(core, x, z, j) * 8 + g, load(part, j * 8 + g)
            )
            for t in range(GROUP):
                for p, (_, to, n) in enumerate(PIECES[part]):
                    acc_ref[j * 8 + g + t, 0, :, to : to + n] = acc[t][p]
                    acc_ref[j * 8 + g + t, 1, :, to : to + n] = acc[t][k + p]
            return carry

        lax.fori_loop(0, 32 // GROUP, group, 0)

    def last_pass(part, j, blocks):
        s_ref, x_ref, _, p_ref = parts[part]
        k = len(PIECES[part])

        def group(i, carry):
            g = i * GROUP
            acc = load(part, j * 8 + g)
            for block in blocks:
                acc = add_pairs(
                    part, index_ref, table_ref, s_ref, x_ref, block, reduce_member(core, x, z, j) * 8 + g, acc
                )
            for t in range(GROUP):
                for p, (_, to, n) in enumerate(PIECES[part]):
                    a, b = acc[t][p], acc[t][k + p]
                    p_ref[j * 8 + g + t, 0:1, to : to + n] = a[0:1] - a[1:2]
                    p_ref[j * 8 + g + t, 1:2, to : to + n] = b[0:1] + b[1:2]
            return carry

        lax.fori_loop(0, PAR // GROUP, group, 0)

    even = even_lanes()
    at1, at2, at6 = (pl.ds(pair, TILES, stride=8) for pair in (1, 2, 6))

    def from_before():
        forward.wait_recv()
        got = halo_ref[0]
        tile_ref[at1, :] = tile_ref[at1, :] + jnp.where(even, 0.0, got)
        tile_ref[at2, :] = tile_ref[at2, :] + jnp.where(even, got, 0.0)
        relay(tile_ref, sb_ref, 1, own, (0, 1))

    def from_after():
        backward.wait_recv()
        tile_ref[at6, :] = tile_ref[at6, :] + halo_ref[1]
        relay(tile_ref, sb_ref, 1, own, (2,))

    def b_copy(first, lanes, late, r):
        n = (19 if late else 5) + r - 1
        block = sb_ref.at[pl.ds(own, 8), :, pl.ds(first, lanes)]
        return pltpu.make_async_remote_copy(
            block, block, send_sem.at[n], recv_sem.at[n], device_id=source_peers[r - 1], device_id_type=MESH
        )

    def b_wait(r, send_side):
        for c in range(2):

            @pl.when(core == c)
            def _():
                for first, lanes, late in ((0, 768, c == 0), (768, 384, c == 1)):
                    copy = b_copy(first, lanes, late, r)
                    if send_side:
                        copy.wait_send()
                    else:
                        copy.wait_recv()

    for late in (False, True):

        @pl.when(core == int(late))
        def _(late=late):
            from_after()
            for r in (1, 2, 3):
                b_copy(768, 384, late, r).start()

        @pl.when(core == 1 - int(late))
        def _(late=late):
            from_before()
            for r in (1, 2, 3):
                b_copy(0, 768, late, r).start()

        if not late:
            own_pass(0)
    swap(sb_ref, xb_ref, source_me)
    own_pass(1)

    def gathered(part, r):
        if part == 0:
            gather_a[r - 1].wait_recv()
        else:
            b_wait(r, False)
        swap(parts[part][0], parts[part][1], source_blocks[r])

    def reduce_to(part, r, got_ref):
        block = parts[part][3].at[pl.ds(target_blocks[r] * 8, 8)]
        return send(8 + 3 * part + r - 1, block, got_ref.at[r - 1], target_peers[r - 1])

    for r in (3, 2, 1):
        gathered(0, r)
    for r in (1, 2):
        last_pass(0, target_blocks[r], source_blocks[1:])
    for r in (3, 2):
        gathered(1, r)
        block_pass(1, source_blocks[r])
    gathered(1, 1)
    low = lax.broadcasted_iota(jnp.int32, (2, 128), 1) < 64
    for_before, for_after = 2 * core, 2 - 2 * core

    def pack(j):
        def parent(g, carry):
            t = j * 8 + g
            p = [pb_ref[t, :, 128 * n : 128 * n + 128] for n in range(9)]
            chunks = (
                (for_before, (p[3], jnp.where(low, p[4], p[1]), p[2])),
                (1, (p[0], jnp.where(low, p[1], p[4]), p[5])),
                (for_after, p[6:9]),
            )
            for chunk, tiles in chunks:
                for c in range(3):
                    pu_ref[chunk, t, :, 128 * c : 128 * c + 128] = tiles[c]
            return carry

        lax.fori_loop(0, PAR, parent, 0, unroll=2)

    urgent = []
    for r in (1, 2, 3):
        last_pass(1, target_blocks[r], source_blocks[1:2])
        pack(target_blocks[r])
        chunk = pu_ref.at[0, pl.ds(target_blocks[r] * 8, 8)]
        urgent.append(send(10 + r, chunk, gotu_ref.at[r - 1], target_peers[r - 1]))
    others = []
    for r in (1, 2, 3):
        chunks = pu_ref.at[pl.ds(1, 2), pl.ds(target_blocks[r] * 8, 8)]
        others.append(send(15 + r, chunks, goto_ref.at[r - 1], target_peers[r - 1]))
    reduces = [reduce_to(0, r, gota_ref) for r in (1, 2)]
    last_pass(0, target_blocks[3], source_blocks[1:])
    reduces.append(reduce_to(0, 3, gota_ref))
    last_pass(1, target_blocks[0], source_blocks[1:2])
    pack(target_blocks[0])
    last_pass(0, target_blocks[0], source_blocks[1:])

    def to_rows(chunk, slot):
        def parent(g, carry):
            for c in range(3):
                pack_ref[slot, pl.ds(g * 6 + c, 2, stride=3), :] = su_ref[chunk, g, :, 128 * c : 128 * c + 128]
            return carry

        lax.fori_loop(0, PAR, parent, 0, unroll=2)

    for copy in urgent:
        copy.wait_recv()

    def first_total(g, carry):
        su_ref[0, g] = (pu_ref[0, target_me * 8 + g] + gotu_ref[0, g]) + (gotu_ref[1, g] + gotu_ref[2, g])
        return carry

    lax.fori_loop(0, PAR, first_total, 0, unroll=2)
    to_rows(0, 2)
    far = (clus, lax.rem(direction + N_DIR - 1 + 2 * core, N_DIR))
    near = (clus, direction + 1 - 2 * core)
    last_far = send(14, pack_ref.at[2], halo_ref.at[2 + core], far)
    for copy in others:
        copy.wait_recv()

    def other_totals(g, carry):
        for n in range(2):
            own_sum = pu_ref[1 + n, target_me * 8 + g]
            su_ref[1 + n, g] = (own_sum + goto_ref[0, n, g]) + (goto_ref[1, n, g] + goto_ref[2, n, g])
        return carry

    lax.fori_loop(0, PAR, other_totals, 0, unroll=2)
    to_rows(2, 3)
    last_near = send(15, pack_ref.at[3], halo_ref.at[3 - core], near)

    def unpack(g, carry):
        f, rest, last = (
            [su_ref[chunk, g, :, 128 * c : 128 * c + 128] for c in range(3)] for chunk in (for_before, 1, for_after)
        )
        pairs = (
            (0, (rest[0], jnp.where(low, rest[1], f[1]), f[2])),
            (1, (f[0], jnp.where(low, f[1], rest[1]), rest[2])),
            (5, last),
        )
        for q, tiles in pairs:
            for c in range(3):
                tile_ref[pl.ds((g * 6 + c) * 8 + q + 1, 2, stride=24), :] = tiles[c]
        return carry

    lax.fori_loop(0, PAR, unpack, 0)
    for copy in reduces:
        copy.wait_recv()

    def last_total(g, carry):
        sum_ref[g] = (pa_ref[target_me * 8 + g] + gota_ref[0, g]) + (gota_ref[1, g] + gota_ref[2, g])
        return carry

    lax.fori_loop(0, PAR, last_total, 0, unroll=2)
    unrelay(sum_ref, tile_ref, 0)
    pair = lax.broadcasted_iota(jnp.int32, (8, 128), 0)
    inside = (pair > 0) & (pair < 7)
    for t in range(TILES):
        inc_ref[t] = jnp.where(inside, tile_ref[8 * t : 8 * t + 8, :], 0.0)

    def child(k, carry):
        g, o = parents_ref[0, k], octant_ref[0, k]
        for c in range(3):
            re, im = inc_ref[g * 6 + c], inc_ref[g * 6 + 3 + c]
            fr, fi = phase_ref[o * 6 + c], phase_ref[o * 6 + 3 + c]
            r_ref[k * 2, :, 128 * c : 128 * c + 128] = re * fr + im * fi
            r_ref[k * 2 + 1, :, 128 * c : 128 * c + 128] = im * fr - re * fi
        return carry

    lax.fori_loop(0, KIDS, child, 0, unroll=4)

    def to_child(r):
        hi, lo = split(r)
        return (
            dot3((hi[:, :256], lo[:, :256]), (right2_ref[0, 0], right2_ref[1, 0])),
            dot3((hi[:, 128:], lo[:, 128:]), (right2_ref[0, 1], right2_ref[1, 1])),
        )

    v_ref[0], v_ref[1] = to_child(r_ref[...].reshape(768, 384))
    for n in range(6):
        at = slice(128 * n, 128 * n + 128)
        out_ref[at, :] = dot2(left2_ref[...], split(jnp.concatenate([v_ref[0, at, :], v_ref[1, at, :]], axis=0)))
    hot_parent, hot_octant = one_hot(parent_ref[...], 8), one_hot(octants_ref[...], 8)
    shifts = [pick(hot_octant, [edge_ref[e, t] for t in range(6)]) for e in range(2)]
    for copy in (forward, backward, *gather_a, *reduces, *urgent, *others):
        copy.wait_send()
    for r in (1, 2, 3):
        b_wait(r, True)
    last_near.wait()
    last_far.wait()
    rows = []
    for e in range(2):
        values = pick(hot_parent, [halo_ref[3 - e, pl.ds(t, 8, stride=6), :] for t in range(6)])
        re, im, fr, fi = values[:, :384], values[:, 384:], shifts[e][:, :384], shifts[e][:, 384:]
        rows += [re * fr + im * fi, im * fr - re * fi]
    even_part, odd_part = to_child(jnp.concatenate(rows, axis=0))
    weight_even, weight_odd = azimuth_rows(EVEN), azimuth_rows(ODD)
    for e, s in enumerate((0, 7)):
        for a in range(2):
            at = (2 * e + a) * KIDS
            for i in range(8):
                we, wo = float(weight_even[s, i]), float(weight_odd[s, i])
                if we or wo:
                    place = pl.ds(a * 8 + i, KIDS, stride=16)
                    out_ref[place, :] = out_ref[place, :] + (
                        we * even_part[at : at + KIDS] + wo * odd_part[at : at + KIDS]
                    )


VMEM_SPEC = pl.BlockSpec(memory_space=pltpu.VMEM)
HBM_SPEC = pl.BlockSpec(memory_space=pltpu.HBM)
LIMIT = 63 * 2**20


def f32(*shape):
    return jax.ShapeDtypeStruct(shape, jnp.float32)


def on_device(child, table, child_parent, child_octant, partner_src, partner_off, partner_count):
    up_left, up_right, down_right, down_left, phases = (jnp.asarray(a) for a in constants())
    vm = functools.partial(pltpu.VMEM, dtype=jnp.float32)
    ints = functools.partial(pltpu.VMEM, dtype=jnp.int32)
    bf16 = functools.partial(pltpu.VMEM, dtype=jnp.bfloat16)
    scalars = functools.partial(pltpu.SMEM, dtype=jnp.int32)
    out = pl.pallas_call(
        middle_kernel,
        out_shape=f32(KIDS * 16, 128),
        in_specs=[HBM_SPEC] * 12,
        out_specs=VMEM_SPEC,
        scratch_shapes=[
            ints((1, KIDS)), ints((1, KIDS)), scalars((1, KIDS)), scalars((1, KIDS)), vm((KIDS, 2, 8, 128)),
            ints((56, 128)), ints((56, 128)), ints((1, 128)), bf16((OFFSETS + 1, 2, 2304)), bf16((256, 128)),
            bf16((2, 256, 384)), vm((144, 128)), bf16((2, 2, 256, 128)), bf16((128, 256)), vm((2, 6, 8, 128)),
            ints((32, 128)), scalars((32, 128)), ints((8, 128)), scalars((8, 128)),
            bf16((2, 768, 256)), vm((2 * KIDS + 2, 8, 384)), vm((48, 8, 128)), vm((8 * TILES, 128)), vm((TILES, 8, 128)),
            vm((2 * KIDS, 8, 384)), vm((2, 768, 128)), vm((4, TILES, 128)), vm((4, TILES, 128)),
            *[vm((32, 2, HALF))] * 4, *[vm((32, 2, 2, HALF))] * 2, *[vm((32, 2, HALF))] * 2,
            vm((3, 8, 2, HALF)), vm((3, 32, 2, 384)), vm((3, 8, 2, 384)), vm((3, 2, 8, 2, 384)), vm((3, 8, 2, 384)),
            vm((8, 2, HALF)),
            pltpu.SemaphoreType.DMA((14,)), pltpu.SemaphoreType.DMA((22,)), pltpu.SemaphoreType.DMA((22,)),
        ],
        compiler_params=pltpu.CompilerParams(collective_id=0, has_side_effects=True, vmem_limit_bytes=LIMIT),
        name="middle",
    )(
        child_parent, child_octant.reshape(1, KIDS), child, partner_src.T, partner_off.T, partner_count.reshape(1, 128),
        table, up_left, up_right, phases, down_right, down_left,
    )
    return out.reshape(KIDS, 2, 8, 128)


def solution(mesh):
    return jax.shard_map(
        on_device,
        mesh=mesh,
        in_specs=(P("clus", None, "dir", None), P(None, None, "dir"), P("clus", None), P("clus"), P(), P(), P()),
        out_specs=P("clus", None, "dir", None),
        check_vma=False,
    )
```

```python
import functools
import math

import jax
import jax.numpy as jnp
import ml_dtypes
import numpy as np
from jax import lax
from jax.experimental import pallas as pl
from jax.experimental.pallas import tpu as pltpu
from jax.sharding import PartitionSpec as P

NT_C, NP_C, NT_P, NP_P = 128, 256, 192, 384
OFFSETS = 316
N_CLUS, N_DIR = 16, 32
PAR, KIDS = 8, 48
TILES = PAR * 6
MESH = pl.DeviceIdType.MESH
EVEN = np.array([-2, 0, 2, 4, 6, 8, 10, 14])
ODD = np.array([-1, 1, 3, 5, 7, 9, 11, 13])


def lagrange(t):
    out = []
    for m in range(5):
        w = np.ones_like(t)
        for n in range(5):
            if n != m:
                w = w * (t - n) / (m - n)
        out.append(w)
    return out


def polar_matrix():
    x = (np.arange(NT_P) + 0.5) * NT_C / NT_P - 0.5
    s = np.clip(np.floor(x + 0.5).astype(int) - 2, 0, NT_C - 5)
    w = lagrange(x - s)
    m = np.zeros((NT_P, NT_C))
    for k in range(5):
        m[np.arange(NT_P), s + k] = w[k]
    return m


SCALE = 243


def azimuth_rows(rows):
    x = rows * NP_C / NP_P
    b = np.floor(x + 0.5).astype(int)
    w = lagrange(x - b + 2)
    m = np.zeros((len(rows), 8))
    for k in range(5):
        for j in range(len(rows)):
            i = b[j] + k - 2
            if 0 <= i < 8:
                m[j, i] = w[k][j] * SCALE
    return np.round(m)


def halves(a):
    a = a.astype(np.float32)
    hi = a.astype(ml_dtypes.bfloat16)
    lo = (a - hi.astype(np.float32)).astype(ml_dtypes.bfloat16)
    return np.stack([hi, lo])


def in_tiles(even, odd):
    return np.stack([even[:, :128], np.concatenate([even[:, 128:], odd[:, :64]], 1), odd[:, 64:]])


@functools.cache
def constants():
    p = polar_matrix()
    ae, ao = azimuth_rows(EVEN), azimuth_rows(ODD)
    eye = np.eye(16)
    up_left = np.concatenate([np.kron(eye, ae), np.kron(eye, ao)], 0).astype(ml_dtypes.bfloat16)
    w = np.zeros((256, 384))
    w[:128, :192] = p.T
    w[128:, 192:] = p.T
    w = w / SCALE
    up_right = halves(w)
    down_right = halves(np.stack([w[:128, :256].T, w[128:, 128:].T]))
    down_left = np.concatenate([np.kron(eye, ae.T), np.kron(eye, ao.T)], 1).astype(ml_dtypes.bfloat16)
    theta = math.pi * (np.arange(NT_P) + 0.5) / NT_P
    phases = np.zeros((N_DIR, 3, 2, 3, 8, 128))
    for d in range(N_DIR):
        angle = []
        for rows in (EVEN, ODD):
            phi = 2 * math.pi * ((12 * d + rows) % NP_P) / NP_P
            angle.append(
                8 * math.pi
                * np.stack(
                    [
                        np.sin(theta) * np.cos(phi)[:, None],
                        np.sin(theta) * np.sin(phi)[:, None],
                        np.cos(theta) * np.ones((8, 1)),
                    ]
                )
            )
        for k in range(3):
            t = in_tiles(angle[0][k], angle[1][k])
            phases[d, k] = np.stack([np.cos(t), np.sin(t)])
    return up_left, up_right, down_right, down_left, phases.reshape(N_DIR, 144, 128).astype(np.float32)


def split(x):
    hi = x.astype(jnp.bfloat16)
    return hi, (x - hi.astype(jnp.float32)).astype(jnp.bfloat16)


def dot3(a, b):
    f = functools.partial(jnp.dot, preferred_element_type=jnp.float32)
    return f(a[0], b[0]) + (f(a[1], b[0]) + f(a[0], b[1]))


def dot2(a, b):
    f = functools.partial(jnp.dot, preferred_element_type=jnp.float32)
    return f(a, b[0]) + f(a, b[1])


def position():
    clus, direction = lax.axis_index("clus"), lax.axis_index("dir")
    core = lax.rem(direction, 2)
    x, z = lax.rem(clus, 4), lax.div(clus, 4)
    return clus, direction, core, x, z


def gather_member(core, x, z, k):
    return (1 - core) * (z * 4 + k) + core * (k * 4 + x)


def reduce_member(core, x, z, k):
    return (1 - core) * (k * 4 + x) + core * (z * 4 + k)


def octant_tables(base, table, edge):
    def tile(k, a, c):
        r = (k * 6 + a * 3 + c) * 8
        return base[r : r + 8, :]

    for c in range(3):
        ar, ai, br, bi, cr, ci = (tile(k, a, c) for k in range(3) for a in range(2))
        rr, ii, ri, ir = ar * br, ai * bi, ar * bi, ai * br
        for sx, sy, re, im in ((1, 1, rr - ii, ri + ir), (1, -1, rr + ii, ir - ri)):
            pr, pi, qr, qi = re * cr, im * ci, re * ci, im * cr
            for sz, fr, fi in ((1, pr - pi, qr + qi), (-1, pr + pi, qi - qr)):
                for sign in (1, -1):
                    o = (sx * sign < 0) + 2 * (sy * sign < 0) + 4 * (sz * sign < 0)
                    for t, f in ((c, fr), (3 + c, fi if sign > 0 else -fi)):
                        table[o * 6 + t] = f
                        edge[0, t, o : o + 1, :] = f[0:1]
                        edge[1, t, o : o + 1, :] = f[7:8]


def aligned(i, n=8):
    return pl.multiple_of(i, n)


def build_kids(parent_ref, kids_ref):
    parent = lax.broadcasted_iota(jnp.int32, (8, KIDS), 0)
    start = jnp.sum((parent_ref[...] < parent).astype(jnp.int32), axis=1, keepdims=True)
    number = jnp.sum((parent_ref[...] == parent).astype(jnp.int32), axis=1, keepdims=True)
    lane = lax.broadcasted_iota(jnp.int32, (8, 128), 1)
    own = jnp.where(lane < number, start + lane, KIDS)
    kids_ref[...] = jnp.where(lane < 8, own, jnp.minimum(start + lane - 8, KIDS - 1))


def build_index(src_ref, off_ref, count_ref, key_ref):
    clus, direction, core, x, z = position()
    src = src_ref[...]
    off = off_ref[...]
    slot = lax.broadcasted_iota(jnp.int32, src.shape, 0)
    own_x, own_z = (src >> 3) & 3, src >> 5
    here = jnp.where(core == 0, own_z, own_x) == jnp.where(core == 0, z, x)
    local = jnp.where(core == 0, own_x, own_z) * 8 + (src & 7)
    local = jnp.where(here & (slot < count_ref[...]), local, -1)
    which = lax.broadcasted_iota(jnp.int32, (32, 128), 0)
    key = jnp.full((32, 128), OFFSETS, jnp.int32)
    for p in range(src.shape[0]):
        key = jnp.where(which == local[p : p + 1], off[p : p + 1], key)
    key_ref[...] = key


def one_hot(row, n):
    square = (KIDS, KIDS)
    diagonal = lax.broadcasted_iota(jnp.int32, square, 0) == lax.broadcasted_iota(jnp.int32, square, 1)
    column = jnp.sum(jnp.where(diagonal, row, 0), axis=1, keepdims=True)
    hot = column == lax.broadcasted_iota(jnp.int32, (KIDS, n), 1)
    return jnp.where(hot, 1.0, 0.0).astype(jnp.bfloat16)


def pick(hot, tiles):
    return dot2(hot, split(jnp.concatenate(tiles, axis=1)))


def even_lanes():
    column = lax.rem(lax.broadcasted_iota(jnp.int32, (TILES, 128), 0), 3)
    lane = lax.broadcasted_iota(jnp.int32, (TILES, 128), 1)
    return (column == 0) | ((column == 1) & (lane < 64))


PAIRS = ((2, 3, 4), (0, 1, 5))
PIECES = (((768, 0, 1152),), ((0, 0, 768), (1920, 768, 384)))
HALF = 1152


def relay(tile_ref, s_ref, part, first, places=(0, 1, 2)):
    def parent(g, carry):
        for n, q in ((n, PAIRS[part][n]) for n in places):
            for c in range(3):
                lanes = slice(128 * (3 * n + c), 128 * (3 * n + c) + 128)
                s_ref[first + g, :, lanes] = tile_ref[pl.ds((g * 6 + c) * 8 + q + 1, 2, stride=24), :]
        return carry

    lax.fori_loop(0, PAR, parent, 0)


def unrelay(sum_ref, tile_ref, part):
    def parent(g, carry):
        for n, q in enumerate(PAIRS[part]):
            for c in range(3):
                lanes = slice(128 * (3 * n + c), 128 * (3 * n + c) + 128)
                tile_ref[pl.ds((g * 6 + c) * 8 + q + 1, 2, stride=24), :] = sum_ref[g, :, lanes]
        return carry

    lax.fori_loop(0, PAR, parent, 0)


def swap(s_ref, x_ref, block):
    def source(i, carry):
        at = block * 8 + i
        x_ref[at, 0:1, :] = s_ref[at, 1:2, :]
        x_ref[at, 1:2, :] = s_ref[at, 0:1, :]
        return carry

    lax.fori_loop(0, PAR, source, 0, unroll=2)


GROUP = 4


def add_pairs(part, key_ref, table_ref, s_ref, x_ref, block, first_target, acc):
    acc = [list(a) for a in acc]
    pieces = PIECES[part]
    for u in range(PAR):
        source = block * 8 + u
        for p, (at, to, n) in enumerate(pieces):
            s = s_ref[source, :, to : to + n]
            x = x_ref[source, :, to : to + n]
            for j in range(GROUP):
                t = table_ref[key_ref[source, first_target + j], :, at : at + n].astype(jnp.float32)
                acc[j][p] = acc[j][p] + t * s
                acc[j][len(pieces) + p] = acc[j][len(pieces) + p] + t * x
    return tuple(tuple(a) for a in acc)


def middle_kernel(
    parent_hbm, octant_hbm, child_hbm, src_hbm, off_hbm, count_hbm, table_hbm, left_hbm, right_hbm, phases_hbm,
    right2_hbm, left2_hbm,
    out_ref,
    parent_ref, octants_ref, parents_ref, octant_ref, child_ref, src_ref, off_ref, count_ref, table_ref, left_ref,
    right_ref, base_ref, right2_ref, left2_ref, edge_ref,
    key_ref, index_ref, kids_ref, kid_ref, y_ref, z_ref, phase_ref, tile_ref, inc_ref, r_ref, v_ref, pack_ref, halo_ref,
    sa_ref, sb_ref, xa_ref, xb_ref, acca_ref, accb_ref, pa_ref, pb_ref, gota_ref, pu_ref, gotu_ref, goto_ref, su_ref, sum_ref,
    local_sem, send_sem, recv_sem,
):
    clus, direction, core, x, z = position()
    after = (clus, lax.rem(direction + 1, N_DIR))
    before = (clus, lax.rem(direction + N_DIR - 1, N_DIR))
    source_me = (1 - core) * x + core * z
    target_me = (1 - core) * z + core * x
    source_blocks, target_blocks = (
        [me, 3 - me, lax.rem(me + 2, 4), me + 1 - 2 * lax.rem(me, 2)] for me in (source_me, target_me)
    )
    source_peers = [(gather_member(core, x, z, k), direction) for k in source_blocks[1:]]
    target_peers = [(reduce_member(core, x, z, k), direction) for k in target_blocks[1:]]
    barrier = pltpu.get_barrier_semaphore()
    peers = [after, before, *source_peers, *target_peers]
    for peer in peers:
        pl.semaphore_signal(barrier, inc=1, device_id=peer, device_id_type=MESH)

    def fetch(n, src, dst):
        copy = pltpu.make_async_copy(src, dst, local_sem.at[n])
        copy.start()
        return copy

    parents = fetch(0, parent_hbm, parent_ref)
    first = [
        fetch(1, left_hbm, left_ref),
        fetch(2, child_hbm, child_ref),
        fetch(3, right_hbm, right_ref),
        fetch(4, phases_hbm.at[direction], base_ref),
        fetch(5, src_hbm, src_ref),
        fetch(6, off_hbm, off_ref),
        fetch(7, count_hbm, count_ref),
    ]
    second = [
        fetch(8, octant_hbm, octant_ref),
        fetch(9, parent_hbm, parents_ref),
        fetch(10, octant_hbm, octants_ref),
    ]
    z_ref[2 * KIDS : 2 * KIDS + 2] = jnp.zeros((2, 8, 384), jnp.float32)
    table_ref[OFFSETS] = jnp.zeros((2, 2304), jnp.bfloat16)
    parents.wait()
    build_kids(parent_ref, kids_ref)
    kids = fetch(0, kids_ref, kid_ref)
    for copy in first:
        copy.wait()
    third = [
        fetch(11, table_hbm, table_ref.at[pl.ds(0, OFFSETS)]),
        fetch(12, right2_hbm, right2_ref),
        fetch(13, left2_hbm, left2_ref),
    ]
    build_index(src_ref, off_ref, count_ref, key_ref)
    for n in range(6):
        xs = split(child_ref[8 * n : 8 * n + 8].reshape(128, 128))
        eo = dot2(left_ref[...], xs)
        y = split(jnp.concatenate([eo[:128], eo[128:]], axis=1))
        for h in range(2):
            y_ref[h, 128 * n : 128 * n + 128, :] = y[h]
    z_ref[0 : 2 * KIDS] = dot3((y_ref[0], y_ref[1]), (right_ref[0], right_ref[1])).reshape(2 * KIDS, 8, 384)
    octant_tables(base_ref, phase_ref, edge_ref)
    index = fetch(1, key_ref, index_ref)
    kids.wait()
    for copy in second:
        copy.wait()

    def parent(g, carry):
        acc = [jnp.zeros((8, 128), jnp.float32) for _ in range(6)]
        for m in range(8):
            k = kid_ref[g, m]
            o = octant_ref[0, kid_ref[g, 8 + m]]
            for c in range(3):
                re = z_ref[k * 2, :, 128 * c : 128 * c + 128]
                im = z_ref[k * 2 + 1, :, 128 * c : 128 * c + 128]
                fr = phase_ref[o * 6 + c]
                fi = phase_ref[o * 6 + 3 + c]
                acc[c] = acc[c] + (re * fr - im * fi)
                acc[3 + c] = acc[3 + c] + (re * fi + im * fr)
        for t in range(6):
            tile_ref[pl.ds(aligned((g * 6 + t) * 8), 8), :] = acc[t]
        return carry

    lax.fori_loop(0, PAR, parent, 0)

    pl.semaphore_wait(barrier, len(peers))

    def send(n, src, dst, peer):
        copy = pltpu.make_async_remote_copy(
            src, dst, send_sem.at[n], recv_sem.at[n], device_id=peer, device_id_type=MESH
        )
        copy.start()
        return copy

    pack_ref[0] = tile_ref[pl.ds(7, TILES, stride=8), :]
    forward = send(0, pack_ref.at[0], halo_ref.at[0], after)
    pack_ref[1] = tile_ref[pl.ds(0, TILES, stride=8), :]
    backward = send(1, pack_ref.at[1], halo_ref.at[1], before)
    own = source_me * 8
    relay(tile_ref, sa_ref, 0, own)
    block_a = sa_ref.at[pl.ds(own, 8)]
    gather_a = [send(2 + r, block_a, block_a, peer) for r, peer in enumerate(source_peers)]
    swap(sa_ref, xa_ref, source_me)
    for copy in (index, *third):
        copy.wait()

    parts = ((sa_ref, xa_ref, acca_ref, pa_ref), (sb_ref, xb_ref, accb_ref, pb_ref))

    def own_pass(part):
        s_ref, x_ref, acc_ref, _ = parts[part]
        k = len(PIECES[part])

        def group(i, carry):
            j, g = lax.div(i, 2), lax.rem(i, 2) * GROUP
            zero = tuple(jnp.zeros((2, n), jnp.float32) for _ in range(2) for _, _, n in PIECES[part])
            acc = add_pairs(
                part, index_ref, table_ref, s_ref, x_ref, source_me, reduce_member(core, x, z, j) * 8 + g, (zero,) * GROUP
            )
            for t in range(GROUP):
                for p, (_, to, n) in enumerate(PIECES[part]):
                    acc_ref[j * 8 + g + t, 0, :, to : to + n] = acc[t][p]
                    acc_ref[j * 8 + g + t, 1, :, to : to + n] = acc[t][k + p]
            return carry

        lax.fori_loop(0, 32 // GROUP, group, 0)

    def load(part, target):
        acc_ref = parts[part][2]
        return tuple(
            tuple(acc_ref[target + t, h, :, to : to + n] for h in range(2) for _, to, n in PIECES[part])
            for t in range(GROUP)
        )

    def block_pass(part, block):
        s_ref, x_ref, acc_ref, _ = parts[part]
        k = len(PIECES[part])

        def group(i, carry):
            j, g = lax.div(i, 2), lax.rem(i, 2) * GROUP
            acc = add_pairs(
                part, index_ref, table_ref, s_ref, x_ref, block, reduce_member(core, x, z, j) * 8 + g, load(part, j * 8 + g)
            )
            for t in range(GROUP):
                for p, (_, to, n) in enumerate(PIECES[part]):
                    acc_ref[j * 8 + g + t, 0, :, to : to + n] = acc[t][p]
                    acc_ref[j * 8 + g + t, 1, :, to : to + n] = acc[t][k + p]
            return carry

        lax.fori_loop(0, 32 // GROUP, group, 0)

    def last_pass(part, j, blocks):
        s_ref, x_ref, _, p_ref = parts[part]
        k = len(PIECES[part])

        def group(i, carry):
            g = i * GROUP
            acc = load(part, j * 8 + g)
            for block in blocks:
                acc = add_pairs(
                    part, index_ref, table_ref, s_ref, x_ref, block, reduce_member(core, x, z, j) * 8 + g, acc
                )
            for t in range(GROUP):
                for p, (_, to, n) in enumerate(PIECES[part]):
                    a, b = acc[t][p], acc[t][k + p]
                    p_ref[j * 8 + g + t, 0:1, to : to + n] = a[0:1] - a[1:2]
                    p_ref[j * 8 + g + t, 1:2, to : to + n] = b[0:1] + b[1:2]
            return carry

        lax.fori_loop(0, PAR // GROUP, group, 0)

    even = even_lanes()
    at1, at2, at6 = (pl.ds(pair, TILES, stride=8) for pair in (1, 2, 6))

    def from_before():
        forward.wait_recv()
        got = halo_ref[0]
        tile_ref[at1, :] = tile_ref[at1, :] + jnp.where(even, 0.0, got)
        tile_ref[at2, :] = tile_ref[at2, :] + jnp.where(even, got, 0.0)
        relay(tile_ref, sb_ref, 1, own, (0, 1))

    def from_after():
        backward.wait_recv()
        tile_ref[at6, :] = tile_ref[at6, :] + halo_ref[1]
        relay(tile_ref, sb_ref, 1, own, (2,))

    def b_copy(first, lanes, late, r):
        n = (19 if late else 5) + r - 1
        block = sb_ref.at[pl.ds(own, 8), :, pl.ds(first, lanes)]
        return pltpu.make_async_remote_copy(
            block, block, send_sem.at[n], recv_sem.at[n], device_id=source_peers[r - 1], device_id_type=MESH
        )

    def b_wait(r, send_side):
        for c in range(2):

            @pl.when(core == c)
            def _():
                for first, lanes, late in ((0, 768, c == 0), (768, 384, c == 1)):
                    copy = b_copy(first, lanes, late, r)
                    if send_side:
                        copy.wait_send()
                    else:
                        copy.wait_recv()

    for late in (False, True):

        @pl.when(core == int(late))
        def _(late=late):
            from_after()
            for r in (1, 2, 3):
                b_copy(768, 384, late, r).start()

        @pl.when(core == 1 - int(late))
        def _(late=late):
            from_before()
            for r in (1, 2, 3):
                b_copy(0, 768, late, r).start()

        if not late:
            own_pass(0)
    swap(sb_ref, xb_ref, source_me)
    own_pass(1)

    def gathered(part, r):
        if part == 0:
            gather_a[r - 1].wait_recv()
        else:
            b_wait(r, False)
        swap(parts[part][0], parts[part][1], source_blocks[r])

    def reduce_to(part, r, got_ref):
        block = parts[part][3].at[pl.ds(target_blocks[r] * 8, 8)]
        return send(8 + 3 * part + r - 1, block, got_ref.at[r - 1], target_peers[r - 1])

    for r in (3, 2):
        gathered(1, r)
        block_pass(1, source_blocks[r])
    gathered(1, 1)
    low = lax.broadcasted_iota(jnp.int32, (2, 128), 1) < 64
    for_before, for_after = 2 * core, 2 - 2 * core

    def pack(j):
        def parent(g, carry):
            t = j * 8 + g
            p = [pb_ref[t, :, 128 * n : 128 * n + 128] for n in range(9)]
            chunks = (
                (for_before, (p[3], jnp.where(low, p[4], p[1]), p[2])),
                (1, (p[0], jnp.where(low, p[1], p[4]), p[5])),
                (for_after, p[6:9]),
            )
            for chunk, tiles in chunks:
                for c in range(3):
                    pu_ref[chunk, t, :, 128 * c : 128 * c + 128] = tiles[c]
            return carry

        lax.fori_loop(0, PAR, parent, 0, unroll=2)

    urgent = []
    for r in (1, 2, 3):
        last_pass(1, target_blocks[r], source_blocks[1:2])
        pack(target_blocks[r])
        chunk = pu_ref.at[0, pl.ds(target_blocks[r] * 8, 8)]
        urgent.append(send(10 + r, chunk, gotu_ref.at[r - 1], target_peers[r - 1]))
    others = []
    for r in (1, 2, 3):
        chunks = pu_ref.at[pl.ds(1, 2), pl.ds(target_blocks[r] * 8, 8)]
        others.append(send(15 + r, chunks, goto_ref.at[r - 1], target_peers[r - 1]))
    for r in (3, 2, 1):
        gathered(0, r)
    reduces = []
    for r in (1, 2, 3):
        last_pass(0, target_blocks[r], source_blocks[1:])
        reduces.append(reduce_to(0, r, gota_ref))
    last_pass(1, target_blocks[0], source_blocks[1:2])
    pack(target_blocks[0])
    last_pass(0, target_blocks[0], source_blocks[1:])

    def to_rows(chunk, slot):
        def parent(g, carry):
            for c in range(3):
                pack_ref[slot, pl.ds(g * 6 + c, 2, stride=3), :] = su_ref[chunk, g, :, 128 * c : 128 * c + 128]
            return carry

        lax.fori_loop(0, PAR, parent, 0, unroll=2)

    for copy in urgent:
        copy.wait_recv()

    def first_total(g, carry):
        su_ref[0, g] = (pu_ref[0, target_me * 8 + g] + gotu_ref[0, g]) + (gotu_ref[1, g] + gotu_ref[2, g])
        return carry

    lax.fori_loop(0, PAR, first_total, 0, unroll=2)
    to_rows(0, 2)
    far = (clus, lax.rem(direction + N_DIR - 1 + 2 * core, N_DIR))
    near = (clus, direction + 1 - 2 * core)
    last_far = send(14, pack_ref.at[2], halo_ref.at[2 + core], far)
    for copy in others:
        copy.wait_recv()

    def other_totals(g, carry):
        for n in range(2):
            own_sum = pu_ref[1 + n, target_me * 8 + g]
            su_ref[1 + n, g] = (own_sum + goto_ref[0, n, g]) + (goto_ref[1, n, g] + goto_ref[2, n, g])
        return carry

    lax.fori_loop(0, PAR, other_totals, 0, unroll=2)
    to_rows(2, 3)
    last_near = send(15, pack_ref.at[3], halo_ref.at[3 - core], near)

    def unpack(g, carry):
        f, rest, last = (
            [su_ref[chunk, g, :, 128 * c : 128 * c + 128] for c in range(3)] for chunk in (for_before, 1, for_after)
        )
        pairs = (
            (0, (rest[0], jnp.where(low, rest[1], f[1]), f[2])),
            (1, (f[0], jnp.where(low, f[1], rest[1]), rest[2])),
            (5, last),
        )
        for q, tiles in pairs:
            for c in range(3):
                tile_ref[pl.ds((g * 6 + c) * 8 + q + 1, 2, stride=24), :] = tiles[c]
        return carry

    lax.fori_loop(0, PAR, unpack, 0)
    for copy in reduces:
        copy.wait_recv()

    def last_total(g, carry):
        sum_ref[g] = (pa_ref[target_me * 8 + g] + gota_ref[0, g]) + (gota_ref[1, g] + gota_ref[2, g])
        return carry

    lax.fori_loop(0, PAR, last_total, 0, unroll=2)
    unrelay(sum_ref, tile_ref, 0)
    pair = lax.broadcasted_iota(jnp.int32, (8, 128), 0)
    inside = (pair > 0) & (pair < 7)
    for t in range(TILES):
        inc_ref[t] = jnp.where(inside, tile_ref[8 * t : 8 * t + 8, :], 0.0)

    def child(k, carry):
        g, o = parents_ref[0, k], octant_ref[0, k]
        for c in range(3):
            re, im = inc_ref[g * 6 + c], inc_ref[g * 6 + 3 + c]
            fr, fi = phase_ref[o * 6 + c], phase_ref[o * 6 + 3 + c]
            r_ref[k * 2, :, 128 * c : 128 * c + 128] = re * fr + im * fi
            r_ref[k * 2 + 1, :, 128 * c : 128 * c + 128] = im * fr - re * fi
        return carry

    lax.fori_loop(0, KIDS, child, 0, unroll=4)

    def to_child(r):
        hi, lo = split(r)
        return (
            dot3((hi[:, :256], lo[:, :256]), (right2_ref[0, 0], right2_ref[1, 0])),
            dot3((hi[:, 128:], lo[:, 128:]), (right2_ref[0, 1], right2_ref[1, 1])),
        )

    v_ref[0], v_ref[1] = to_child(r_ref[...].reshape(768, 384))
    for n in range(6):
        at = slice(128 * n, 128 * n + 128)
        out_ref[at, :] = dot2(left2_ref[...], split(jnp.concatenate([v_ref[0, at, :], v_ref[1, at, :]], axis=0)))
    hot_parent, hot_octant = one_hot(parent_ref[...], 8), one_hot(octants_ref[...], 8)
    shifts = [pick(hot_octant, [edge_ref[e, t] for t in range(6)]) for e in range(2)]
    for copy in (forward, backward, *gather_a, *reduces, *urgent, *others):
        copy.wait_send()
    for r in (1, 2, 3):
        b_wait(r, True)
    last_near.wait()
    last_far.wait()
    rows = []
    for e in range(2):
        values = pick(hot_parent, [halo_ref[3 - e, pl.ds(t, 8, stride=6), :] for t in range(6)])
        re, im, fr, fi = values[:, :384], values[:, 384:], shifts[e][:, :384], shifts[e][:, 384:]
        rows += [re * fr + im * fi, im * fr - re * fi]
    even_part, odd_part = to_child(jnp.concatenate(rows, axis=0))
    weight_even, weight_odd = azimuth_rows(EVEN), azimuth_rows(ODD)
    for e, s in enumerate((0, 7)):
        for a in range(2):
            at = (2 * e + a) * KIDS
            for i in range(8):
                we, wo = float(weight_even[s, i]), float(weight_odd[s, i])
                if we or wo:
                    place = pl.ds(a * 8 + i, KIDS, stride=16)
                    out_ref[place, :] = out_ref[place, :] + (
                        we * even_part[at : at + KIDS] + wo * odd_part[at : at + KIDS]
                    )


VMEM_SPEC = pl.BlockSpec(memory_space=pltpu.VMEM)
HBM_SPEC = pl.BlockSpec(memory_space=pltpu.HBM)
LIMIT = 63 * 2**20


def f32(*shape):
    return jax.ShapeDtypeStruct(shape, jnp.float32)


def on_device(child, table, child_parent, child_octant, partner_src, partner_off, partner_count):
    up_left, up_right, down_right, down_left, phases = (jnp.asarray(a) for a in constants())
    vm = functools.partial(pltpu.VMEM, dtype=jnp.float32)
    ints = functools.partial(pltpu.VMEM, dtype=jnp.int32)
    bf16 = functools.partial(pltpu.VMEM, dtype=jnp.bfloat16)
    scalars = functools.partial(pltpu.SMEM, dtype=jnp.int32)
    out = pl.pallas_call(
        middle_kernel,
        out_shape=f32(KIDS * 16, 128),
        in_specs=[HBM_SPEC] * 12,
        out_specs=VMEM_SPEC,
        scratch_shapes=[
            ints((1, KIDS)), ints((1, KIDS)), scalars((1, KIDS)), scalars((1, KIDS)), vm((KIDS, 2, 8, 128)),
            ints((56, 128)), ints((56, 128)), ints((1, 128)), bf16((OFFSETS + 1, 2, 2304)), bf16((256, 128)),
            bf16((2, 256, 384)), vm((144, 128)), bf16((2, 2, 256, 128)), bf16((128, 256)), vm((2, 6, 8, 128)),
            ints((32, 128)), scalars((32, 128)), ints((8, 128)), scalars((8, 128)),
            bf16((2, 768, 256)), vm((2 * KIDS + 2, 8, 384)), vm((48, 8, 128)), vm((8 * TILES, 128)), vm((TILES, 8, 128)),
            vm((2 * KIDS, 8, 384)), vm((2, 768, 128)), vm((4, TILES, 128)), vm((4, TILES, 128)),
            *[vm((32, 2, HALF))] * 4, *[vm((32, 2, 2, HALF))] * 2, *[vm((32, 2, HALF))] * 2,
            vm((3, 8, 2, HALF)), vm((3, 32, 2, 384)), vm((3, 8, 2, 384)), vm((3, 2, 8, 2, 384)), vm((3, 8, 2, 384)),
            vm((8, 2, HALF)),
            pltpu.SemaphoreType.DMA((14,)), pltpu.SemaphoreType.DMA((22,)), pltpu.SemaphoreType.DMA((22,)),
        ],
        compiler_params=pltpu.CompilerParams(collective_id=0, has_side_effects=True, vmem_limit_bytes=LIMIT),
        name="middle",
    )(
        child_parent, child_octant.reshape(1, KIDS), child, partner_src.T, partner_off.T, partner_count.reshape(1, 128),
        table, up_left, up_right, phases, down_right, down_left,
    )
    return out.reshape(KIDS, 2, 8, 128)


def solution(mesh):
    return jax.shard_map(
        on_device,
        mesh=mesh,
        in_specs=(P("clus", None, "dir", None), P(None, None, "dir"), P("clus", None), P("clus"), P(), P(), P()),
        out_specs=P("clus", None, "dir", None),
        check_vma=False,
    )
```

```python
import functools
import math

import jax
import jax.numpy as jnp
import ml_dtypes
import numpy as np
from jax import lax
from jax.experimental import pallas as pl
from jax.experimental.pallas import tpu as pltpu
from jax.sharding import PartitionSpec as P

NT_C, NP_C, NT_P, NP_P = 128, 256, 192, 384
OFFSETS = 316
N_CLUS, N_DIR = 16, 32
PAR, KIDS = 8, 48
TILES = PAR * 6
MESH = pl.DeviceIdType.MESH
EVEN = np.array([-2, 0, 2, 4, 6, 8, 10, 14])
ODD = np.array([-1, 1, 3, 5, 7, 9, 11, 13])


def lagrange(t):
    out = []
    for m in range(5):
        w = np.ones_like(t)
        for n in range(5):
            if n != m:
                w = w * (t - n) / (m - n)
        out.append(w)
    return out


def polar_matrix():
    x = (np.arange(NT_P) + 0.5) * NT_C / NT_P - 0.5
    s = np.clip(np.floor(x + 0.5).astype(int) - 2, 0, NT_C - 5)
    w = lagrange(x - s)
    m = np.zeros((NT_P, NT_C))
    for k in range(5):
        m[np.arange(NT_P), s + k] = w[k]
    return m


SCALE = 243


def azimuth_rows(rows):
    x = rows * NP_C / NP_P
    b = np.floor(x + 0.5).astype(int)
    w = lagrange(x - b + 2)
    m = np.zeros((len(rows), 8))
    for k in range(5):
        for j in range(len(rows)):
            i = b[j] + k - 2
            if 0 <= i < 8:
                m[j, i] = w[k][j] * SCALE
    return np.round(m)


def halves(a):
    a = a.astype(np.float32)
    hi = a.astype(ml_dtypes.bfloat16)
    lo = (a - hi.astype(np.float32)).astype(ml_dtypes.bfloat16)
    return np.stack([hi, lo])


def in_tiles(even, odd):
    return np.stack([even[:, :128], np.concatenate([even[:, 128:], odd[:, :64]], 1), odd[:, 64:]])


@functools.cache
def constants():
    p = polar_matrix()
    ae, ao = azimuth_rows(EVEN), azimuth_rows(ODD)
    eye = np.eye(16)
    up_left = np.concatenate([np.kron(eye, ae), np.kron(eye, ao)], 0).astype(ml_dtypes.bfloat16)
    w = np.zeros((256, 384))
    w[:128, :192] = p.T
    w[128:, 192:] = p.T
    w = w / SCALE
    up_right = halves(w)
    down_right = halves(np.stack([w[:128, :256].T, w[128:, 128:].T]))
    down_left = np.concatenate([np.kron(eye, ae.T), np.kron(eye, ao.T)], 1).astype(ml_dtypes.bfloat16)
    theta = math.pi * (np.arange(NT_P) + 0.5) / NT_P
    phases = np.zeros((N_DIR, 3, 2, 3, 8, 128))
    for d in range(N_DIR):
        angle = []
        for rows in (EVEN, ODD):
            phi = 2 * math.pi * ((12 * d + rows) % NP_P) / NP_P
            angle.append(
                8 * math.pi
                * np.stack(
                    [
                        np.sin(theta) * np.cos(phi)[:, None],
                        np.sin(theta) * np.sin(phi)[:, None],
                        np.cos(theta) * np.ones((8, 1)),
                    ]
                )
            )
        for k in range(3):
            t = in_tiles(angle[0][k], angle[1][k])
            phases[d, k] = np.stack([np.cos(t), np.sin(t)])
    return up_left, up_right, down_right, down_left, phases.reshape(N_DIR, 144, 128).astype(np.float32)


def split(x):
    hi = x.astype(jnp.bfloat16)
    return hi, (x - hi.astype(jnp.float32)).astype(jnp.bfloat16)


def dot3(a, b):
    f = functools.partial(jnp.dot, preferred_element_type=jnp.float32)
    return f(a[0], b[0]) + (f(a[1], b[0]) + f(a[0], b[1]))


def dot2(a, b):
    f = functools.partial(jnp.dot, preferred_element_type=jnp.float32)
    return f(a, b[0]) + f(a, b[1])


def position():
    clus, direction = lax.axis_index("clus"), lax.axis_index("dir")
    core = lax.rem(direction, 2)
    x, z = lax.rem(clus, 4), lax.div(clus, 4)
    return clus, direction, core, x, z


def gather_member(core, x, z, k):
    return (1 - core) * (z * 4 + k) + core * (k * 4 + x)


def reduce_member(core, x, z, k):
    return (1 - core) * (k * 4 + x) + core * (z * 4 + k)


def octant_tables(base, table, edge):
    def tile(k, a, c):
        r = (k * 6 + a * 3 + c) * 8
        return base[r : r + 8, :]

    for c in range(3):
        ar, ai, br, bi, cr, ci = (tile(k, a, c) for k in range(3) for a in range(2))
        rr, ii, ri, ir = ar * br, ai * bi, ar * bi, ai * br
        for sx, sy, re, im in ((1, 1, rr - ii, ri + ir), (1, -1, rr + ii, ir - ri)):
            pr, pi, qr, qi = re * cr, im * ci, re * ci, im * cr
            for sz, fr, fi in ((1, pr - pi, qr + qi), (-1, pr + pi, qi - qr)):
                for sign in (1, -1):
                    o = (sx * sign < 0) + 2 * (sy * sign < 0) + 4 * (sz * sign < 0)
                    for t, f in ((c, fr), (3 + c, fi if sign > 0 else -fi)):
                        table[o * 6 + t] = f
                        edge[0, t, o : o + 1, :] = f[0:1]
                        edge[1, t, o : o + 1, :] = f[7:8]


def aligned(i, n=8):
    return pl.multiple_of(i, n)


def build_kids(parent_ref, kids_ref):
    parent = lax.broadcasted_iota(jnp.int32, (8, KIDS), 0)
    start = jnp.sum((parent_ref[...] < parent).astype(jnp.int32), axis=1, keepdims=True)
    number = jnp.sum((parent_ref[...] == parent).astype(jnp.int32), axis=1, keepdims=True)
    lane = lax.broadcasted_iota(jnp.int32, (8, 128), 1)
    own = jnp.where(lane < number, start + lane, KIDS)
    kids_ref[...] = jnp.where(lane < 8, own, jnp.minimum(start + lane - 8, KIDS - 1))


def build_index(src_ref, off_ref, count_ref, key_ref):
    clus, direction, core, x, z = position()
    src = src_ref[...]
    off = off_ref[...]
    slot = lax.broadcasted_iota(jnp.int32, src.shape, 0)
    own_x, own_z = (src >> 3) & 3, src >> 5
    here = jnp.where(core == 0, own_z, own_x) == jnp.where(core == 0, z, x)
    local = jnp.where(core == 0, own_x, own_z) * 8 + (src & 7)
    local = jnp.where(here & (slot < count_ref[...]), local, -1)
    which = lax.broadcasted_iota(jnp.int32, (32, 128), 0)
    key = jnp.full((32, 128), OFFSETS, jnp.int32)
    for p in range(src.shape[0]):
        key = jnp.where(which == local[p : p + 1], off[p : p + 1], key)
    key_ref[...] = key


def one_hot(row, n):
    square = (KIDS, KIDS)
    diagonal = lax.broadcasted_iota(jnp.int32, square, 0) == lax.broadcasted_iota(jnp.int32, square, 1)
    column = jnp.sum(jnp.where(diagonal, row, 0), axis=1, keepdims=True)
    hot = column == lax.broadcasted_iota(jnp.int32, (KIDS, n), 1)
    return jnp.where(hot, 1.0, 0.0).astype(jnp.bfloat16)


def pick(hot, tiles):
    return dot2(hot, split(jnp.concatenate(tiles, axis=1)))


def even_lanes():
    column = lax.rem(lax.broadcasted_iota(jnp.int32, (TILES, 128), 0), 3)
    lane = lax.broadcasted_iota(jnp.int32, (TILES, 128), 1)
    return (column == 0) | ((column == 1) & (lane < 64))


PAIRS = ((2, 3, 4), (0, 1, 5))
PIECES = (((768, 0, 1152),), ((0, 0, 768), (1920, 768, 384)))
HALF = 1152


def relay(tile_ref, s_ref, part, first, places=(0, 1, 2)):
    def parent(g, carry):
        for n, q in ((n, PAIRS[part][n]) for n in places):
            for c in range(3):
                lanes = slice(128 * (3 * n + c), 128 * (3 * n + c) + 128)
                s_ref[first + g, :, lanes] = tile_ref[pl.ds((g * 6 + c) * 8 + q + 1, 2, stride=24), :]
        return carry

    lax.fori_loop(0, PAR, parent, 0)


def unrelay(sum_ref, tile_ref, part):
    def parent(g, carry):
        for n, q in enumerate(PAIRS[part]):
            for c in range(3):
                lanes = slice(128 * (3 * n + c), 128 * (3 * n + c) + 128)
                tile_ref[pl.ds((g * 6 + c) * 8 + q + 1, 2, stride=24), :] = sum_ref[g, :, lanes]
        return carry

    lax.fori_loop(0, PAR, parent, 0)


def swap(s_ref, x_ref, block):
    def source(i, carry):
        at = block * 8 + i
        x_ref[at, 0:1, :] = s_ref[at, 1:2, :]
        x_ref[at, 1:2, :] = s_ref[at, 0:1, :]
        return carry

    lax.fori_loop(0, PAR, source, 0, unroll=2)


GROUP = 4


def add_pairs(part, key_ref, table_ref, s_ref, x_ref, block, first_target, acc):
    acc = [list(a) for a in acc]
    pieces = PIECES[part]
    for u in range(PAR):
        source = block * 8 + u
        for p, (at, to, n) in enumerate(pieces):
            s = s_ref[source, :, to : to + n]
            x = x_ref[source, :, to : to + n]
            for j in range(GROUP):
                t = table_ref[key_ref[source, first_target + j], :, at : at + n].astype(jnp.float32)
                acc[j][p] = acc[j][p] + t * s
                acc[j][len(pieces) + p] = acc[j][len(pieces) + p] + t * x
    return tuple(tuple(a) for a in acc)


def middle_kernel(
    parent_hbm, octant_hbm, child_hbm, src_hbm, off_hbm, count_hbm, table_hbm, left_hbm, right_hbm, phases_hbm,
    right2_hbm, left2_hbm,
    out_ref,
    parent_ref, octants_ref, parents_ref, octant_ref, child_ref, src_ref, off_ref, count_ref, table_ref, left_ref,
    right_ref, base_ref, right2_ref, left2_ref, edge_ref,
    key_ref, index_ref, kids_ref, kid_ref, y_ref, z_ref, phase_ref, tile_ref, inc_ref, r_ref, v_ref, pack_ref, halo_ref,
    sa_ref, sb_ref, xa_ref, xb_ref, acca_ref, accb_ref, pa_ref, pb_ref, gota_ref, pu_ref, gotu_ref, goto_ref, su_ref, sum_ref,
    local_sem, send_sem, recv_sem,
):
    clus, direction, core, x, z = position()
    after = (clus, lax.rem(direction + 1, N_DIR))
    before = (clus, lax.rem(direction + N_DIR - 1, N_DIR))
    source_me = (1 - core) * x + core * z
    target_me = (1 - core) * z + core * x
    source_blocks, target_blocks = (
        [me, 3 - me, lax.rem(me + 2, 4), me + 1 - 2 * lax.rem(me, 2)] for me in (source_me, target_me)
    )
    source_peers = [(gather_member(core, x, z, k), direction) for k in source_blocks[1:]]
    target_peers = [(reduce_member(core, x, z, k), direction) for k in target_blocks[1:]]
    barrier = pltpu.get_barrier_semaphore()
    peers = [after, before, *source_peers, *target_peers]
    for peer in peers:
        pl.semaphore_signal(barrier, inc=1, device_id=peer, device_id_type=MESH)

    def fetch(n, src, dst):
        copy = pltpu.make_async_copy(src, dst, local_sem.at[n])
        copy.start()
        return copy

    parents = fetch(0, parent_hbm, parent_ref)
    first = [
        fetch(1, left_hbm, left_ref),
        fetch(2, child_hbm, child_ref),
        fetch(3, right_hbm, right_ref),
        fetch(4, phases_hbm.at[direction], base_ref),
        fetch(5, src_hbm, src_ref),
        fetch(6, off_hbm, off_ref),
        fetch(7, count_hbm, count_ref),
    ]
    second = [
        fetch(8, octant_hbm, octant_ref),
        fetch(9, parent_hbm, parents_ref),
        fetch(10, octant_hbm, octants_ref),
    ]
    z_ref[2 * KIDS : 2 * KIDS + 2] = jnp.zeros((2, 8, 384), jnp.float32)
    table_ref[OFFSETS] = jnp.zeros((2, 2304), jnp.bfloat16)
    parents.wait()
    build_kids(parent_ref, kids_ref)
    kids = fetch(0, kids_ref, kid_ref)
    for copy in first:
        copy.wait()
    third = [
        fetch(11, table_hbm, table_ref.at[pl.ds(0, OFFSETS)]),
        fetch(12, right2_hbm, right2_ref),
        fetch(13, left2_hbm, left2_ref),
    ]
    build_index(src_ref, off_ref, count_ref, key_ref)
    for n in range(6):
        xs = split(child_ref[8 * n : 8 * n + 8].reshape(128, 128))
        eo = dot2(left_ref[...], xs)
        y = split(jnp.concatenate([eo[:128], eo[128:]], axis=1))
        for h in range(2):
            y_ref[h, 128 * n : 128 * n + 128, :] = y[h]
    z_ref[0 : 2 * KIDS] = dot3((y_ref[0], y_ref[1]), (right_ref[0], right_ref[1])).reshape(2 * KIDS, 8, 384)
    octant_tables(base_ref, phase_ref, edge_ref)
    index = fetch(1, key_ref, index_ref)
    kids.wait()
    for copy in second:
        copy.wait()

    def parent(g, carry):
        acc = [jnp.zeros((8, 128), jnp.float32) for _ in range(6)]
        for m in range(8):
            k = kid_ref[g, m]
            o = octant_ref[0, kid_ref[g, 8 + m]]
            for c in range(3):
                re = z_ref[k * 2, :, 128 * c : 128 * c + 128]
                im = z_ref[k * 2 + 1, :, 128 * c : 128 * c + 128]
                fr = phase_ref[o * 6 + c]
                fi = phase_ref[o * 6 + 3 + c]
                acc[c] = acc[c] + (re * fr - im * fi)
                acc[3 + c] = acc[3 + c] + (re * fi + im * fr)
        for t in range(6):
            tile_ref[pl.ds(aligned((g * 6 + t) * 8), 8), :] = acc[t]
        return carry

    lax.fori_loop(0, PAR, parent, 0)

    pl.semaphore_wait(barrier, len(peers))

    def send(n, src, dst, peer):
        copy = pltpu.make_async_remote_copy(
            src, dst, send_sem.at[n], recv_sem.at[n], device_id=peer, device_id_type=MESH
        )
        copy.start()
        return copy

    pack_ref[0] = tile_ref[pl.ds(7, TILES, stride=8), :]
    forward = send(0, pack_ref.at[0], halo_ref.at[0], after)
    pack_ref[1] = tile_ref[pl.ds(0, TILES, stride=8), :]
    backward = send(1, pack_ref.at[1], halo_ref.at[1], before)
    own = source_me * 8
    relay(tile_ref, sa_ref, 0, own)
    block_a = sa_ref.at[pl.ds(own, 8)]
    gather_a = [send(2 + r, block_a, block_a, peer) for r, peer in enumerate(source_peers)]
    swap(sa_ref, xa_ref, source_me)
    for copy in (index, *third):
        copy.wait()

    parts = ((sa_ref, xa_ref, acca_ref, pa_ref), (sb_ref, xb_ref, accb_ref, pb_ref))

    def own_pass(part):
        s_ref, x_ref, acc_ref, _ = parts[part]
        k = len(PIECES[part])

        def group(i, carry):
            j, g = lax.div(i, 2), lax.rem(i, 2) * GROUP
            zero = tuple(jnp.zeros((2, n), jnp.float32) for _ in range(2) for _, _, n in PIECES[part])
            acc = add_pairs(
                part, index_ref, table_ref, s_ref, x_ref, source_me, reduce_member(core, x, z, j) * 8 + g, (zero,) * GROUP
            )
            for t in range(GROUP):
                for p, (_, to, n) in enumerate(PIECES[part]):
                    acc_ref[j * 8 + g + t, 0, :, to : to + n] = acc[t][p]
                    acc_ref[j * 8 + g + t, 1, :, to : to + n] = acc[t][k + p]
            return carry

        lax.fori_loop(0, 32 // GROUP, group, 0)

    def load(part, target):
        acc_ref = parts[part][2]
        return tuple(
            tuple(acc_ref[target + t, h, :, to : to + n] for h in range(2) for _, to, n in PIECES[part])
            for t in range(GROUP)
        )

    def block_pass(part, block):
        s_ref, x_ref, acc_ref, _ = parts[part]
        k = len(PIECES[part])

        def group(i, carry):
            j, g = lax.div(i, 2), lax.rem(i, 2) * GROUP
            acc = add_pairs(
                part, index_ref, table_ref, s_ref, x_ref, block, reduce_member(core, x, z, j) * 8 + g, load(part, j * 8 + g)
            )
            for t in range(GROUP):
                for p, (_, to, n) in enumerate(PIECES[part]):
                    acc_ref[j * 8 + g + t, 0, :, to : to + n] = acc[t][p]
                    acc_ref[j * 8 + g + t, 1, :, to : to + n] = acc[t][k + p]
            return carry

        lax.fori_loop(0, 32 // GROUP, group, 0)

    def last_pass(part, j, blocks):
        s_ref, x_ref, _, p_ref = parts[part]
        k = len(PIECES[part])

        def group(i, carry):
            g = i * GROUP
            acc = load(part, j * 8 + g)
            for block in blocks:
                acc = add_pairs(
                    part, index_ref, table_ref, s_ref, x_ref, block, reduce_member(core, x, z, j) * 8 + g, acc
                )
            for t in range(GROUP):
                for p, (_, to, n) in enumerate(PIECES[part]):
                    a, b = acc[t][p], acc[t][k + p]
                    p_ref[j * 8 + g + t, 0:1, to : to + n] = a[0:1] - a[1:2]
                    p_ref[j * 8 + g + t, 1:2, to : to + n] = b[0:1] + b[1:2]
            return carry

        lax.fori_loop(0, PAR // GROUP, group, 0)

    even = even_lanes()
    at1, at2, at6 = (pl.ds(pair, TILES, stride=8) for pair in (1, 2, 6))

    def from_before():
        forward.wait_recv()
        got = halo_ref[0]
        tile_ref[at1, :] = tile_ref[at1, :] + jnp.where(even, 0.0, got)
        tile_ref[at2, :] = tile_ref[at2, :] + jnp.where(even, got, 0.0)
        relay(tile_ref, sb_ref, 1, own, (0, 1))

    def from_after():
        backward.wait_recv()
        tile_ref[at6, :] = tile_ref[at6, :] + halo_ref[1]
        relay(tile_ref, sb_ref, 1, own, (2,))

    def b_copy(first, lanes, late, r):
        n = (19 if late else 5) + r - 1
        block = sb_ref.at[pl.ds(own, 8), :, pl.ds(first, lanes)]
        return pltpu.make_async_remote_copy(
            block, block, send_sem.at[n], recv_sem.at[n], device_id=source_peers[r - 1], device_id_type=MESH
        )

    def b_wait(r, send_side):
        for c in range(2):

            @pl.when(core == c)
            def _():
                for first, lanes, late in ((0, 768, c == 0), (768, 384, c == 1)):
                    copy = b_copy(first, lanes, late, r)
                    if send_side:
                        copy.wait_send()
                    else:
                        copy.wait_recv()

    for late in (False, True):

        @pl.when(core == int(late))
        def _(late=late):
            from_after()
            for r in (1, 2, 3):
                b_copy(768, 384, late, r).start()

        @pl.when(core == 1 - int(late))
        def _(late=late):
            from_before()
            for r in (1, 2, 3):
                b_copy(0, 768, late, r).start()

        if not late:
            own_pass(0)
    swap(sb_ref, xb_ref, source_me)
    own_pass(1)

    def gathered(part, r):
        if part == 0:
            gather_a[r - 1].wait_recv()
        else:
            b_wait(r, False)
        swap(parts[part][0], parts[part][1], source_blocks[r])

    def reduce_to(part, r, got_ref):
        block = parts[part][3].at[pl.ds(target_blocks[r] * 8, 8)]
        return send(8 + 3 * part + r - 1, block, got_ref.at[r - 1], target_peers[r - 1])

    for r in (3, 2):
        gathered(1, r)
        block_pass(1, source_blocks[r])
    gathered(1, 1)
    low = lax.broadcasted_iota(jnp.int32, (2, 128), 1) < 64
    for_before, for_after = 2 * core, 2 - 2 * core

    def pack(j):
        def parent(g, carry):
            t = j * 8 + g
            p = [pb_ref[t, :, 128 * n : 128 * n + 128] for n in range(9)]
            chunks = (
                (for_before, (p[3], jnp.where(low, p[4], p[1]), p[2])),
                (1, (p[0], jnp.where(low, p[1], p[4]), p[5])),
                (for_after, p[6:9]),
            )
            for chunk, tiles in chunks:
                for c in range(3):
                    pu_ref[chunk, t, :, 128 * c : 128 * c + 128] = tiles[c]
            return carry

        lax.fori_loop(0, PAR, parent, 0, unroll=2)

    urgent = []
    for r in (1, 2, 3):
        last_pass(1, target_blocks[r], source_blocks[1:2])
        pack(target_blocks[r])
        chunk = pu_ref.at[0, pl.ds(target_blocks[r] * 8, 8)]
        urgent.append(send(10 + r, chunk, gotu_ref.at[r - 1], target_peers[r - 1]))
    others = []
    for r in (1, 2, 3):
        chunks = pu_ref.at[pl.ds(1, 2), pl.ds(target_blocks[r] * 8, 8)]
        others.append(send(15 + r, chunks, goto_ref.at[r - 1], target_peers[r - 1]))
    for r in (3, 2, 1):
        gathered(0, r)
    reduces = []
    for r in (1, 2, 3):
        last_pass(0, target_blocks[r], source_blocks[1:])
        reduces.append(reduce_to(0, r, gota_ref))
    last_pass(1, target_blocks[0], source_blocks[1:2])
    pack(target_blocks[0])

    def to_rows(chunk, slot):
        def parent(g, carry):
            for c in range(3):
                pack_ref[slot, pl.ds(g * 6 + c, 2, stride=3), :] = su_ref[chunk, g, :, 128 * c : 128 * c + 128]
            return carry

        lax.fori_loop(0, PAR, parent, 0, unroll=2)

    for copy in urgent:
        copy.wait_recv()

    def first_total(g, carry):
        su_ref[0, g] = (pu_ref[0, target_me * 8 + g] + gotu_ref[0, g]) + (gotu_ref[1, g] + gotu_ref[2, g])
        return carry

    lax.fori_loop(0, PAR, first_total, 0, unroll=2)
    to_rows(0, 2)
    far = (clus, lax.rem(direction + N_DIR - 1 + 2 * core, N_DIR))
    near = (clus, direction + 1 - 2 * core)
    last_far = send(14, pack_ref.at[2], halo_ref.at[2 + core], far)
    last_pass(0, target_blocks[0], source_blocks[1:])
    for copy in others:
        copy.wait_recv()

    def other_totals(g, carry):
        for n in range(2):
            own_sum = pu_ref[1 + n, target_me * 8 + g]
            su_ref[1 + n, g] = (own_sum + goto_ref[0, n, g]) + (goto_ref[1, n, g] + goto_ref[2, n, g])
        return carry

    lax.fori_loop(0, PAR, other_totals, 0, unroll=2)
    to_rows(2, 3)
    last_near = send(15, pack_ref.at[3], halo_ref.at[3 - core], near)

    def unpack(g, carry):
        f, rest, last = (
            [su_ref[chunk, g, :, 128 * c : 128 * c + 128] for c in range(3)] for chunk in (for_before, 1, for_after)
        )
        pairs = (
            (0, (rest[0], jnp.where(low, rest[1], f[1]), f[2])),
            (1, (f[0], jnp.where(low, f[1], rest[1]), rest[2])),
            (5, last),
        )
        for q, tiles in pairs:
            for c in range(3):
                tile_ref[pl.ds((g * 6 + c) * 8 + q + 1, 2, stride=24), :] = tiles[c]
        return carry

    lax.fori_loop(0, PAR, unpack, 0)
    for copy in reduces:
        copy.wait_recv()

    def last_total(g, carry):
        sum_ref[g] = (pa_ref[target_me * 8 + g] + gota_ref[0, g]) + (gota_ref[1, g] + gota_ref[2, g])
        return carry

    lax.fori_loop(0, PAR, last_total, 0, unroll=2)
    unrelay(sum_ref, tile_ref, 0)
    pair = lax.broadcasted_iota(jnp.int32, (8, 128), 0)
    inside = (pair > 0) & (pair < 7)
    for t in range(TILES):
        inc_ref[t] = jnp.where(inside, tile_ref[8 * t : 8 * t + 8, :], 0.0)

    def child(k, carry):
        g, o = parents_ref[0, k], octant_ref[0, k]
        for c in range(3):
            re, im = inc_ref[g * 6 + c], inc_ref[g * 6 + 3 + c]
            fr, fi = phase_ref[o * 6 + c], phase_ref[o * 6 + 3 + c]
            r_ref[k * 2, :, 128 * c : 128 * c + 128] = re * fr + im * fi
            r_ref[k * 2 + 1, :, 128 * c : 128 * c + 128] = im * fr - re * fi
        return carry

    lax.fori_loop(0, KIDS, child, 0, unroll=4)

    def to_child(r):
        hi, lo = split(r)
        return (
            dot3((hi[:, :256], lo[:, :256]), (right2_ref[0, 0], right2_ref[1, 0])),
            dot3((hi[:, 128:], lo[:, 128:]), (right2_ref[0, 1], right2_ref[1, 1])),
        )

    v_ref[0], v_ref[1] = to_child(r_ref[...].reshape(768, 384))
    for n in range(6):
        at = slice(128 * n, 128 * n + 128)
        out_ref[at, :] = dot2(left2_ref[...], split(jnp.concatenate([v_ref[0, at, :], v_ref[1, at, :]], axis=0)))
    hot_parent, hot_octant = one_hot(parent_ref[...], 8), one_hot(octants_ref[...], 8)
    shifts = [pick(hot_octant, [edge_ref[e, t] for t in range(6)]) for e in range(2)]
    for copy in (forward, backward, *gather_a, *reduces, *urgent, *others):
        copy.wait_send()
    for r in (1, 2, 3):
        b_wait(r, True)
    last_near.wait()
    last_far.wait()
    rows = []
    for e in range(2):
        values = pick(hot_parent, [halo_ref[3 - e, pl.ds(t, 8, stride=6), :] for t in range(6)])
        re, im, fr, fi = values[:, :384], values[:, 384:], shifts[e][:, :384], shifts[e][:, 384:]
        rows += [re * fr + im * fi, im * fr - re * fi]
    even_part, odd_part = to_child(jnp.concatenate(rows, axis=0))
    weight_even, weight_odd = azimuth_rows(EVEN), azimuth_rows(ODD)
    for e, s in enumerate((0, 7)):
        for a in range(2):
            at = (2 * e + a) * KIDS
            for i in range(8):
                we, wo = float(weight_even[s, i]), float(weight_odd[s, i])
                if we or wo:
                    place = pl.ds(a * 8 + i, KIDS, stride=16)
                    out_ref[place, :] = out_ref[place, :] + (
                        we * even_part[at : at + KIDS] + wo * odd_part[at : at + KIDS]
                    )


VMEM_SPEC = pl.BlockSpec(memory_space=pltpu.VMEM)
HBM_SPEC = pl.BlockSpec(memory_space=pltpu.HBM)
LIMIT = 63 * 2**20


def f32(*shape):
    return jax.ShapeDtypeStruct(shape, jnp.float32)


def on_device(child, table, child_parent, child_octant, partner_src, partner_off, partner_count):
    up_left, up_right, down_right, down_left, phases = (jnp.asarray(a) for a in constants())
    vm = functools.partial(pltpu.VMEM, dtype=jnp.float32)
    ints = functools.partial(pltpu.VMEM, dtype=jnp.int32)
    bf16 = functools.partial(pltpu.VMEM, dtype=jnp.bfloat16)
    scalars = functools.partial(pltpu.SMEM, dtype=jnp.int32)
    out = pl.pallas_call(
        middle_kernel,
        out_shape=f32(KIDS * 16, 128),
        in_specs=[HBM_SPEC] * 12,
        out_specs=VMEM_SPEC,
        scratch_shapes=[
            ints((1, KIDS)), ints((1, KIDS)), scalars((1, KIDS)), scalars((1, KIDS)), vm((KIDS, 2, 8, 128)),
            ints((56, 128)), ints((56, 128)), ints((1, 128)), bf16((OFFSETS + 1, 2, 2304)), bf16((256, 128)),
            bf16((2, 256, 384)), vm((144, 128)), bf16((2, 2, 256, 128)), bf16((128, 256)), vm((2, 6, 8, 128)),
            ints((32, 128)), scalars((32, 128)), ints((8, 128)), scalars((8, 128)),
            bf16((2, 768, 256)), vm((2 * KIDS + 2, 8, 384)), vm((48, 8, 128)), vm((8 * TILES, 128)), vm((TILES, 8, 128)),
            vm((2 * KIDS, 8, 384)), vm((2, 768, 128)), vm((4, TILES, 128)), vm((4, TILES, 128)),
            *[vm((32, 2, HALF))] * 4, *[vm((32, 2, 2, HALF))] * 2, *[vm((32, 2, HALF))] * 2,
            vm((3, 8, 2, HALF)), vm((3, 32, 2, 384)), vm((3, 8, 2, 384)), vm((3, 2, 8, 2, 384)), vm((3, 8, 2, 384)),
            vm((8, 2, HALF)),
            pltpu.SemaphoreType.DMA((14,)), pltpu.SemaphoreType.DMA((22,)), pltpu.SemaphoreType.DMA((22,)),
        ],
        compiler_params=pltpu.CompilerParams(collective_id=0, has_side_effects=True, vmem_limit_bytes=LIMIT),
        name="middle",
    )(
        child_parent, child_octant.reshape(1, KIDS), child, partner_src.T, partner_off.T, partner_count.reshape(1, 128),
        table, up_left, up_right, phases, down_right, down_left,
    )
    return out.reshape(KIDS, 2, 8, 128)


def solution(mesh):
    return jax.shard_map(
        on_device,
        mesh=mesh,
        in_specs=(P("clus", None, "dir", None), P(None, None, "dir"), P("clus", None), P("clus"), P(), P(), P()),
        out_specs=P("clus", None, "dir", None),
        check_vma=False,
    )
```

```python
import functools
import math

import jax
import jax.numpy as jnp
import ml_dtypes
import numpy as np
from jax import lax
from jax.experimental import pallas as pl
from jax.experimental.pallas import tpu as pltpu
from jax.sharding import PartitionSpec as P

NT_C, NP_C, NT_P, NP_P = 128, 256, 192, 384
OFFSETS = 316
N_CLUS, N_DIR = 16, 32
PAR, KIDS = 8, 48
TILES = PAR * 6
MESH = pl.DeviceIdType.MESH
EVEN = np.array([-2, 0, 2, 4, 6, 8, 10, 14])
ODD = np.array([-1, 1, 3, 5, 7, 9, 11, 13])


def lagrange(t):
    out = []
    for m in range(5):
        w = np.ones_like(t)
        for n in range(5):
            if n != m:
                w = w * (t - n) / (m - n)
        out.append(w)
    return out


def polar_matrix():
    x = (np.arange(NT_P) + 0.5) * NT_C / NT_P - 0.5
    s = np.clip(np.floor(x + 0.5).astype(int) - 2, 0, NT_C - 5)
    w = lagrange(x - s)
    m = np.zeros((NT_P, NT_C))
    for k in range(5):
        m[np.arange(NT_P), s + k] = w[k]
    return m


SCALE = 243


def azimuth_rows(rows):
    x = rows * NP_C / NP_P
    b = np.floor(x + 0.5).astype(int)
    w = lagrange(x - b + 2)
    m = np.zeros((len(rows), 8))
    for k in range(5):
        for j in range(len(rows)):
            i = b[j] + k - 2
            if 0 <= i < 8:
                m[j, i] = w[k][j] * SCALE
    return np.round(m)


def halves(a):
    a = a.astype(np.float32)
    hi = a.astype(ml_dtypes.bfloat16)
    lo = (a - hi.astype(np.float32)).astype(ml_dtypes.bfloat16)
    return np.stack([hi, lo])


def in_tiles(even, odd):
    return np.stack([even[:, :128], np.concatenate([even[:, 128:], odd[:, :64]], 1), odd[:, 64:]])


@functools.cache
def constants():
    p = polar_matrix()
    ae, ao = azimuth_rows(EVEN), azimuth_rows(ODD)
    eye = np.eye(16)
    up_left = np.concatenate([np.kron(eye, ae), np.kron(eye, ao)], 0).astype(ml_dtypes.bfloat16)
    w = np.zeros((256, 384))
    w[:128, :192] = p.T
    w[128:, 192:] = p.T
    w = w / SCALE
    up_right = halves(w)
    down_right = halves(np.stack([w[:128, :256].T, w[128:, 128:].T]))
    down_left = np.concatenate([np.kron(eye, ae.T), np.kron(eye, ao.T)], 1).astype(ml_dtypes.bfloat16)
    theta = math.pi * (np.arange(NT_P) + 0.5) / NT_P
    phases = np.zeros((N_DIR, 3, 2, 3, 8, 128))
    for d in range(N_DIR):
        angle = []
        for rows in (EVEN, ODD):
            phi = 2 * math.pi * ((12 * d + rows) % NP_P) / NP_P
            angle.append(
                8 * math.pi
                * np.stack(
                    [
                        np.sin(theta) * np.cos(phi)[:, None],
                        np.sin(theta) * np.sin(phi)[:, None],
                        np.cos(theta) * np.ones((8, 1)),
                    ]
                )
            )
        for k in range(3):
            t = in_tiles(angle[0][k], angle[1][k])
            phases[d, k] = np.stack([np.cos(t), np.sin(t)])
    return up_left, up_right, down_right, down_left, phases.reshape(N_DIR, 144, 128).astype(np.float32)


def split(x):
    hi = x.astype(jnp.bfloat16)
    return hi, (x - hi.astype(jnp.float32)).astype(jnp.bfloat16)


def dot3(a, b):
    f = functools.partial(jnp.dot, preferred_element_type=jnp.float32)
    return f(a[0], b[0]) + (f(a[1], b[0]) + f(a[0], b[1]))


def dot2(a, b):
    f = functools.partial(jnp.dot, preferred_element_type=jnp.float32)
    return f(a, b[0]) + f(a, b[1])


def position():
    clus, direction = lax.axis_index("clus"), lax.axis_index("dir")
    core = lax.rem(direction, 2)
    x, z = lax.rem(clus, 4), lax.div(clus, 4)
    return clus, direction, core, x, z


def gather_member(core, x, z, k):
    return (1 - core) * (z * 4 + k) + core * (k * 4 + x)


def reduce_member(core, x, z, k):
    return (1 - core) * (k * 4 + x) + core * (z * 4 + k)


def octant_tables(base, table, edge):
    def tile(k, a, c):
        r = (k * 6 + a * 3 + c) * 8
        return base[r : r + 8, :]

    for c in range(3):
        ar, ai, br, bi, cr, ci = (tile(k, a, c) for k in range(3) for a in range(2))
        rr, ii, ri, ir = ar * br, ai * bi, ar * bi, ai * br
        for sx, sy, re, im in ((1, 1, rr - ii, ri + ir), (1, -1, rr + ii, ir - ri)):
            pr, pi, qr, qi = re * cr, im * ci, re * ci, im * cr
            for sz, fr, fi in ((1, pr - pi, qr + qi), (-1, pr + pi, qi - qr)):
                for sign in (1, -1):
                    o = (sx * sign < 0) + 2 * (sy * sign < 0) + 4 * (sz * sign < 0)
                    for t, f in ((c, fr), (3 + c, fi if sign > 0 else -fi)):
                        table[o * 6 + t] = f
                        edge[0, t, o : o + 1, :] = f[0:1]
                        edge[1, t, o : o + 1, :] = f[7:8]


def aligned(i, n=8):
    return pl.multiple_of(i, n)


def build_kids(parent_ref, kids_ref):
    parent = lax.broadcasted_iota(jnp.int32, (8, KIDS), 0)
    start = jnp.sum((parent_ref[...] < parent).astype(jnp.int32), axis=1, keepdims=True)
    number = jnp.sum((parent_ref[...] == parent).astype(jnp.int32), axis=1, keepdims=True)
    lane = lax.broadcasted_iota(jnp.int32, (8, 128), 1)
    own = jnp.where(lane < number, start + lane, KIDS)
    kids_ref[...] = jnp.where(lane < 8, own, jnp.minimum(start + lane - 8, KIDS - 1))


def build_index(src_ref, off_ref, count_ref, key_ref):
    clus, direction, core, x, z = position()
    src = src_ref[...]
    off = off_ref[...]
    slot = lax.broadcasted_iota(jnp.int32, src.shape, 0)
    own_x, own_z = (src >> 3) & 3, src >> 5
    here = jnp.where(core == 0, own_z, own_x) == jnp.where(core == 0, z, x)
    local = jnp.where(core == 0, own_x, own_z) * 8 + (src & 7)
    local = jnp.where(here & (slot < count_ref[...]), local, -1)
    which = lax.broadcasted_iota(jnp.int32, (32, 128), 0)
    key = jnp.full((32, 128), OFFSETS, jnp.int32)
    for p in range(src.shape[0]):
        key = jnp.where(which == local[p : p + 1], off[p : p + 1], key)
    key_ref[...] = key


def one_hot(row, n):
    square = (KIDS, KIDS)
    diagonal = lax.broadcasted_iota(jnp.int32, square, 0) == lax.broadcasted_iota(jnp.int32, square, 1)
    column = jnp.sum(jnp.where(diagonal, row, 0), axis=1, keepdims=True)
    hot = column == lax.broadcasted_iota(jnp.int32, (KIDS, n), 1)
    return jnp.where(hot, 1.0, 0.0).astype(jnp.bfloat16)


def pick(hot, tiles):
    return dot2(hot, split(jnp.concatenate(tiles, axis=1)))


def even_lanes():
    column = lax.rem(lax.broadcasted_iota(jnp.int32, (TILES, 128), 0), 3)
    lane = lax.broadcasted_iota(jnp.int32, (TILES, 128), 1)
    return (column == 0) | ((column == 1) & (lane < 64))


PAIRS = ((2, 3, 4), (0, 1, 5))
PIECES = (((768, 0, 1152),), ((0, 0, 768), (1920, 768, 384)))
HALF = 1152


def relay(tile_ref, s_ref, part, first, places=(0, 1, 2)):
    def parent(g, carry):
        for n, q in ((n, PAIRS[part][n]) for n in places):
            for c in range(3):
                lanes = slice(128 * (3 * n + c), 128 * (3 * n + c) + 128)
                s_ref[first + g, :, lanes] = tile_ref[pl.ds((g * 6 + c) * 8 + q + 1, 2, stride=24), :]
        return carry

    lax.fori_loop(0, PAR, parent, 0)


def unrelay(sum_ref, tile_ref, part):
    def parent(g, carry):
        for n, q in enumerate(PAIRS[part]):
            for c in range(3):
                lanes = slice(128 * (3 * n + c), 128 * (3 * n + c) + 128)
                tile_ref[pl.ds((g * 6 + c) * 8 + q + 1, 2, stride=24), :] = sum_ref[g, :, lanes]
        return carry

    lax.fori_loop(0, PAR, parent, 0)


def swap(s_ref, x_ref, block):
    def source(i, carry):
        at = block * 8 + i
        x_ref[at, 0:1, :] = s_ref[at, 1:2, :]
        x_ref[at, 1:2, :] = s_ref[at, 0:1, :]
        return carry

    lax.fori_loop(0, PAR, source, 0, unroll=2)


GROUP = 4


def add_pairs(part, key_ref, table_ref, s_ref, x_ref, block, first_target, acc):
    acc = [list(a) for a in acc]
    pieces = PIECES[part]
    for u in range(PAR):
        source = block * 8 + u
        for p, (at, to, n) in enumerate(pieces):
            s = s_ref[source, :, to : to + n]
            x = x_ref[source, :, to : to + n]
            for j in range(GROUP):
                t = table_ref[key_ref[source, first_target + j], :, at : at + n].astype(jnp.float32)
                acc[j][p] = acc[j][p] + t * s
                acc[j][len(pieces) + p] = acc[j][len(pieces) + p] + t * x
    return tuple(tuple(a) for a in acc)


def middle_kernel(
    parent_hbm, octant_hbm, child_hbm, src_hbm, off_hbm, count_hbm, table_hbm, left_hbm, right_hbm, phases_hbm,
    right2_hbm, left2_hbm,
    out_ref,
    parent_ref, octants_ref, parents_ref, octant_ref, child_ref, src_ref, off_ref, count_ref, table_ref, left_ref,
    right_ref, base_ref, right2_ref, left2_ref, edge_ref,
    key_ref, index_ref, kids_ref, kid_ref, y_ref, z_ref, phase_ref, tile_ref, inc_ref, r_ref, v_ref, pack_ref, halo_ref,
    sa_ref, sb_ref, xa_ref, xb_ref, acca_ref, accb_ref, pa_ref, pb_ref, gota_ref, pu_ref, gotu_ref, goto_ref, su_ref, sum_ref,
    local_sem, send_sem, recv_sem,
):
    clus, direction, core, x, z = position()
    after = (clus, lax.rem(direction + 1, N_DIR))
    before = (clus, lax.rem(direction + N_DIR - 1, N_DIR))
    source_me = (1 - core) * x + core * z
    target_me = (1 - core) * z + core * x
    source_blocks, target_blocks = (
        [me, 3 - me, lax.rem(me + 2, 4), me + 1 - 2 * lax.rem(me, 2)] for me in (source_me, target_me)
    )
    source_peers = [(gather_member(core, x, z, k), direction) for k in source_blocks[1:]]
    target_peers = [(reduce_member(core, x, z, k), direction) for k in target_blocks[1:]]
    barrier = pltpu.get_barrier_semaphore()
    peers = [after, before, *source_peers, *target_peers]
    for peer in peers:
        pl.semaphore_signal(barrier, inc=1, device_id=peer, device_id_type=MESH)

    def fetch(n, src, dst):
        copy = pltpu.make_async_copy(src, dst, local_sem.at[n])
        copy.start()
        return copy

    parents = fetch(0, parent_hbm, parent_ref)
    first = [
        fetch(1, left_hbm, left_ref),
        fetch(2, child_hbm, child_ref),
        fetch(3, right_hbm, right_ref),
        fetch(4, phases_hbm.at[direction], base_ref),
        fetch(5, src_hbm, src_ref),
        fetch(6, off_hbm, off_ref),
        fetch(7, count_hbm, count_ref),
    ]
    second = [
        fetch(8, octant_hbm, octant_ref),
        fetch(9, parent_hbm, parents_ref),
        fetch(10, octant_hbm, octants_ref),
    ]
    z_ref[2 * KIDS : 2 * KIDS + 2] = jnp.zeros((2, 8, 384), jnp.float32)
    table_ref[OFFSETS] = jnp.zeros((2, 2304), jnp.bfloat16)
    parents.wait()
    build_kids(parent_ref, kids_ref)
    kids = fetch(0, kids_ref, kid_ref)
    for copy in first:
        copy.wait()
    third = [
        fetch(11, table_hbm, table_ref.at[pl.ds(0, OFFSETS)]),
        fetch(12, right2_hbm, right2_ref),
        fetch(13, left2_hbm, left2_ref),
    ]
    build_index(src_ref, off_ref, count_ref, key_ref)
    for n in range(6):
        xs = split(child_ref[8 * n : 8 * n + 8].reshape(128, 128))
        eo = dot2(left_ref[...], xs)
        y = split(jnp.concatenate([eo[:128], eo[128:]], axis=1))
        for h in range(2):
            y_ref[h, 128 * n : 128 * n + 128, :] = y[h]
    z_ref[0 : 2 * KIDS] = dot3((y_ref[0], y_ref[1]), (right_ref[0], right_ref[1])).reshape(2 * KIDS, 8, 384)
    octant_tables(base_ref, phase_ref, edge_ref)
    index = fetch(1, key_ref, index_ref)
    kids.wait()
    for copy in second:
        copy.wait()

    def parent(g, carry):
        acc = [jnp.zeros((8, 128), jnp.float32) for _ in range(6)]
        for m in range(8):
            k = kid_ref[g, m]
            o = octant_ref[0, kid_ref[g, 8 + m]]
            for c in range(3):
                re = z_ref[k * 2, :, 128 * c : 128 * c + 128]
                im = z_ref[k * 2 + 1, :, 128 * c : 128 * c + 128]
                fr = phase_ref[o * 6 + c]
                fi = phase_ref[o * 6 + 3 + c]
                acc[c] = acc[c] + (re * fr - im * fi)
                acc[3 + c] = acc[3 + c] + (re * fi + im * fr)
        for t in range(6):
            tile_ref[pl.ds(aligned((g * 6 + t) * 8), 8), :] = acc[t]
        return carry

    lax.fori_loop(0, PAR, parent, 0)

    pl.semaphore_wait(barrier, len(peers))

    def send(n, src, dst, peer):
        copy = pltpu.make_async_remote_copy(
            src, dst, send_sem.at[n], recv_sem.at[n], device_id=peer, device_id_type=MESH
        )
        copy.start()
        return copy

    pack_ref[0] = tile_ref[pl.ds(7, TILES, stride=8), :]
    forward = send(0, pack_ref.at[0], halo_ref.at[0], after)
    pack_ref[1] = tile_ref[pl.ds(0, TILES, stride=8), :]
    backward = send(1, pack_ref.at[1], halo_ref.at[1], before)
    own = source_me * 8
    relay(tile_ref, sa_ref, 0, own)
    block_a = sa_ref.at[pl.ds(own, 8)]
    gather_a = [send(2 + r, block_a, block_a, peer) for r, peer in enumerate(source_peers)]
    swap(sa_ref, xa_ref, source_me)
    for copy in (index, *third):
        copy.wait()

    parts = ((sa_ref, xa_ref, acca_ref, pa_ref), (sb_ref, xb_ref, accb_ref, pb_ref))

    def own_pass(part):
        s_ref, x_ref, acc_ref, _ = parts[part]
        k = len(PIECES[part])

        def group(i, carry):
            j, g = lax.div(i, 2), lax.rem(i, 2) * GROUP
            zero = tuple(jnp.zeros((2, n), jnp.float32) for _ in range(2) for _, _, n in PIECES[part])
            acc = add_pairs(
                part, index_ref, table_ref, s_ref, x_ref, source_me, reduce_member(core, x, z, j) * 8 + g, (zero,) * GROUP
            )
            for t in range(GROUP):
                for p, (_, to, n) in enumerate(PIECES[part]):
                    acc_ref[j * 8 + g + t, 0, :, to : to + n] = acc[t][p]
                    acc_ref[j * 8 + g + t, 1, :, to : to + n] = acc[t][k + p]
            return carry

        lax.fori_loop(0, 32 // GROUP, group, 0)

    def load(part, target):
        acc_ref = parts[part][2]
        return tuple(
            tuple(acc_ref[target + t, h, :, to : to + n] for h in range(2) for _, to, n in PIECES[part])
            for t in range(GROUP)
        )

    def block_pass(part, block):
        s_ref, x_ref, acc_ref, _ = parts[part]
        k = len(PIECES[part])

        def group(i, carry):
            j, g = lax.div(i, 2), lax.rem(i, 2) * GROUP
            acc = add_pairs(
                part, index_ref, table_ref, s_ref, x_ref, block, reduce_member(core, x, z, j) * 8 + g, load(part, j * 8 + g)
            )
            for t in range(GROUP):
                for p, (_, to, n) in enumerate(PIECES[part]):
                    acc_ref[j * 8 + g + t, 0, :, to : to + n] = acc[t][p]
                    acc_ref[j * 8 + g + t, 1, :, to : to + n] = acc[t][k + p]
            return carry

        lax.fori_loop(0, 32 // GROUP, group, 0)

    def last_pass(part, j, blocks):
        s_ref, x_ref, _, p_ref = parts[part]
        k = len(PIECES[part])

        def group(i, carry):
            g = i * GROUP
            acc = load(part, j * 8 + g)
            for block in blocks:
                acc = add_pairs(
                    part, index_ref, table_ref, s_ref, x_ref, block, reduce_member(core, x, z, j) * 8 + g, acc
                )
            for t in range(GROUP):
                for p, (_, to, n) in enumerate(PIECES[part]):
                    a, b = acc[t][p], acc[t][k + p]
                    p_ref[j * 8 + g + t, 0:1, to : to + n] = a[0:1] - a[1:2]
                    p_ref[j * 8 + g + t, 1:2, to : to + n] = b[0:1] + b[1:2]
            return carry

        lax.fori_loop(0, PAR // GROUP, group, 0)

    even = even_lanes()
    at1, at2, at6 = (pl.ds(pair, TILES, stride=8) for pair in (1, 2, 6))

    def from_before():
        forward.wait_recv()
        got = halo_ref[0]
        tile_ref[at1, :] = tile_ref[at1, :] + jnp.where(even, 0.0, got)
        tile_ref[at2, :] = tile_ref[at2, :] + jnp.where(even, got, 0.0)
        relay(tile_ref, sb_ref, 1, own, (0, 1))

    def from_after():
        backward.wait_recv()
        tile_ref[at6, :] = tile_ref[at6, :] + halo_ref[1]
        relay(tile_ref, sb_ref, 1, own, (2,))

    def b_copy(first, lanes, late, r):
        n = (19 if late else 5) + r - 1
        block = sb_ref.at[pl.ds(own, 8), :, pl.ds(first, lanes)]
        return pltpu.make_async_remote_copy(
            block, block, send_sem.at[n], recv_sem.at[n], device_id=source_peers[r - 1], device_id_type=MESH
        )

    def b_wait(r, send_side):
        for c in range(2):

            @pl.when(core == c)
            def _():
                for first, lanes, late in ((0, 768, c == 0), (768, 384, c == 1)):
                    copy = b_copy(first, lanes, late, r)
                    if send_side:
                        copy.wait_send()
                    else:
                        copy.wait_recv()

    for late in (False, True):

        @pl.when(core == int(late))
        def _(late=late):
            from_after()
            for r in (1, 2, 3):
                b_copy(768, 384, late, r).start()

        @pl.when(core == 1 - int(late))
        def _(late=late):
            from_before()
            for r in (1, 2, 3):
                b_copy(0, 768, late, r).start()

        if not late:
            own_pass(0)
    swap(sb_ref, xb_ref, source_me)
    own_pass(1)

    def gathered(part, r):
        if part == 0:
            gather_a[r - 1].wait_recv()
        else:
            b_wait(r, False)
        swap(parts[part][0], parts[part][1], source_blocks[r])

    def reduce_to(part, r, got_ref):
        block = parts[part][3].at[pl.ds(target_blocks[r] * 8, 8)]
        return send(8 + 3 * part + r - 1, block, got_ref.at[r - 1], target_peers[r - 1])

    for r in (3, 2):
        gathered(1, r)
        block_pass(1, source_blocks[r])
    gathered(1, 1)
    low = lax.broadcasted_iota(jnp.int32, (2, 128), 1) < 64
    for_before, for_after = 2 * core, 2 - 2 * core

    def pack(j):
        def parent(g, carry):
            t = j * 8 + g
            p = [pb_ref[t, :, 128 * n : 128 * n + 128] for n in range(9)]
            chunks = (
                (for_before, (p[3], jnp.where(low, p[4], p[1]), p[2])),
                (1, (p[0], jnp.where(low, p[1], p[4]), p[5])),
                (for_after, p[6:9]),
            )
            for chunk, tiles in chunks:
                for c in range(3):
                    pu_ref[chunk, t, :, 128 * c : 128 * c + 128] = tiles[c]
            return carry

        lax.fori_loop(0, PAR, parent, 0, unroll=2)

    urgent = []
    for r in (1, 2, 3):
        last_pass(1, target_blocks[r], source_blocks[1:2])
        pack(target_blocks[r])
        chunk = pu_ref.at[0, pl.ds(target_blocks[r] * 8, 8)]
        urgent.append(send(10 + r, chunk, gotu_ref.at[r - 1], target_peers[r - 1]))
    for r in (3, 2, 1):
        gathered(0, r)
    last_pass(0, target_blocks[1], source_blocks[1:])
    others = []
    for r in (1, 2, 3):
        chunks = pu_ref.at[pl.ds(1, 2), pl.ds(target_blocks[r] * 8, 8)]
        others.append(send(15 + r, chunks, goto_ref.at[r - 1], target_peers[r - 1]))
    reduces = []
    for r in (1, 2, 3):
        if r > 1:
            last_pass(0, target_blocks[r], source_blocks[1:])
        reduces.append(reduce_to(0, r, gota_ref))
    last_pass(1, target_blocks[0], source_blocks[1:2])
    pack(target_blocks[0])

    def to_rows(chunk, slot):
        def parent(g, carry):
            for c in range(3):
                pack_ref[slot, pl.ds(g * 6 + c, 2, stride=3), :] = su_ref[chunk, g, :, 128 * c : 128 * c + 128]
            return carry

        lax.fori_loop(0, PAR, parent, 0, unroll=2)

    for copy in urgent:
        copy.wait_recv()

    def first_total(g, carry):
        su_ref[0, g] = (pu_ref[0, target_me * 8 + g] + gotu_ref[0, g]) + (gotu_ref[1, g] + gotu_ref[2, g])
        return carry

    lax.fori_loop(0, PAR, first_total, 0, unroll=2)
    to_rows(0, 2)
    far = (clus, lax.rem(direction + N_DIR - 1 + 2 * core, N_DIR))
    near = (clus, direction + 1 - 2 * core)
    last_far = send(14, pack_ref.at[2], halo_ref.at[2 + core], far)
    last_pass(0, target_blocks[0], source_blocks[1:])
    for copy in others:
        copy.wait_recv()

    def other_totals(g, carry):
        for n in range(2):
            own_sum = pu_ref[1 + n, target_me * 8 + g]
            su_ref[1 + n, g] = (own_sum + goto_ref[0, n, g]) + (goto_ref[1, n, g] + goto_ref[2, n, g])
        return carry

    lax.fori_loop(0, PAR, other_totals, 0, unroll=2)
    to_rows(2, 3)
    last_near = send(15, pack_ref.at[3], halo_ref.at[3 - core], near)

    def unpack(g, carry):
        f, rest, last = (
            [su_ref[chunk, g, :, 128 * c : 128 * c + 128] for c in range(3)] for chunk in (for_before, 1, for_after)
        )
        pairs = (
            (0, (rest[0], jnp.where(low, rest[1], f[1]), f[2])),
            (1, (f[0], jnp.where(low, f[1], rest[1]), rest[2])),
            (5, last),
        )
        for q, tiles in pairs:
            for c in range(3):
                tile_ref[pl.ds((g * 6 + c) * 8 + q + 1, 2, stride=24), :] = tiles[c]
        return carry

    lax.fori_loop(0, PAR, unpack, 0)
    for copy in reduces:
        copy.wait_recv()

    def last_total(g, carry):
        sum_ref[g] = (pa_ref[target_me * 8 + g] + gota_ref[0, g]) + (gota_ref[1, g] + gota_ref[2, g])
        return carry

    lax.fori_loop(0, PAR, last_total, 0, unroll=2)
    unrelay(sum_ref, tile_ref, 0)
    pair = lax.broadcasted_iota(jnp.int32, (8, 128), 0)
    inside = (pair > 0) & (pair < 7)
    for t in range(TILES):
        inc_ref[t] = jnp.where(inside, tile_ref[8 * t : 8 * t + 8, :], 0.0)

    def child(k, carry):
        g, o = parents_ref[0, k], octant_ref[0, k]
        for c in range(3):
            re, im = inc_ref[g * 6 + c], inc_ref[g * 6 + 3 + c]
            fr, fi = phase_ref[o * 6 + c], phase_ref[o * 6 + 3 + c]
            r_ref[k * 2, :, 128 * c : 128 * c + 128] = re * fr + im * fi
            r_ref[k * 2 + 1, :, 128 * c : 128 * c + 128] = im * fr - re * fi
        return carry

    lax.fori_loop(0, KIDS, child, 0, unroll=4)

    def to_child(r):
        hi, lo = split(r)
        return (
            dot3((hi[:, :256], lo[:, :256]), (right2_ref[0, 0], right2_ref[1, 0])),
            dot3((hi[:, 128:], lo[:, 128:]), (right2_ref[0, 1], right2_ref[1, 1])),
        )

    v_ref[0], v_ref[1] = to_child(r_ref[...].reshape(768, 384))
    for n in range(6):
        at = slice(128 * n, 128 * n + 128)
        out_ref[at, :] = dot2(left2_ref[...], split(jnp.concatenate([v_ref[0, at, :], v_ref[1, at, :]], axis=0)))
    hot_parent, hot_octant = one_hot(parent_ref[...], 8), one_hot(octants_ref[...], 8)
    shifts = [pick(hot_octant, [edge_ref[e, t] for t in range(6)]) for e in range(2)]
    for copy in (forward, backward, *gather_a, *reduces, *urgent, *others):
        copy.wait_send()
    for r in (1, 2, 3):
        b_wait(r, True)
    last_near.wait()
    last_far.wait()
    rows = []
    for e in range(2):
        values = pick(hot_parent, [halo_ref[3 - e, pl.ds(t, 8, stride=6), :] for t in range(6)])
        re, im, fr, fi = values[:, :384], values[:, 384:], shifts[e][:, :384], shifts[e][:, 384:]
        rows += [re * fr + im * fi, im * fr - re * fi]
    even_part, odd_part = to_child(jnp.concatenate(rows, axis=0))
    weight_even, weight_odd = azimuth_rows(EVEN), azimuth_rows(ODD)
    for e, s in enumerate((0, 7)):
        for a in range(2):
            at = (2 * e + a) * KIDS
            for i in range(8):
                we, wo = float(weight_even[s, i]), float(weight_odd[s, i])
                if we or wo:
                    place = pl.ds(a * 8 + i, KIDS, stride=16)
                    out_ref[place, :] = out_ref[place, :] + (
                        we * even_part[at : at + KIDS] + wo * odd_part[at : at + KIDS]
                    )


VMEM_SPEC = pl.BlockSpec(memory_space=pltpu.VMEM)
HBM_SPEC = pl.BlockSpec(memory_space=pltpu.HBM)
LIMIT = 63 * 2**20


def f32(*shape):
    return jax.ShapeDtypeStruct(shape, jnp.float32)


def on_device(child, table, child_parent, child_octant, partner_src, partner_off, partner_count):
    up_left, up_right, down_right, down_left, phases = (jnp.asarray(a) for a in constants())
    vm = functools.partial(pltpu.VMEM, dtype=jnp.float32)
    ints = functools.partial(pltpu.VMEM, dtype=jnp.int32)
    bf16 = functools.partial(pltpu.VMEM, dtype=jnp.bfloat16)
    scalars = functools.partial(pltpu.SMEM, dtype=jnp.int32)
    out = pl.pallas_call(
        middle_kernel,
        out_shape=f32(KIDS * 16, 128),
        in_specs=[HBM_SPEC] * 12,
        out_specs=VMEM_SPEC,
        scratch_shapes=[
            ints((1, KIDS)), ints((1, KIDS)), scalars((1, KIDS)), scalars((1, KIDS)), vm((KIDS, 2, 8, 128)),
            ints((56, 128)), ints((56, 128)), ints((1, 128)), bf16((OFFSETS + 1, 2, 2304)), bf16((256, 128)),
            bf16((2, 256, 384)), vm((144, 128)), bf16((2, 2, 256, 128)), bf16((128, 256)), vm((2, 6, 8, 128)),
            ints((32, 128)), scalars((32, 128)), ints((8, 128)), scalars((8, 128)),
            bf16((2, 768, 256)), vm((2 * KIDS + 2, 8, 384)), vm((48, 8, 128)), vm((8 * TILES, 128)), vm((TILES, 8, 128)),
            vm((2 * KIDS, 8, 384)), vm((2, 768, 128)), vm((4, TILES, 128)), vm((4, TILES, 128)),
            *[vm((32, 2, HALF))] * 4, *[vm((32, 2, 2, HALF))] * 2, *[vm((32, 2, HALF))] * 2,
            vm((3, 8, 2, HALF)), vm((3, 32, 2, 384)), vm((3, 8, 2, 384)), vm((3, 2, 8, 2, 384)), vm((3, 8, 2, 384)),
            vm((8, 2, HALF)),
            pltpu.SemaphoreType.DMA((14,)), pltpu.SemaphoreType.DMA((22,)), pltpu.SemaphoreType.DMA((22,)),
        ],
        compiler_params=pltpu.CompilerParams(collective_id=0, has_side_effects=True, vmem_limit_bytes=LIMIT),
        name="middle",
    )(
        child_parent, child_octant.reshape(1, KIDS), child, partner_src.T, partner_off.T, partner_count.reshape(1, 128),
        table, up_left, up_right, phases, down_right, down_left,
    )
    return out.reshape(KIDS, 2, 8, 128)


def solution(mesh):
    return jax.shard_map(
        on_device,
        mesh=mesh,
        in_specs=(P("clus", None, "dir", None), P(None, None, "dir"), P("clus", None), P("clus"), P(), P(), P()),
        out_specs=P("clus", None, "dir", None),
        check_vma=False,
    )
```
